128 devices in a mesh: brick: 128 (over z, x, y, core).
Axes of the slice: x: 4, y: 4, z: 4, core: 2. Of those that a mesh axis runs over, the one named last changes fastest.
Arguments:
- positions: float32 [3, 65536], P(None, 'brick'), may hold values from 0 to 3
- species: int32 [65536], P('brick'), may hold values from 0 to 7
- pair_first: int32 [6144, 128], P('brick'), may hold values from 0 to 511
- pair_second: int32 [6144, 128], P('brick'), may hold values from 0 to 1535, as said below
- pair_valid: int32 [6144, 128], P('brick'), may hold values from 0 to 1, as said below
- send_list: int32 [512, 256], P('brick'), may hold values from 0 to 511, as said below
- w_radial: float32 [64, 8], replicated, may hold values from -2 to 2
- w_first: float32 [64, 8], replicated, may hold values from -3.5 to 3.5
- w_second: float32 [64, 8], replicated, may hold values from -3.5 to 3.5
- w_value: float32 [2, 32, 64], replicated, may hold values from -0.75 to 0.75
- w_env: float32 [2, 32, 64], replicated, may hold values from -0.75 to 0.75
- w_latent: float32 [2, 64, 64], replicated, may hold values from -0.75 to 0.75
- w_tensor: float32 [2, 64, 32], replicated, may hold values from -1 to 1
- w_mix: float32 [2, 64, 64], replicated, may hold values from -0.75 to 0.75
- w_read: float32 [64, 64], replicated, may hold values from -0.75 to 0.75
- read_vec: float32 [64], replicated, may hold values from -0.75 to 0.75
Outputs:
- forces: float32 [3, 65536], P(None, 'brick')
- energy: float32 [], replicated
The draws below stay inside these ranges and needn't reach their ends.
Inputs may be any that keep to these rules, and one draw needn't show every extreme that they name: `pair_second`: below 512: an atom of the block's brick. Otherwise a ghost slot as in the first step, only toward bricks that exist. `pair_valid`: A brick's valid pairs fill whole blocks from its first block on; the last brick's blocks are all valid. `send_list`: each row holds 256 distinct atoms of its brick.
All inputs are finite; a program needn't handle non-finite values.
Results may differ from the reference program's by a relative error of at most 0.0003.
Values sent between devices are 32-bit elements; how exact they have to be, the bound alone decides.
No kernel may reach another device: no remote copies, remote signals or barrier semaphores. Data moves between devices by JAX's collectives and lax.ppermute only.
A program may use at most 128 MiB of HBM per device.

```python
import math
import jax
import jax.numpy as jnp
from jax import lax

LAT = 64
CH = 32
NRB = 8
NSPC = 8
LAYERS = 2
PAIR_BLOCK = 128
A_DEV = 512
BLOCKS_DEV = 48
GHOSTS = 256
ATOMS = 65536
BLOCKS = 6144
N_BRICK = 128


def draw_pair_second(key, part):
    key = jax.random.fold_in(key, 11)
    key_local, key_group, key_place, key_choose = jax.random.split(key, 4)
    bricks = BLOCKS // BLOCKS_DEV
    brick_ids = (jnp.arange(BLOCKS, dtype=jnp.int32) // BLOCKS_DEV)[:, None]
    local_pick = jax.random.randint(key_local, (BLOCKS, PAIR_BLOCK), 0, A_DEV)
    ghost_group = jax.random.randint(key_group, (BLOCKS, PAIR_BLOCK), 0, 4)
    ghost_place = jax.random.randint(key_place, (BLOCKS, PAIR_BLOCK), 0, GHOSTS)
    offsets = jnp.array([1, -1, 2, -2], dtype=jnp.int32)
    source = brick_ids - offsets[ghost_group]
    exists = (source >= 0) & (source < bricks)
    use_ghost = jax.random.randint(key_choose, (BLOCKS, PAIR_BLOCK), 0, 3) < 2
    return jnp.where(use_ghost & exists, A_DEV + ghost_group * GHOSTS + ghost_place, local_pick).astype(jnp.int32)


def draw_pair_valid(key, part):
    key = jax.random.fold_in(key, 23)
    bricks = BLOCKS // BLOCKS_DEV
    brick_range = jnp.arange(bricks, dtype=jnp.int32)
    base_live = BLOCKS_DEV // 3 + (BLOCKS_DEV - BLOCKS_DEV // 3) * brick_range // max(bricks - 1, 1)
    reach = BLOCKS_DEV // 6 + 1
    jitter = jax.random.randint(key, (bricks,), -reach, reach + 1)
    live_blocks = jnp.clip(base_live + jitter, 1, BLOCKS_DEV)
    live_blocks = jnp.where(brick_range == bricks - 1, BLOCKS_DEV, live_blocks)
    block_ids = jnp.arange(BLOCKS, dtype=jnp.int32)
    inside = block_ids % BLOCKS_DEV < live_blocks[block_ids // BLOCKS_DEV]
    return jnp.broadcast_to(inside[:, None], (BLOCKS, PAIR_BLOCK)).astype(jnp.int32)


def draw_send_list(key, part):
    key = jax.random.fold_in(key, 37)
    row_count = 4 * (BLOCKS // BLOCKS_DEV)
    row_keys = jax.random.split(key, row_count)
    picked = jax.vmap(lambda row_key: jax.random.permutation(row_key, A_DEV)[:GHOSTS])(row_keys)
    return picked.astype(jnp.int32)


def place_ends(drawn, rng, smallest, high):
    place = [jax.random.randint(jax.random.fold_in(rng, axis), (), 0, length) for axis, length in enumerate(drawn.shape)]
    longest = drawn.shape.index(max(drawn.shape))
    neighbour = place[:longest] + [(place[longest] + 1) % drawn.shape[longest]] + place[longest + 1:]
    return drawn.at[tuple(place)].set(smallest).at[tuple(neighbour)].set(high)


def levels(own_key, shape, cuts, least, largest):
    def one(axis_at, parts):
        draws = jax.random.uniform(jax.random.fold_in(jax.random.fold_in(own_key, 6), axis_at), (parts,), jnp.float32, least / len(cuts), largest / len(cuts))
        return jnp.repeat(jnp.exp(draws), shape[axis_at] // parts).reshape((-1,) + (1,) * (len(shape) - axis_at - 1))

    factor_of = one(*cuts[0])
    for cut in cuts[1:]:
        factor_of = factor_of * one(*cut)
    return factor_of


def noise(stream_key, dims, spread, most, held_as=jnp.bfloat16):
    return jnp.clip(spread * jax.random.normal(stream_key, dims, jnp.float32), -most, most).astype(held_as)


def setup_inputs(seed: int = 0) -> dict:
    keys = jax.random.split(jax.random.key(seed), 17)
    positions = jnp.clip(3.0 * jax.random.uniform(keys[0], (3, ATOMS), jnp.float32) ** levels(keys[0], (3, ATOMS), ((1, 128),), -0.2, 0.2), 0.0, 3.0)
    species = place_ends(jax.random.randint(keys[1], (ATOMS,), 0, NSPC), jax.random.fold_in(keys[1], 1), 0, NSPC - 1).astype(jnp.int32)
    pair_first = place_ends(jax.random.randint(keys[2], (BLOCKS, PAIR_BLOCK), 0, A_DEV), jax.random.fold_in(keys[2], 1), 0, A_DEV - 1).astype(jnp.int32)
    pair_second = draw_pair_second(jax.random.fold_in(keys[16], 71), 0)
    pair_valid = draw_pair_valid(jax.random.fold_in(keys[16], 71), 0)
    send_list = draw_send_list(jax.random.fold_in(keys[16], 71), 0)
    w_radial = noise(keys[6], (LAT, NRB), NRB ** -0.5, 2.0, jnp.float32)
    w_first = noise(keys[7], (LAT, NSPC), 3 ** -0.5, 3.5, jnp.float32)
    w_second = noise(keys[8], (LAT, NSPC), 3 ** -0.5, 3.5, jnp.float32)
    w_value = noise(keys[9], (LAYERS, CH, LAT), LAT ** -0.5, 0.75, jnp.float32)
    w_env = noise(keys[10], (LAYERS, CH, LAT), LAT ** -0.5, 0.75, jnp.float32)
    w_latent = noise(keys[11], (LAYERS, LAT, LAT), LAT ** -0.5, 0.75, jnp.float32)
    w_tensor = noise(keys[12], (LAYERS, LAT, CH), CH ** -0.5, 1.0, jnp.float32)
    w_mix = noise(keys[13], (LAYERS, LAT, LAT), LAT ** -0.5, 0.75, jnp.float32)
    w_read = noise(keys[14], (LAT, LAT), LAT ** -0.5, 0.75, jnp.float32)
    read_vec = noise(keys[15], (LAT,), LAT ** -0.5, 0.75, jnp.float32)
    return dict(positions=positions, species=species, pair_first=pair_first, pair_second=pair_second, pair_valid=pair_valid, send_list=send_list, w_radial=w_radial, w_first=w_first, w_second=w_second, w_value=w_value, w_env=w_env, w_latent=w_latent, w_tensor=w_tensor, w_mix=w_mix, w_read=w_read, read_vec=read_vec)


CUTOFF = 6.0
SOFTENING = 0.25
ENV_SCALE = 0.25
PAIR_SHIFT = 1.0
OFFSETS = (1, -1, 2, -2)

def matmul(left, right):
    return jnp.dot(left, right, precision=lax.Precision.HIGHEST, preferred_element_type=jnp.float32)

def geometry(coord_first, coord_second, nbasis):
    difference = coord_second - coord_first
    distance = jnp.sqrt(lax.optimization_barrier(jnp.sum(difference * difference, axis=0)) + SOFTENING)
    direction = difference / distance
    envelope = (1.0 - (distance / CUTOFF) ** 2) ** 2
    frequency = jnp.arange(1, nbasis + 1).astype(distance.dtype) * (math.pi / CUTOFF)
    radial_basis = jnp.sin(frequency[:, None] * distance[None, :]) / distance[None, :] * envelope[None, :]
    return (direction, envelope, radial_basis)

def embed_pairs(coord_first, coord_second, species_first, species_second, w_radial, w_first, w_second):
    direction, envelope, radial_basis = geometry(coord_first, coord_second, w_radial.shape[1])
    species_kinds = jnp.arange(w_first.shape[1], dtype=jnp.int32)
    onehot_first = (species_first[None, :] == species_kinds[:, None]).astype(radial_basis.dtype)
    onehot_second = (species_second[None, :] == species_kinds[:, None]).astype(radial_basis.dtype)
    return jax.nn.silu(matmul(w_radial, radial_basis) + matmul(w_first, onehot_first) + matmul(w_second, onehot_second))

def contributions(latent_in, coord_first, coord_second, env_weight, live_mask, first_ids, second_ids, table_rows):
    direction, envelope, radial_basis = geometry(coord_first, coord_second, 1)
    scaled = matmul(env_weight, latent_in) * (envelope * live_mask)[None, :]
    vectors = (direction[:, None, :] * scaled[None, :, :]).reshape(-1, latent_in.shape[1])
    flat_rows = vectors.T
    summed = jax.ops.segment_sum(flat_rows, first_ids, num_segments=table_rows) - jax.ops.segment_sum(flat_rows, second_ids, num_segments=table_rows)
    return summed.T

def update_latent(latent_in, coord_first, coord_second, table_in, value_weight, latent_weight, tensor_weight, mix_weight, first_ids, second_ids):
    direction, envelope, radial_basis = geometry(coord_first, coord_second, 1)
    channel_values = matmul(value_weight, latent_in)
    channels = channel_values.shape[0]
    gap_table = (table_in[:, first_ids] - table_in[:, second_ids]).reshape(3, channels, -1)
    scalars = ENV_SCALE * lax.optimization_barrier(jnp.sum(direction[:, None, :] * channel_values[None, :, :] * gap_table, axis=0))
    hidden = jax.nn.silu(matmul(latent_weight, latent_in) + matmul(tensor_weight, scalars))
    return latent_in + matmul(mix_weight, hidden)

def readout(latent_in, coord_first, coord_second, w_read, read_vec, live_mask):
    direction, envelope, radial_basis = geometry(coord_first, coord_second, 1)
    energies = matmul(read_vec, jax.nn.silu(matmul(w_read, latent_in)))
    return jnp.sum((energies + PAIR_SHIFT) * envelope * live_mask)

def reference(positions, species, pair_first, pair_second, pair_valid, send_list, w_radial, w_first, w_second, w_value, w_env, w_latent, w_tensor, w_mix, w_read, read_vec):
    bricks = N_BRICK
    own_count = A_DEV
    ghost_count = GHOSTS
    first_local = pair_first.reshape(bricks, -1)
    second_local = pair_second.reshape(bricks, -1)
    brick_ids = jnp.arange(bricks, dtype=jnp.int32)[:, None]
    ghost_slot = jnp.maximum(second_local - own_count, 0)
    ghost_group = jnp.minimum(ghost_slot // ghost_count, 3).astype(jnp.int32)
    ghost_place = (ghost_slot % ghost_count).astype(jnp.int32)
    offsets = jnp.array(OFFSETS, dtype=jnp.int32)
    source = jnp.clip(brick_ids - offsets[ghost_group], 0, bricks - 1).astype(jnp.int32)
    send_rows = send_list.reshape(bricks, 4, ghost_count)
    remote = source * own_count + send_rows[source, ghost_group, ghost_place]
    first_ids = (brick_ids * own_count + first_local).reshape(-1).astype(jnp.int32)
    second_ids = jnp.where(second_local < own_count, brick_ids * own_count + second_local, remote).reshape(-1).astype(jnp.int32)
    live_mask = pair_valid.reshape(-1).astype(jnp.float32)
    species_first = species[first_ids]
    species_second = species[second_ids]
    atoms = positions.shape[1]

    def energy_total(coords):
        coord_first = coords[:, first_ids]
        coord_second = coords[:, second_ids]
        latent = embed_pairs(coord_first, coord_second, species_first, species_second, w_radial, w_first, w_second)
        for layer_index in range(w_value.shape[0]):
            table = contributions(latent, coord_first, coord_second, w_env[layer_index], live_mask, first_ids, second_ids, atoms)
            latent = update_latent(latent, coord_first, coord_second, table, w_value[layer_index], w_latent[layer_index], w_tensor[layer_index], w_mix[layer_index], first_ids, second_ids)
        return readout(latent, coord_first, coord_second, w_read, read_vec, live_mask)
    total, gradient = jax.value_and_grad(energy_total)(positions)
    return (-gradient, total / live_mask.shape[0])
```

```python
import math

import jax
import jax.numpy as jnp
import numpy as np
from jax import lax
from jax.experimental import pallas as pl
from jax.experimental.pallas import tpu as pltpu
from jax.sharding import PartitionSpec as P

F32 = jnp.float32
BF16 = jnp.bfloat16

CUTOFF = 6.0
SOFTENING = 0.25
ENV_SCALE = 0.25
PAIR_SHIFT = 1.0

LAT = 64
CH = 32
NB = 8
VEC = 3 * CH
OWN = 512
GHOST = 256
ROWS = OWN + 4 * GHOST
WIN = 256
BRICK_BLOCKS = 48
PAIRS = BRICK_BLOCKS * 128
CHUNK = 512
CHUNKS = PAIRS // CHUNK

VMEM_LIMIT = 56 * 1024 * 1024


def fit_trig():
    r = np.cos(np.linspace(0.0, np.pi, 4001)) * 0.5
    x = r * r
    base = np.polynomial.chebyshev.Chebyshev
    safe = np.where(r == 0.0, 1.0, r)
    sine = np.where(r == 0.0, 2 * np.pi, np.sin(2 * np.pi * safe) / safe)
    s = base.fit(x, sine, 8, domain=[0.0, 0.25]).convert(kind=np.polynomial.Polynomial)
    c = base.fit(x, np.cos(2 * np.pi * r), 8, domain=[0.0, 0.25]).convert(kind=np.polynomial.Polynomial)
    return [float(v) for v in s.coef], [float(v) for v in c.coef]


SIN_COEF, COS_COEF = fit_trig()


def horner(coef, x):
    out = jnp.full_like(x, coef[-1])
    for c in coef[-2::-1]:
        out = out * x + c
    return out


def dot(a, b):
    return lax.dot_general(a, b, (((1,), (0,)), ((), ())), preferred_element_type=F32)


def dot_nt(a, b):
    return lax.dot_general(a, b, (((1,), (1,)), ((), ())), preferred_element_type=F32)


def split2(x):
    hi = x.astype(BF16)
    lo = (x - hi.astype(F32)).astype(BF16)
    return hi, lo


def split3(x):
    hi = x.astype(BF16).astype(F32)
    rest = x - hi
    mid = rest.astype(BF16).astype(F32)
    return hi, mid, (rest - mid)


def stack2(x):
    hi, lo = split2(x)
    return jnp.concatenate([hi, lo], axis=0)


def weight3(w):
    hi, lo = split2(w)
    return jnp.concatenate([hi.astype(F32), hi.astype(F32), lo.astype(F32)], axis=1).astype(BF16)


def dense(w3, x):
    hi, lo = split2(x)
    return dot(w3, jnp.concatenate([hi, lo, hi], axis=0))


def sigmoid(x):
    return 1.0 / (1.0 + jnp.exp(-x))


def silu_and_slope(x):
    s = sigmoid(x)
    y = x * s
    return y, s + y * (1.0 - s)


def hot(ids, start, rows):
    at = lax.broadcasted_iota(jnp.int32, (rows, ids.shape[1]), 0)
    return jnp.where(at == ids - start, 1.0, 0.0)


def hot_first(first):
    return hot(first, 0, OWN).astype(BF16)


def incidence(first, second):
    own = hot(first, 0, OWN) - hot(second, 0, OWN)
    return jnp.concatenate([own.astype(BF16), (-hot(second, OWN, 4 * GHOST)).astype(BF16)], axis=0)


def fold2(x):
    half = x.shape[0] // 2
    return x[:half] + x[half:]


def radial(dist):
    k = (lax.broadcasted_iota(jnp.int32, (NB, dist.shape[1]), 0) + 1).astype(F32)
    turns = k * (dist * (1.0 / (2.0 * CUTOFF)))
    r = turns - jnp.round(turns)
    x = r * r
    return r * horner(SIN_COEF, x), horner(COS_COEF, x), k * (math.pi / CUTOFF)


def lanes(c):
    return pl.ds(pl.multiple_of(c * CHUNK, CHUNK), CHUNK)


def ids_of(ref, c):
    return ref[0:1, lanes(c)]


def gap_vectors(table_ref, oh):
    return fold2(dot(table_ref[...], oh))


def weigh(geo, values):
    return jnp.concatenate([geo[m : m + 1] * values for m in range(3)], axis=0)


def project(geo, vectors):
    return (
        geo[0:1] * vectors[:CH]
        + geo[1:2] * vectors[CH : 2 * CH]
        + geo[2:3] * vectors[2 * CH :]
    )


def put_rows(rows, n):
    at = lax.broadcasted_iota(jnp.int32, (8, n), 0)
    out = jnp.zeros((8, n), F32)
    for i, row in enumerate(rows):
        out = jnp.where(at == i, row, out)
    return out


def dir_grad(dq, vectors):
    return [jnp.sum(dq * vectors[m * CH : (m + 1) * CH], axis=0, keepdims=True) for m in range(3)]


def fill_table(table_ref, own_ref, ghost_refs):
    hi, lo = split2(own_ref[...])
    table_ref[:VEC, :OWN] = hi
    table_ref[VEC:, :OWN] = lo
    for m, ghost in enumerate(ghost_refs):
        hi, lo = split2(ghost[...])
        at = OWN + m * GHOST
        table_ref[:VEC, at : at + GHOST] = hi
        table_ref[VEC:, at : at + GHOST] = lo


def emit(acc_ref, own_out, ghost_outs):
    own_out[...] = acc_ref[:, :OWN]
    for m, out in enumerate(ghost_outs):
        at = OWN + m * GHOST
        out[...] = acc_ref[:, at : at + GHOST]


def send_kernel(pos_ref, spec_ref, send_ref, m0, m1, m2, m3, ohs_ref):
    oh = jnp.concatenate([hot(send_ref[m : m + 1, :], 0, OWN).astype(BF16) for m in range(4)], axis=1)
    ohs_ref[...] = oh
    hi, mid, lo = split3(pos_ref[...])
    rows = jnp.concatenate(
        [
            put_rows([hi[i : i + 1] for i in range(3)] + [spec_ref[...].astype(F32)], OWN),
            put_rows([mid[i : i + 1] for i in range(3)], OWN),
            put_rows([lo[i : i + 1] for i in range(3)], OWN),
            jnp.zeros((8, OWN), F32),
        ],
        axis=0,
    ).astype(BF16)
    got = dot(rows, oh)
    got = got[0:8] + got[8:16] + got[16:24]
    for m, out in enumerate((m0, m1, m2, m3)):
        out[...] = got[:, m * GHOST : (m + 1) * GHOST]


def weights_kernel(
    w_radial, w_first, w_second, w_value, w_env, w_latent, w_tensor, w_mix, w_read, embed, evl, tens, mix, read, read_t,
    mix_t, lt_t, val_t, env_t, rad_t,
):
    def parts(w):
        hi, lo = split2(w)
        return hi.astype(F32), lo.astype(F32)

    rh, rl = parts(w_radial[...])
    fh, fl = parts(w_first[...])
    sh, sl = parts(w_second[...])
    embed[...] = jnp.concatenate([rh, rh, rl, fh, sh, fl, sl, jnp.zeros_like(rh)], axis=1).astype(BF16)
    for l in range(2):
        evl[l] = weight3(jnp.concatenate([w_env[l], w_value[l], w_latent[l]], axis=0))
        tens[l] = weight3(w_tensor[l])
        mix[l] = weight3(w_mix[l])
        mix_t[l] = weight3(w_mix[l].T)
        lt_t[l] = weight3(jnp.concatenate([w_latent[l].T, w_tensor[l].T], axis=0))
        val_t[l] = weight3(w_value[l].T)
        env_t[l] = weight3(w_env[l].T)
    read[...] = weight3(w_read[...])
    read_t[...] = weight3(w_read[...].T)
    rad_t[...] = weight3(w_radial[...].T)


def embed_kernel(
    live_ref, pos_ref, spec_ref, c0, c1, c2, c3, first_ref, second_ref, valid_ref, w_embed, w_evl,
    geo_out, slope_out, lat_out, evh_out, own_out, g0, g1, g2, g3, atoms_ref, acc_ref,
):
    def put(at, width, coords):
        hi, mid, lo = split3(coords)
        atoms_ref[:, at : at + width] = jnp.concatenate([hi, mid, lo, jnp.zeros_like(hi)], axis=0).astype(BF16)

    put(0, OWN, put_rows([pos_ref[i : i + 1, :] for i in range(3)] + [spec_ref[...].astype(F32)], OWN))
    for m, c in enumerate((c0, c1, c2, c3)):
        put(OWN + m * GHOST, GHOST, c[...])
    acc_ref[...] = jnp.zeros_like(acc_ref)

    def body(c, carry):
        at = lanes(c)
        first, second = first_ref[0:1, at], second_ref[0:1, at]
        mask = valid_ref[0:1, at].astype(F32)
        hf = hot(first, 0, OWN)
        hs = hot(second, 0, OWN)
        ghost = hot(second, OWN, 4 * GHOST).astype(BF16)
        oh = jnp.concatenate([(hf - hs).astype(BF16), -ghost], axis=0)
        a = dot(atoms_ref[:, :OWN], hf.astype(BF16))
        b = dot(atoms_ref[...], jnp.concatenate([hs.astype(BF16), ghost], axis=0))
        a = a[0:8] + a[8:16] + a[16:24]
        b = b[0:8] + b[8:16] + b[16:24]
        row = lax.broadcasted_iota(jnp.int32, (8, CHUNK), 0)
        diff = jnp.where(row < 3, b - a, 0.0)
        sq = jnp.sum(diff * diff, axis=0, keepdims=True) + SOFTENING
        dist = jnp.sqrt(sq)
        inv = 1.0 / dist
        shrink = 1.0 - sq * (1.0 / CUTOFF**2)
        env = shrink * shrink
        direction = diff * inv
        weight = env * mask
        geo = direction + jnp.where(row == 3, weight, 0.0) + jnp.where(row == 4, dist, 0.0)
        geo = geo + jnp.where(row == 5, mask, 0.0)
        geo_out[:, at] = geo
        sines, _, _ = radial(dist)
        basis = sines * (inv * env)
        bh = basis.astype(BF16).astype(F32)
        bl = basis - bh
        rowf = row.astype(F32)
        sf = jnp.where(rowf == a[3:4], 1.0, 0.0)
        ss = jnp.where(rowf == b[3:4], 1.0, 0.0)
        pre = dot(
            w_embed[...],
            jnp.concatenate([bh, bl, bh, sf, ss, sf, ss, jnp.zeros_like(bh)], axis=0).astype(BF16),
        )
        lat, slope = silu_and_slope(pre)
        slope_out[:, at] = slope
        lat_out[:, at] = lat
        evh = dense(w_evl[0], lat)
        evh_out[:, at] = evh
        vec = weigh(geo, evh[:CH] * weight)
        acc_ref[...] += fold2(dot_nt(stack2(vec), oh))
        return carry

    lax.fori_loop(0, live_ref[0, 0], body, 0)
    emit(acc_ref, own_out, (g0, g1, g2, g3))


def combine_kernel(own_ref, r0, r1, r2, r3, ohs_ref, own_out, g0, g1, g2, g3):
    arrived = jnp.concatenate([r[...] for r in (r0, r1, r2, r3)], axis=1)
    owned = own_ref[...] + fold2(dot_nt(stack2(arrived), ohs_ref[...]))
    own_out[...] = owned
    ghosts = fold2(dot(stack2(owned), ohs_ref[...]))
    for m, out in enumerate((g0, g1, g2, g3)):
        out[...] = ghosts[:, m * GHOST : (m + 1) * GHOST]


def middle_kernel(
    live_ref, own_ref, t0, t1, t2, t3, first_ref, second_ref, geo_ref, lat_ref, evh_ref, w_evl, w_tens, w_mix,
    gap_out, hid_out, lat_out, evh_out, own_out, g0, g1, g2, g3, table_ref, acc_ref,
):
    fill_table(table_ref, own_ref, (t0, t1, t2, t3))
    acc_ref[...] = jnp.zeros_like(acc_ref)

    def body(c, carry):
        at = lanes(c)
        oh = incidence(first_ref[0:1, at], second_ref[0:1, at])
        gap = gap_vectors(table_ref, oh)
        gap_out[:, at] = gap
        geo = geo_ref[:, at]
        scalars = (ENV_SCALE * evh_ref[CH : 2 * CH, at]) * project(geo, gap)
        hid = evh_ref[2 * CH :, at] + dense(w_tens[0], scalars)
        hid_out[:, at] = hid
        lat = lat_ref[:, at] + dense(w_mix[0], hid * sigmoid(hid))
        lat_out[:, at] = lat
        evh = dense(w_evl[1], lat)
        evh_out[:, at] = evh
        vec = weigh(geo, evh[:CH] * geo[3:4])
        acc_ref[...] += fold2(dot_nt(stack2(vec), oh))
        return carry

    lax.fori_loop(0, live_ref[0, 0], body, 0)
    emit(acc_ref, own_out, (g0, g1, g2, g3))


def update_back(geo, gap, values, hid_slope, dlat, w_mix_t, w_lt_t, w_val_t):
    dhid = dense(w_mix_t, dlat) * hid_slope
    both = dense(w_lt_t, dhid)
    dscal = both[LAT:] * ENV_SCALE
    dval = project(geo, gap) * dscal
    dq = values * dscal
    return dlat + both[:LAT] + dense(w_val_t, dval), dq


def turn_kernel(
    live_ref, own_ref, t0, t1, t2, t3, first_ref, second_ref, geo_ref, lat_ref, evh_ref, read_vec, w_tens, w_mix, w_read,
    w_read_t, w_mix_t, w_lt_t, w_val_t,
    energy_out, dlat_out, dgeo_out, own_out, g0, g1, g2, g3, table_ref, acc_ref,
):
    fill_table(table_ref, own_ref, (t0, t1, t2, t3))
    acc_ref[...] = jnp.zeros_like(acc_ref)
    rv = read_vec[...]

    def body(c, energy):
        at = lanes(c)
        oh = incidence(first_ref[0:1, at], second_ref[0:1, at])
        gap = gap_vectors(table_ref, oh)
        geo = geo_ref[:, at]
        weight = geo[3:4]
        values = evh_ref[CH : 2 * CH, at]
        scalars = (ENV_SCALE * values) * project(geo, gap)
        hid = evh_ref[2 * CH :, at] + dense(w_tens[1], scalars)
        act, hid_slope = silu_and_slope(hid)
        lat = lat_ref[:, at] + dense(w_mix[1], act)
        out, out_slope = silu_and_slope(dense(w_read[...], lat))
        pair_energy = jnp.sum(rv * out, axis=0, keepdims=True) + PAIR_SHIFT
        dlat = dense(w_read_t[...], out_slope * (rv * weight))
        dlat, dq = update_back(geo, gap, values, hid_slope, dlat, w_mix_t[1], w_lt_t[1], w_val_t[1])
        dlat_out[:, at] = dlat
        dgeo_out[:, at] = put_rows(dir_grad(dq, gap) + [pair_energy], CHUNK)
        acc_ref[...] += fold2(dot_nt(stack2(weigh(geo, dq)), oh))
        return energy + pair_energy * weight

    energy = lax.fori_loop(0, live_ref[0, 0], body, jnp.zeros((1, CHUNK), F32))
    energy_out[...] = jnp.broadcast_to(jnp.sum(energy, axis=1, keepdims=True), energy_out.shape)
    emit(acc_ref, own_out, (g0, g1, g2, g3))


def environment_back(geo, dvec, env_values, dlat, dgeo, w_env_t):
    weight = geo[3:4]
    dscaled = project(geo, dvec)
    rows = dir_grad(env_values * weight, dvec)
    rows.append(jnp.sum(env_values * dscaled, axis=0, keepdims=True))
    return dlat + dense(w_env_t, dscaled * weight), dgeo + put_rows(rows, CHUNK)


def back_kernel(
    live_ref, own_ref, t0, t1, t2, t3, first_ref, second_ref, geo_ref, evh1_ref, dlat_ref, dgeo_ref, gap_ref, hid_ref,
    evh0_ref, w_mix_t, w_lt_t, w_val_t, w_env_t,
    dlat_out, dgeo_out, own_out, g0, g1, g2, g3, table_ref, acc_ref,
):
    fill_table(table_ref, own_ref, (t0, t1, t2, t3))
    acc_ref[...] = jnp.zeros_like(acc_ref)

    def body(c, carry):
        at = lanes(c)
        oh = incidence(first_ref[0:1, at], second_ref[0:1, at])
        dvec = gap_vectors(table_ref, oh)
        geo = geo_ref[:, at]
        dlat, dgeo = environment_back(geo, dvec, evh1_ref[:CH, at], dlat_ref[:, at], dgeo_ref[:, at], w_env_t[1])
        gap = gap_ref[:, at]
        _, hid_slope = silu_and_slope(hid_ref[:, at])
        dlat, dq = update_back(geo, gap, evh0_ref[CH : 2 * CH, at], hid_slope, dlat, w_mix_t[0], w_lt_t[0], w_val_t[0])
        dlat_out[:, at] = dlat
        dgeo_out[:, at] = dgeo + put_rows(dir_grad(dq, gap), CHUNK)
        acc_ref[...] += fold2(dot_nt(stack2(weigh(geo, dq)), oh))
        return carry

    lax.fori_loop(0, live_ref[0, 0], body, 0)
    emit(acc_ref, own_out, (g0, g1, g2, g3))


def force_kernel(
    live_ref, own_ref, t0, t1, t2, t3, first_ref, second_ref, geo_ref, evh0_ref, dlat_ref, dgeo_ref, slope_ref,
    w_env_t, w_rad_t,
    own_out, g0, g1, g2, g3, table_ref, acc_ref,
):
    fill_table(table_ref, own_ref, (t0, t1, t2, t3))
    acc_ref[...] = jnp.zeros_like(acc_ref)

    def body(c, carry):
        at = lanes(c)
        oh = incidence(first_ref[0:1, at], second_ref[0:1, at])
        dvec = gap_vectors(table_ref, oh)
        geo = geo_ref[:, at]
        dlat, dgeo = environment_back(geo, dvec, evh0_ref[:CH, at], dlat_ref[:, at], dgeo_ref[:, at], w_env_t[0])
        dbasis = dense(w_rad_t[...], dlat * slope_ref[:, at])
        dist, mask = geo[4:5], geo[5:6]
        inv = 1.0 / dist
        shrink = 1.0 - dist * dist * (1.0 / CUTOFF**2)
        env = shrink * shrink
        sines, cosines, freq = radial(dist)
        along = jnp.sum(dbasis * sines, axis=0, keepdims=True) * inv
        ddist = (jnp.sum(dbasis * (freq * cosines), axis=0, keepdims=True) - along) * (inv * env)
        denv = along + mask * dgeo[3:4]
        ddist = ddist - denv * shrink * dist * (4.0 / CUTOFF**2)
        row = lax.broadcasted_iota(jnp.int32, (8, CHUNK), 0)
        unit = jnp.where(row < 3, geo, 0.0)
        dunit = jnp.where(row < 3, dgeo, 0.0)
        radial_part = ddist - jnp.sum(unit * dunit, axis=0, keepdims=True) * inv
        ddiff = dunit * inv + unit * radial_part
        hi = ddiff.astype(BF16).astype(F32)
        both = jnp.concatenate([hi, ddiff - hi], axis=0).astype(BF16)
        acc_ref[...] += fold2(dot_nt(both, oh))
        return carry

    lax.fori_loop(0, live_ref[0, 0], body, 0)
    emit(acc_ref, own_out, (g0, g1, g2, g3))


def final_kernel(own_ref, r0, r1, r2, r3, ohs_ref, out_ref):
    arrived = jnp.concatenate([r[...] for r in (r0, r1, r2, r3)], axis=1)
    hi, mid, lo = split3(arrived)
    parts = jnp.concatenate([hi, mid, lo, jnp.zeros_like(hi)], axis=0).astype(BF16)
    got = dot_nt(parts, ohs_ref[...])
    out_ref[...] = (own_ref[...] + got[0:8] + got[8:16] + got[16:24])[0:3]


def call(kernel, outs, *args, scratch=(), smem=0):
    vmem = pl.BlockSpec(memory_space=pltpu.VMEM)
    specs = [pl.BlockSpec(memory_space=pltpu.SMEM)] * smem + [vmem] * (len(args) - smem)
    return pl.pallas_call(
        kernel,
        out_shape=[jax.ShapeDtypeStruct(s, d) for s, d in outs],
        in_specs=specs,
        out_specs=[vmem] * len(outs),
        scratch_shapes=[pltpu.VMEM(s, d) for s, d in scratch],
        compiler_params=pltpu.CompilerParams(vmem_limit_bytes=VMEM_LIMIT),
    )(*args)


def matching(m, count):
    pairs = []
    for i in range(count):
        j = (i ^ 1, ((i + 1) ^ 1) - 1, i ^ 2, ((i + 2) ^ 2) - 2)[m]
        if 0 <= j < count:
            pairs.append((i, j))
    return pairs


def swap(blocks):
    count = lax.axis_size("brick")
    return [lax.ppermute(block, "brick", matching(m, count)) for m, block in enumerate(blocks)]


def total_of(value):
    count = lax.axis_size("brick")
    step = 1
    while step < count:
        value = value + lax.ppermute(value, "brick", [(i, i ^ step) for i in range(count)])
        step *= 2
    return value


def per_device(
    positions, species, pair_first, pair_second, pair_valid, send_list, w_radial, w_first, w_second, w_value, w_env,
    w_latent, w_tensor, w_mix, w_read, read_vec,
):
    brick = lax.axis_index("brick")
    flip_near = brick & 1
    flip_far = (brick >> 1) & 1
    send = jnp.concatenate(
        [
            jnp.where(flip_near == 1, send_list[1::-1], send_list[0:2]),
            jnp.where(flip_far == 1, send_list[3:1:-1], send_list[2:4]),
        ],
        axis=0,
    )
    spec = species[None, :]
    first = pair_first.reshape(1, PAIRS)
    second = pair_second.reshape(1, PAIRS)
    valid = pair_valid.reshape(1, PAIRS)
    slot = second - OWN
    group = slot // GHOST
    group = group ^ jnp.where(group < 2, 1 - flip_near, 1 - flip_far)
    second = jnp.where(second < OWN, second, OWN + group * GHOST + slot % GHOST)
    live_blocks = jnp.sum(pair_valid[:, 0])
    live = ((live_blocks * 128 + CHUNK - 1) // CHUNK).reshape(1, 1)

    message = ((8, GHOST), F32)
    *messages, ohs = call(send_kernel, [message] * 4 + [((OWN, 4 * GHOST), BF16)], positions, spec, send)
    coords = swap(messages)
    embed, evl, tens, mix, read, read_t, mix_t, lt_t, val_t, env_t, rad_t = call(
        weights_kernel,
        [
            (s, BF16)
            for s in (
                (LAT, 64), (2, 2 * CH + LAT, 3 * LAT), (2, LAT, 3 * CH), (2, LAT, 3 * LAT), (LAT, 3 * LAT), (LAT, 3 * LAT),
                (2, LAT, 3 * LAT), (2, LAT + CH, 3 * LAT), (2, LAT, 3 * CH), (2, LAT, 3 * CH), (NB, 3 * LAT),
            )
        ],
        w_radial, w_first, w_second, w_value, w_env, w_latent, w_tensor, w_mix, w_read,
    )

    def rows(n):
        return ((n, PAIRS), F32)

    partials = [((VEC, OWN), F32)] + [((VEC, GHOST), F32)] * 4
    scratch = [((2 * VEC, ROWS), BF16), ((VEC, ROWS), F32)]

    def complete(own, ghosts):
        own, *listed = call(combine_kernel, partials, own, *swap(ghosts), ohs)
        return [own] + swap(listed)

    geo, slope, lat0, evh0, own, *ghosts = call(
        embed_kernel,
        [rows(8), rows(LAT), rows(LAT), rows(2 * CH + LAT)] + partials,
        live, positions, spec, *coords, first, second, valid, embed, evl,
        scratch=[((32, ROWS), BF16), ((VEC, ROWS), F32)],
        smem=1,
    )
    table = complete(own, ghosts)
    gap0, hid0, lat1, evh1, own, *ghosts = call(
        middle_kernel,
        [rows(VEC), rows(LAT), rows(LAT), rows(2 * CH + LAT)] + partials,
        live, *table, first, second, geo, lat0, evh0, evl, tens, mix,
        scratch=scratch, smem=1,
    )
    table = complete(own, ghosts)
    energy, dlat, dgeo, own, *ghosts = call(
        turn_kernel,
        [((8, 128), F32), rows(LAT), rows(8)] + partials,
        live, *table, first, second, geo, lat1, evh1, read_vec[:, None], tens, mix, read, read_t, mix_t, lt_t, val_t,
        scratch=scratch, smem=1,
    )
    table = complete(own, ghosts)
    dlat, dgeo, own, *ghosts = call(
        back_kernel,
        [rows(LAT), rows(8)] + partials,
        live, *table, first, second, geo, evh1, dlat, dgeo, gap0, hid0, evh0, mix_t, lt_t, val_t, env_t,
        scratch=scratch, smem=1,
    )
    table = complete(own, ghosts)
    own, *ghosts = call(
        force_kernel,
        [((8, OWN), F32)] + [((8, GHOST), F32)] * 4,
        live, *table, first, second, geo, evh0, dlat, dgeo, slope, env_t, rad_t,
        scratch=[scratch[0], ((8, ROWS), F32)], smem=1,
    )
    (forces,) = call(final_kernel, [((3, OWN), F32)], own, *swap(ghosts), ohs)
    total = total_of(energy)
    return (forces, total[0, 0] / (lax.axis_size("brick") * PAIRS))


def solution(mesh):
    line = P("brick", None)
    return jax.shard_map(
        per_device,
        mesh=mesh,
        in_specs=(P(None, "brick"), P("brick"), line, line, line, line) + (P(),) * 10,
        out_specs=(P(None, "brick"), P()),
        check_vma=False,
    )
```

```python
import math

import jax
import jax.numpy as jnp
import numpy as np
from jax import lax
from jax.experimental import pallas as pl
from jax.experimental.pallas import tpu as pltpu
from jax.sharding import PartitionSpec as P

F32 = jnp.float32
BF16 = jnp.bfloat16

CUTOFF = 6.0
SOFTENING = 0.25
ENV_SCALE = 0.25
PAIR_SHIFT = 1.0

LAT = 64
CH = 32
NB = 8
VEC = 3 * CH
OWN = 512
GHOST = 256
ROWS = OWN + 4 * GHOST
WIN = 256
BRICK_BLOCKS = 48
PAIRS = BRICK_BLOCKS * 128
CHUNK = 2048
CHUNK_BLOCKS = CHUNK // 128
WIDE = 128

VMEM_LIMIT = 12 * 1024 * 1024


def fit_trig():
    r = np.cos(np.linspace(0.0, np.pi, 4001)) * 0.5
    x = r * r
    base = np.polynomial.chebyshev.Chebyshev
    safe = np.where(r == 0.0, 1.0, r)
    sine = np.where(r == 0.0, 2 * np.pi, np.sin(2 * np.pi * safe) / safe)
    s = base.fit(x, sine, 8, domain=[0.0, 0.25]).convert(kind=np.polynomial.Polynomial)
    c = base.fit(x, np.cos(2 * np.pi * r), 8, domain=[0.0, 0.25]).convert(kind=np.polynomial.Polynomial)
    return [float(v) for v in s.coef], [float(v) for v in c.coef]


SIN_COEF, COS_COEF = fit_trig()


def horner(coef, x):
    out = jnp.full_like(x, coef[-1])
    for c in coef[-2::-1]:
        out = out * x + c
    return out


def dot(a, b):
    return lax.dot_general(a, b, (((1,), (0,)), ((), ())), preferred_element_type=F32)


def dot_nt(a, b):
    return lax.dot_general(a, b, (((1,), (1,)), ((), ())), preferred_element_type=F32)


def split2(x):
    hi = x.astype(BF16)
    lo = (x - hi.astype(F32)).astype(BF16)
    return hi, lo


def split3(x):
    hi = x.astype(BF16).astype(F32)
    rest = x - hi
    mid = rest.astype(BF16).astype(F32)
    return hi, mid, (rest - mid)


def stack2(x):
    hi, lo = split2(x)
    return jnp.concatenate([hi, lo], axis=0)


def spread2(x):
    hi, lo = split2(x)
    pad = jnp.zeros((WIDE - x.shape[0], x.shape[1]), BF16)
    return jnp.concatenate([hi, pad, lo, pad], axis=0)


def weight3(w):
    hi, lo = split2(w)
    return jnp.concatenate([hi.astype(F32), hi.astype(F32), lo.astype(F32)], axis=1).astype(BF16)


def dense(w3, x):
    hi, lo = split2(x)
    return dot(w3, jnp.concatenate([hi, lo, hi], axis=0))


def sigmoid(x):
    return 0.5 * jnp.tanh(0.5 * x) + 0.5


def silu_and_slope(x):
    s = sigmoid(x)
    y = x * s
    return y, s + y * (1.0 - s)


def hot(ids, rows):
    at = lax.broadcasted_iota(jnp.int32, (rows, ids.shape[1]), 0)
    return jnp.where(at == ids, 1.0, 0.0).astype(BF16)


def window_hot(ids, window, value, at):
    local = jnp.clip(ids - window * WIN, -1, WIN).astype(F32).astype(BF16)
    return jnp.where(at == local, jnp.full((), value, BF16), jnp.zeros((), BF16))


def fold2(x):
    half = x.shape[0] // 2
    return x[:half] + x[half:]


def radial(dist):
    k = (lax.broadcasted_iota(jnp.int32, (NB, dist.shape[1]), 0) + 1).astype(F32)
    turns = k * (dist * (1.0 / (2.0 * CUTOFF)))
    r = turns - jnp.round(turns)
    x = r * r
    return r * horner(SIN_COEF, x), horner(COS_COEF, x), k * (math.pi / CUTOFF)


def lanes(c):
    return pl.ds(pl.multiple_of(c * CHUNK, CHUNK), CHUNK)


def weigh(geo, values):
    return jnp.concatenate([geo[m : m + 1] * values for m in range(3)], axis=0)


def project(geo, vectors):
    return (
        geo[0:1] * vectors[:CH]
        + geo[1:2] * vectors[CH : 2 * CH]
        + geo[2:3] * vectors[2 * CH :]
    )


def put_rows(rows, n):
    at = lax.broadcasted_iota(jnp.int32, (8, n), 0)
    out = jnp.zeros((8, n), F32)
    for i, row in enumerate(rows):
        out = jnp.where(at == i, row, out)
    return out


def dir_grad(dq, vectors):
    return [jnp.sum(dq * vectors[m * CH : (m + 1) * CH], axis=0, keepdims=True) for m in range(3)]


def fill_table(table_ref, own_ref, ghost_refs):
    hi, lo = split2(own_ref[...])
    table_ref[:VEC, :OWN] = hi
    table_ref[VEC:, :OWN] = lo
    for m, ghost in enumerate(ghost_refs):
        hi, lo = split2(ghost[...])
        at = OWN + m * GHOST
        table_ref[:VEC, at : at + GHOST] = hi
        table_ref[VEC:, at : at + GHOST] = lo


def gather(table_ref, oh):
    return fold2(dot(table_ref[...], oh))


def scatter(acc_ref, vectors, oh):
    acc_ref[...] += dot_nt(oh, spread2(vectors))


def emit(acc_ref, own_out, ghost_outs):
    rows = own_out.shape[0]
    own_out[...] = (acc_ref[:OWN, :WIDE] + acc_ref[:OWN, WIDE:]).T[:rows]
    for m, out in enumerate(ghost_outs):
        at = OWN + m * GHOST
        out[...] = (acc_ref[at : at + GHOST, :WIDE] + acc_ref[at : at + GHOST, WIDE:]).T[:rows]


def fetch(sources, targets, sems):
    copies = [pltpu.make_async_copy(a, b, sems.at[i]) for i, (a, b) in enumerate(zip(sources, targets))]
    for copy in copies:
        copy.start()
    for copy in copies:
        copy.wait()


def send_kernel(
    flip_ref, pos_in, spec_in, send_in, valid_in, m0, m1, m2, m3, ohs_ref, live_ref, atoms_ref,
    pos_ref, spec_ref, send_ref, valid_ref, sems,
):
    fetch((pos_in, spec_in, send_in, valid_in), (pos_ref, spec_ref, send_ref, valid_ref), sems)
    live = jnp.sum(valid_ref[:, 0:1].astype(F32)).astype(jnp.int32)
    live_ref[0, 0] = (live + CHUNK_BLOCKS - 1) // CHUNK_BLOCKS
    columns = []
    for m in range(4):
        other = jnp.full((1, GHOST), flip_ref[0, m // 2], jnp.int32) == 1
        ids = jnp.where(other, send_ref[m ^ 1 : (m ^ 1) + 1, :], send_ref[m : m + 1, :])
        columns.append(hot(ids, OWN))
    oh = jnp.concatenate(columns, axis=1)
    ohs_ref[...] = oh
    hi, mid, lo = split3(pos_ref[...])
    rows = jnp.concatenate(
        [
            put_rows([hi[i : i + 1] for i in range(3)] + [spec_ref[...].astype(F32)], OWN),
            put_rows([mid[i : i + 1] for i in range(3)], OWN),
            put_rows([lo[i : i + 1] for i in range(3)], OWN),
            jnp.zeros((8, OWN), F32),
        ],
        axis=0,
    ).astype(BF16)
    atoms_ref[...] = rows
    got = dot(rows, oh)
    got = got[0:8] + got[8:16] + got[16:24]
    for m, out in enumerate((m0, m1, m2, m3)):
        out[...] = got[:, m * GHOST : (m + 1) * GHOST]


def prepare_kernel(
    flip_ref, live_ref, *refs
):
    sources, refs = refs[:14], refs[14:]
    oh_ref, info_ref, embed, evl, tens, mix, read, read_t, mix_t, lt_t, val_t, env_t, rad_t, column = refs[:14]
    fetch(sources, refs[14:28], refs[28])
    (
        spec_ref, first_ref, second_ref, valid_ref,
        w_radial_t, w_first_t, w_second_t, w_value, w_env, w_latent, w_tensor_t, w_mix, w_read, read_vec,
    ) = refs[14:28]

    def parts(w):
        hi, lo = split2(w)
        return hi.astype(F32), lo.astype(F32)

    rh, rl = parts(w_radial_t[...].T)
    fh, fl = parts(w_first_t[...].T)
    sh, sl = parts(w_second_t[...].T)
    embed[...] = jnp.concatenate([rh, rh, rl, fh, sh, fl, sl, jnp.zeros_like(rh)], axis=1).astype(BF16)
    for l in range(2):
        evl[l] = weight3(jnp.concatenate([w_env[l], w_value[l], w_latent[l]], axis=0))
        tens[l] = weight3(w_tensor_t[l].T)
        mix[l] = weight3(w_mix[l])
        mix_t[l] = weight3(w_mix[l].T)
        lt_t[l] = weight3(jnp.concatenate([w_latent[l].T, w_tensor_t[l]], axis=0))
        val_t[l] = weight3(w_value[l].T)
        env_t[l] = weight3(w_env[l].T)
    read[...] = weight3(w_read[...])
    read_t[...] = weight3(w_read[...].T)
    rad_t[...] = weight3(w_radial_t[...])
    diagonal = lax.broadcasted_iota(jnp.int32, (LAT, LAT), 0) == lax.broadcasted_iota(jnp.int32, (LAT, LAT), 1)
    column[...] = jnp.sum(jnp.where(diagonal, read_vec[...], 0.0), axis=1, keepdims=True)

    own_kinds = jnp.broadcast_to(spec_ref[...], (16, OWN)).astype(F32).astype(BF16)
    span = 512
    at = lax.broadcasted_iota(jnp.int32, (WIN, span), 0).astype(F32).astype(BF16)
    near, far = 1 - flip_ref[0, 0], 1 - flip_ref[0, 1]

    def body(c, carry):
        blocks = [pl.ds(c * (span // 128) + i, 1) for i in range(span // 128)]
        first = jnp.concatenate([first_ref[b, :] for b in blocks], axis=1)
        second = jnp.concatenate([second_ref[b, :] for b in blocks], axis=1)
        slot = second - OWN
        group = slot >> 8
        group = group ^ jnp.where(group < 2, near, far)
        second = jnp.where(second < OWN, second, OWN + group * GHOST + (slot & (GHOST - 1)))
        out = pl.ds(pl.multiple_of(c * span, span), span)
        firsts = []
        for w in range(ROWS // WIN):
            tile = window_hot(second, w, -1.0, at)
            if w < OWN // WIN:
                firsts.append(window_hot(first, w, 1.0, at))
                tile = tile + firsts[-1]
            oh_ref[w * WIN : (w + 1) * WIN, out] = tile
        info_ref[0:8, out] = dot(own_kinds, jnp.concatenate(firsts, axis=0))[0:8]
        valid = jnp.concatenate([valid_ref[b, :] for b in blocks], axis=1).astype(F32)
        info_ref[8:16, out] = jnp.broadcast_to(valid, (8, span))
        return carry

    lax.fori_loop(0, live_ref[0, 0] * (CHUNK // span), body, 0)


def embed_kernel(
    live_ref, own_ref, c0, c1, c2, c3, oh_ref, info_ref, w_embed, w_evl,
    geo_out, slope_out, lat_out, evh_out, own_out, g0, g1, g2, g3, atoms_ref, acc_ref,
):
    def put(at, width, coords):
        hi, mid, lo = split3(coords)
        atoms_ref[:, at : at + width] = jnp.concatenate([hi, mid, lo, jnp.zeros_like(hi)], axis=0).astype(BF16)

    atoms_ref[:, :OWN] = own_ref[...]
    for m, c in enumerate((c0, c1, c2, c3)):
        put(OWN + m * GHOST, GHOST, c[...])
    acc_ref[...] = jnp.zeros_like(acc_ref)

    def body(c, carry):
        at = lanes(c)
        mask = info_ref[8:9, at]
        oh = oh_ref[:, at]
        gap = dot(atoms_ref[...], oh)
        gap = gap[0:8] + gap[8:16] + gap[16:24]
        row = lax.broadcasted_iota(jnp.int32, (8, CHUNK), 0)
        diff = jnp.where(row < 3, -gap, 0.0)
        sq = jnp.sum(diff * diff, axis=0, keepdims=True) + SOFTENING
        dist = jnp.sqrt(sq)
        inv = 1.0 / dist
        shrink = 1.0 - sq * (1.0 / CUTOFF**2)
        env = shrink * shrink
        direction = diff * inv
        weight = env * mask
        geo = direction + jnp.where(row == 3, weight, 0.0) + jnp.where(row == 4, dist, 0.0)
        geo = geo + jnp.where(row == 5, mask, 0.0)
        geo_out[:, at] = geo
        sines, _, _ = radial(dist)
        basis = sines * (inv * env)
        bh = basis.astype(BF16).astype(F32)
        bl = basis - bh
        rowf = row.astype(F32)
        kind = info_ref[0:8, at]
        sf = jnp.where(rowf == kind, 1.0, 0.0)
        ss = jnp.where(rowf == kind - gap[3:4], 1.0, 0.0)
        pre = dot(
            w_embed[...],
            jnp.concatenate([bh, bl, bh, sf, ss, sf, ss, jnp.zeros_like(bh)], axis=0).astype(BF16),
        )
        lat, slope = silu_and_slope(pre)
        slope_out[:, at] = slope
        lat_out[:, at] = lat
        evh = dense(w_evl[0], lat)
        evh_out[:, at] = evh
        scatter(acc_ref, weigh(geo, evh[:CH] * weight), oh)
        return carry

    lax.fori_loop(0, live_ref[0, 0], body, 0)
    emit(acc_ref, own_out, (g0, g1, g2, g3))

def combine_kernel(own_ref, r0, r1, r2, r3, ohs_ref, own_out, g0, g1, g2, g3):
    arrived = jnp.concatenate([r[...] for r in (r0, r1, r2, r3)], axis=1)
    owned = own_ref[...] + fold2(dot_nt(stack2(arrived), ohs_ref[...]))
    own_out[...] = owned
    ghosts = fold2(dot(stack2(owned), ohs_ref[...]))
    for m, out in enumerate((g0, g1, g2, g3)):
        out[...] = ghosts[:, m * GHOST : (m + 1) * GHOST]


def middle_kernel(
    live_ref, own_ref, t0, t1, t2, t3, oh_ref, geo_ref, lat_ref, evh_ref, w_evl, w_tens, w_mix,
    gap_out, hid_out, lat_out, evh_out, own_out, g0, g1, g2, g3, table_ref, acc_ref,
):
    fill_table(table_ref, own_ref, (t0, t1, t2, t3))
    acc_ref[...] = jnp.zeros_like(acc_ref)

    def body(c, carry):
        at = lanes(c)
        oh = oh_ref[:, at]
        gap = gather(table_ref, oh)
        gap_out[:, at] = gap
        geo = geo_ref[:, at]
        scalars = (ENV_SCALE * evh_ref[CH : 2 * CH, at]) * project(geo, gap)
        hid = evh_ref[2 * CH :, at] + dense(w_tens[0], scalars)
        hid_out[:, at] = hid
        lat = lat_ref[:, at] + dense(w_mix[0], hid * sigmoid(hid))
        lat_out[:, at] = lat
        evh = dense(w_evl[1], lat)
        evh_out[:, at] = evh
        vec = weigh(geo, evh[:CH] * geo[3:4])
        scatter(acc_ref, vec, oh)
        return carry

    lax.fori_loop(0, live_ref[0, 0], body, 0)
    emit(acc_ref, own_out, (g0, g1, g2, g3))


def update_back(geo, gap, values, hid_slope, dlat, w_mix_t, w_lt_t, w_val_t):
    dhid = dense(w_mix_t, dlat) * hid_slope
    both = dense(w_lt_t, dhid)
    dscal = both[LAT:] * ENV_SCALE
    dval = project(geo, gap) * dscal
    dq = values * dscal
    return dlat + both[:LAT] + dense(w_val_t, dval), dq


def turn_kernel(
    live_ref, own_ref, t0, t1, t2, t3, oh_ref, geo_ref, lat_ref, evh_ref, read_vec, w_tens, w_mix, w_read,
    w_read_t, w_mix_t, w_lt_t, w_val_t,
    energy_out, dlat_out, dgeo_out, own_out, g0, g1, g2, g3, table_ref, acc_ref,
):
    fill_table(table_ref, own_ref, (t0, t1, t2, t3))
    acc_ref[...] = jnp.zeros_like(acc_ref)
    rv = read_vec[...]

    def body(c, energy):
        at = lanes(c)
        oh = oh_ref[:, at]
        gap = gather(table_ref, oh)
        geo = geo_ref[:, at]
        weight = geo[3:4]
        values = evh_ref[CH : 2 * CH, at]
        scalars = (ENV_SCALE * values) * project(geo, gap)
        hid = evh_ref[2 * CH :, at] + dense(w_tens[1], scalars)
        act, hid_slope = silu_and_slope(hid)
        lat = lat_ref[:, at] + dense(w_mix[1], act)
        out, out_slope = silu_and_slope(dense(w_read[...], lat))
        pair_energy = jnp.sum(rv * out, axis=0, keepdims=True) + PAIR_SHIFT
        dlat = dense(w_read_t[...], out_slope * (rv * weight))
        dlat, dq = update_back(geo, gap, values, hid_slope, dlat, w_mix_t[1], w_lt_t[1], w_val_t[1])
        dlat_out[:, at] = dlat
        dgeo_out[:, at] = put_rows(dir_grad(dq, gap) + [pair_energy], CHUNK)
        scatter(acc_ref, weigh(geo, dq), oh)
        return energy + pair_energy * weight

    energy = lax.fori_loop(0, live_ref[0, 0], body, jnp.zeros((1, CHUNK), F32))
    energy_out[...] = jnp.broadcast_to(jnp.sum(energy, axis=1, keepdims=True), energy_out.shape)
    emit(acc_ref, own_out, (g0, g1, g2, g3))


def environment_back(geo, dvec, env_values, dlat, dgeo, w_env_t):
    weight = geo[3:4]
    dscaled = project(geo, dvec)
    rows = dir_grad(env_values * weight, dvec)
    rows.append(jnp.sum(env_values * dscaled, axis=0, keepdims=True))
    return dlat + dense(w_env_t, dscaled * weight), dgeo + put_rows(rows, CHUNK)


def back_kernel(
    live_ref, own_ref, t0, t1, t2, t3, oh_ref, geo_ref, evh1_ref, dlat_ref, dgeo_ref, gap_ref, hid_ref,
    evh0_ref, w_mix_t, w_lt_t, w_val_t, w_env_t,
    dlat_out, dgeo_out, own_out, g0, g1, g2, g3, table_ref, acc_ref,
):
    fill_table(table_ref, own_ref, (t0, t1, t2, t3))
    acc_ref[...] = jnp.zeros_like(acc_ref)

    def body(c, carry):
        at = lanes(c)
        oh = oh_ref[:, at]
        dvec = gather(table_ref, oh)
        geo = geo_ref[:, at]
        dlat, dgeo = environment_back(geo, dvec, evh1_ref[:CH, at], dlat_ref[:, at], dgeo_ref[:, at], w_env_t[1])
        gap = gap_ref[:, at]
        _, hid_slope = silu_and_slope(hid_ref[:, at])
        dlat, dq = update_back(geo, gap, evh0_ref[CH : 2 * CH, at], hid_slope, dlat, w_mix_t[0], w_lt_t[0], w_val_t[0])
        dlat_out[:, at] = dlat
        dgeo_out[:, at] = dgeo + put_rows(dir_grad(dq, gap), CHUNK)
        scatter(acc_ref, weigh(geo, dq), oh)
        return carry

    lax.fori_loop(0, live_ref[0, 0], body, 0)
    emit(acc_ref, own_out, (g0, g1, g2, g3))


def force_kernel(
    live_ref, own_ref, t0, t1, t2, t3, oh_ref, geo_ref, evh0_ref, dlat_ref, dgeo_ref, slope_ref,
    w_env_t, w_rad_t,
    own_out, g0, g1, g2, g3, table_ref, acc_ref,
):
    fill_table(table_ref, own_ref, (t0, t1, t2, t3))
    acc_ref[...] = jnp.zeros_like(acc_ref)

    def body(c, carry):
        at = lanes(c)
        oh = oh_ref[:, at]
        dvec = gather(table_ref, oh)
        geo = geo_ref[:, at]
        dlat, dgeo = environment_back(geo, dvec, evh0_ref[:CH, at], dlat_ref[:, at], dgeo_ref[:, at], w_env_t[0])
        dbasis = dense(w_rad_t[...], dlat * slope_ref[:, at])
        dist, mask = geo[4:5], geo[5:6]
        inv = 1.0 / dist
        shrink = 1.0 - dist * dist * (1.0 / CUTOFF**2)
        env = shrink * shrink
        sines, cosines, freq = radial(dist)
        along = jnp.sum(dbasis * sines, axis=0, keepdims=True) * inv
        ddist = (jnp.sum(dbasis * (freq * cosines), axis=0, keepdims=True) - along) * (inv * env)
        denv = along + mask * dgeo[3:4]
        ddist = ddist - denv * shrink * dist * (4.0 / CUTOFF**2)
        row = lax.broadcasted_iota(jnp.int32, (8, CHUNK), 0)
        unit = jnp.where(row < 3, geo, 0.0)
        dunit = jnp.where(row < 3, dgeo, 0.0)
        radial_part = ddist - jnp.sum(unit * dunit, axis=0, keepdims=True) * inv
        ddiff = dunit * inv + unit * radial_part
        hi = ddiff.astype(BF16).astype(F32)
        both = jnp.concatenate([hi, ddiff - hi], axis=0).astype(BF16)
        acc_ref[...] += fold2(dot_nt(both, oh))
        return carry

    lax.fori_loop(0, live_ref[0, 0], body, 0)
    own_out[...] = acc_ref[:, :OWN]
    for m, out in enumerate((g0, g1, g2, g3)):
        at = OWN + m * GHOST
        out[...] = acc_ref[:, at : at + GHOST]


def final_kernel(own_ref, r0, r1, r2, r3, ohs_ref, out_ref):
    arrived = jnp.concatenate([r[...] for r in (r0, r1, r2, r3)], axis=1)
    hi, mid, lo = split3(arrived)
    parts = jnp.concatenate([hi, mid, lo, jnp.zeros_like(hi)], axis=0).astype(BF16)
    got = dot_nt(parts, ohs_ref[...])
    out_ref[...] = (own_ref[...] + got[0:8] + got[8:16] + got[16:24])[0:3]


def call(kernel, outs, *args, scratch=(), smem=0, fetched=0):
    vmem = pl.BlockSpec(memory_space=pltpu.VMEM)
    scalar = pl.BlockSpec(memory_space=pltpu.SMEM)
    anywhere = pl.BlockSpec(memory_space=pltpu.HBM)
    held = len(args) - fetched
    args = args[:held] + tuple(pltpu.with_memory_space_constraint(a, pltpu.HBM) for a in args[held:])
    buffers = [pltpu.VMEM(a.shape, a.dtype) for a in args[len(args) - fetched :]]
    if fetched:
        buffers.append(pltpu.SemaphoreType.DMA((fetched,)))
    return pl.pallas_call(
        kernel,
        out_shape=[jax.ShapeDtypeStruct(s, d) for s, d in outs],
        in_specs=[scalar] * smem + [vmem] * (len(args) - smem - fetched) + [anywhere] * fetched,
        out_specs=[scalar if d == jnp.int32 else vmem for _, d in outs],
        scratch_shapes=buffers + [pltpu.VMEM(s, d) for s, d in scratch],
        compiler_params=pltpu.CompilerParams(vmem_limit_bytes=VMEM_LIMIT),
    )(*args)


def matching(m, count):
    pairs = []
    for i in range(count):
        j = (i ^ 1, ((i + 1) ^ 1) - 1, i ^ 2, ((i + 2) ^ 2) - 2)[m]
        if 0 <= j < count:
            pairs.append((i, j))
    return pairs


def exchange(blocks):
    count = lax.axis_size("brick")
    got = [None] * 4
    for m in (2, 3, 1, 0):
        got[m] = lax.ppermute(blocks[m], "brick", matching(m, count))
    return got


def exchange_and_add(blocks, energy, step):
    blocks, energy = lax.optimization_barrier((blocks, energy))
    energy = add_across(energy, step)
    return exchange(blocks), energy


def add_across(value, step):
    count = lax.axis_size("brick")
    if step >= count:
        return value
    return value + lax.ppermute(value, "brick", [(i, i ^ step) for i in range(count)])


def per_device(
    positions, species, pair_first, pair_second, pair_valid, send_list, w_radial, w_first, w_second, w_value, w_env,
    w_latent, w_tensor, w_mix, w_read, read_vec,
):
    brick = lax.axis_index("brick")
    flips = jnp.stack([brick & 1, (brick >> 1) & 1]).reshape(1, 2)
    spec = species[None, :]

    message = ((8, GHOST), F32)
    *messages, ohs, live, atoms = call(
        send_kernel,
        [message] * 4 + [((OWN, 4 * GHOST), BF16), ((1, 1), jnp.int32), ((32, OWN), BF16)],
        flips, positions, spec, send_list, pair_valid, smem=1, fetched=4,
    )
    coords = exchange(messages)
    shapes = (
        (LAT, 64), (2, 2 * CH + LAT, 3 * LAT), (2, LAT, 3 * CH), (2, LAT, 3 * LAT), (LAT, 3 * LAT), (LAT, 3 * LAT),
        (2, LAT, 3 * LAT), (2, LAT + CH, 3 * LAT), (2, LAT, 3 * CH), (2, LAT, 3 * CH), (NB, 3 * LAT),
    )
    oh, info, embed, evl, tens, mix, read, read_t, mix_t, lt_t, val_t, env_t, rad_t, column = call(
        prepare_kernel,
        [((ROWS, PAIRS), BF16), ((16, PAIRS), F32)]
        + [(s, BF16) for s in shapes]
        + [((LAT, 1), F32)],
        flips, live, spec, pair_first, pair_second, pair_valid, w_radial.T, w_first.T, w_second.T, w_value, w_env, w_latent,
        jnp.swapaxes(w_tensor, 1, 2), w_mix, w_read, read_vec[None, :],
        smem=2, fetched=14,
    )

    def rows(n):
        return ((n, PAIRS), F32)

    partials = [((VEC, OWN), F32)] + [((VEC, GHOST), F32)] * 4
    scratch = [((2 * VEC, ROWS), BF16), ((ROWS, 2 * WIDE), F32)]

    def combine(own, arrived):
        own, *listed = call(combine_kernel, partials, own, *arrived, ohs)
        return own, listed

    def complete(own, ghosts):
        own, listed = combine(own, exchange(ghosts))
        return [own] + exchange(listed)

    def complete_and_add(own, ghosts, energy, steps):
        arrived, energy = exchange_and_add(ghosts, energy, steps[0])
        own, listed = combine(own, arrived)
        listed, energy = exchange_and_add(listed, energy, steps[1])
        return [own] + listed, energy

    geo, slope, lat0, evh0, own, *ghosts = call(
        embed_kernel,
        [rows(8), rows(LAT), rows(LAT), rows(2 * CH + LAT)] + partials,
        live, atoms, *coords, oh, info, embed, evl,
        scratch=[((32, ROWS), BF16), scratch[1]],
        smem=1,
    )
    table = complete(own, ghosts)
    gap0, hid0, lat1, evh1, own, *ghosts = call(
        middle_kernel,
        [rows(VEC), rows(LAT), rows(LAT), rows(2 * CH + LAT)] + partials,
        live, *table, oh, geo, lat0, evh0, evl, tens, mix,
        scratch=scratch, smem=1,
    )
    table = complete(own, ghosts)
    energy, dlat, dgeo, own, *ghosts = call(
        turn_kernel,
        [((8, 128), F32), rows(LAT), rows(8)] + partials,
        live, *table, oh, geo, lat1, evh1, column, tens, mix, read, read_t, mix_t, lt_t, val_t,
        scratch=scratch, smem=1,
    )
    energy = add_across(energy, 1)
    table, energy = complete_and_add(own, ghosts, energy, (2, 4))
    dlat, dgeo, own, *ghosts = call(
        back_kernel,
        [rows(LAT), rows(8)] + partials,
        live, *table, oh, geo, evh1, dlat, dgeo, gap0, hid0, evh0, mix_t, lt_t, val_t, env_t,
        scratch=scratch, smem=1,
    )
    table, energy = complete_and_add(own, ghosts, energy, (8, 16))
    own, *ghosts = call(
        force_kernel,
        [((8, OWN), F32)] + [((8, GHOST), F32)] * 4,
        live, *table, oh, geo, evh0, dlat, dgeo, slope, env_t, rad_t,
        scratch=[scratch[0], ((8, ROWS), F32)], smem=1,
    )
    arrived, energy = exchange_and_add(ghosts, energy, 32)
    (forces,) = call(final_kernel, [((3, OWN), F32)], own, *arrived, ohs)
    total = add_across(energy, 64)
    return (forces, total[0, 0] / (lax.axis_size("brick") * PAIRS))


def solution(mesh):
    line = P("brick", None)
    return jax.shard_map(
        per_device,
        mesh=mesh,
        in_specs=(P(None, "brick"), P("brick"), line, line, line, line) + (P(),) * 10,
        out_specs=(P(None, "brick"), P()),
        check_vma=False,
    )
```

```python
import math

import jax
import jax.numpy as jnp
import numpy as np
from jax import lax
from jax.experimental import pallas as pl
from jax.experimental.pallas import tpu as pltpu
from jax.sharding import PartitionSpec as P

F32 = jnp.float32
BF16 = jnp.bfloat16
ID = jnp.int32

CUTOFF = 6.0
SOFTENING = 0.25
ENV_SCALE = 0.25
PAIR_SHIFT = 1.0

LAT = 64
CH = 32
NB = 8
VEC = 3 * CH
OWN = 512
GHOST = 256
ROWS = OWN + 4 * GHOST
WIN = 256
BRICK_BLOCKS = 48
PAIRS = BRICK_BLOCKS * 128
CHUNK = 2048
CHUNK_BLOCKS = CHUNK // 128
WIDE = 128

VMEM_LIMIT = 7 * 1024 * 1024


def fit_trig():
    r = np.cos(np.linspace(0.0, np.pi, 4001)) * 0.5
    x = r * r
    base = np.polynomial.chebyshev.Chebyshev
    safe = np.where(r == 0.0, 1.0, r)
    sine = np.where(r == 0.0, 2 * np.pi, np.sin(2 * np.pi * safe) / safe)
    s = base.fit(x, sine, 8, domain=[0.0, 0.25]).convert(kind=np.polynomial.Polynomial)
    c = base.fit(x, np.cos(2 * np.pi * r), 8, domain=[0.0, 0.25]).convert(kind=np.polynomial.Polynomial)
    return [float(v) for v in s.coef], [float(v) for v in c.coef]


SIN_COEF, COS_COEF = fit_trig()


def horner(coef, x):
    out = jnp.full_like(x, coef[-1])
    for c in coef[-2::-1]:
        out = out * x + c
    return out


def dot(a, b):
    return lax.dot_general(a, b, (((1,), (0,)), ((), ())), preferred_element_type=F32)


def dot_nt(a, b):
    return lax.dot_general(a, b, (((1,), (1,)), ((), ())), preferred_element_type=F32)


def split2(x):
    hi = x.astype(BF16)
    lo = (x - hi.astype(F32)).astype(BF16)
    return hi, lo


def split3(x):
    hi = x.astype(BF16).astype(F32)
    rest = x - hi
    mid = rest.astype(BF16).astype(F32)
    return hi, mid, (rest - mid)


def stack2(x):
    hi, lo = split2(x)
    return jnp.concatenate([hi, lo], axis=0)


def spread2(x):
    hi, lo = split2(x)
    pad = jnp.zeros((WIDE - x.shape[0], x.shape[1]), BF16)
    return jnp.concatenate([hi, pad, lo, pad], axis=0)


def weight3(w):
    hi, lo = split2(w)
    return jnp.concatenate([hi.astype(F32), hi.astype(F32), lo.astype(F32)], axis=1).astype(BF16)


def dense(w3, x):
    hi, lo = split2(x)
    return dot(w3, jnp.concatenate([hi, lo, hi], axis=0))


def sigmoid(x):
    return 0.5 * jnp.tanh(0.5 * x) + 0.5


def silu_and_slope(x):
    s = sigmoid(x)
    y = x * s
    return y, s + y * (1.0 - s)


def hot(ids, rows):
    at = lax.broadcasted_iota(jnp.int32, (rows, ids.shape[1]), 0)
    return jnp.where(at == ids, 1.0, 0.0).astype(BF16)


def window_hot(ids, window, value, at):
    local = jnp.clip(ids - window * WIN, -1, WIN).astype(F32).astype(BF16)
    return jnp.where(at == local, jnp.full((), value, BF16), jnp.zeros((), BF16))


def fold2(x):
    half = x.shape[0] // 2
    return x[:half] + x[half:]


def radial(dist):
    k = (lax.broadcasted_iota(jnp.int32, (NB, dist.shape[1]), 0) + 1).astype(F32)
    turns = k * (dist * (1.0 / (2.0 * CUTOFF)))
    r = turns - jnp.round(turns)
    x = r * r
    return r * horner(SIN_COEF, x), horner(COS_COEF, x), k * (math.pi / CUTOFF)


def lanes(c):
    return pl.ds(pl.multiple_of(c * CHUNK, CHUNK), CHUNK)


def weigh(geo, values):
    return jnp.concatenate([geo[m : m + 1] * values for m in range(3)], axis=0)


def project(geo, vectors):
    return (
        geo[0:1] * vectors[:CH]
        + geo[1:2] * vectors[CH : 2 * CH]
        + geo[2:3] * vectors[2 * CH :]
    )


def put_rows(rows, n):
    at = lax.broadcasted_iota(jnp.int32, (8, n), 0)
    out = jnp.zeros((8, n), F32)
    for i, row in enumerate(rows):
        out = jnp.where(at == i, row, out)
    return out


def dir_grad(dq, vectors):
    return [jnp.sum(dq * vectors[m * CH : (m + 1) * CH], axis=0, keepdims=True) for m in range(3)]


def fill_table(table_ref, ghost_refs):
    for m, ghost in enumerate(ghost_refs):
        hi, lo = split2(ghost[...])
        at = m * GHOST
        table_ref[:VEC, at : at + GHOST] = hi
        table_ref[VEC:, at : at + GHOST] = lo


def gather_ghosts(own_gap_ref, table_ref, oh_ref, at):
    return own_gap_ref[:, at] + fold2(dot(table_ref[...], oh_ref[OWN:, at]))


def scatter_ghosts(acc_ref, parts_out, parts, oh_ref, at):
    parts_out[:, at] = parts
    acc_ref[...] += dot_nt(oh_ref[OWN:, at], parts)


def emit(acc_ref, ghost_outs):
    for m, out in enumerate(ghost_outs):
        out[...] = join_parts(acc_ref[m * GHOST : (m + 1) * GHOST, :], out.shape[0])


def join_parts(acc, rows):
    if acc.shape[1] == WIDE:
        turned = acc.T
        return turned[:rows] + turned[rows : 2 * rows]
    return (acc[:, :WIDE] + acc[:, WIDE:]).T[:rows]


def fetch(sources, targets, sems):
    copies = [pltpu.make_async_copy(a, b, sems.at[i]) for i, (a, b) in enumerate(zip(sources, targets))]
    for copy in copies:
        copy.start()
    for copy in copies:
        copy.wait()


def send_kernel(
    flip_ref, pos_in, spec_in, send_in, valid_in, m0, m1, m2, m3, ohs_ref, live_ref, atoms_ref,
    pos_ref, spec_ref, send_ref, valid_ref, sems,
):
    fetch((pos_in, spec_in, send_in, valid_in), (pos_ref, spec_ref, send_ref, valid_ref), sems)
    live = jnp.sum(valid_ref[:, 0:1].astype(F32)).astype(jnp.int32)
    live_ref[0, 0] = (live + CHUNK_BLOCKS - 1) // CHUNK_BLOCKS
    columns = []
    for m in range(4):
        other = jnp.full((1, GHOST), flip_ref[0, m // 2], jnp.int32) == 1
        ids = jnp.where(other, send_ref[m ^ 1 : (m ^ 1) + 1, :], send_ref[m : m + 1, :])
        columns.append(hot(ids, OWN))
    oh = jnp.concatenate(columns, axis=1)
    ohs_ref[...] = oh
    atoms = put_rows([pos_ref[i : i + 1, :] for i in range(3)] + [spec_ref[...].astype(F32)], OWN)
    atoms_ref[...] = atoms
    hi, mid, lo = split3(atoms)
    got = dot(jnp.concatenate([hi, mid, lo, jnp.zeros_like(hi)], axis=0).astype(BF16), oh)
    got = got[0:8] + got[8:16] + got[16:24]
    for m, out in enumerate((m0, m1, m2, m3)):
        out[...] = got[:, m * GHOST : (m + 1) * GHOST]


def prepare_kernel(
    flip_ref, live_ref, *refs
):
    sources, refs = refs[:13], refs[13:]
    oh_ref, ids_ref, mask_ref, embed, evl, tens, mix, read, read_t, mix_t, lt_t, val_t, env_t, rad_t, column = refs[:15]
    fetch(sources, refs[15:28], refs[28])
    (
        first_ref, second_ref, valid_ref,
        w_radial_t, w_first_t, w_second_t, w_value, w_env, w_latent, w_tensor_t, w_mix, w_read, read_vec,
    ) = refs[15:28]

    def parts(w):
        hi, lo = split2(w)
        return hi.astype(F32), lo.astype(F32)

    rh, rl = parts(w_radial_t[...].T)
    fh, fl = parts(w_first_t[...].T)
    sh, sl = parts(w_second_t[...].T)
    embed[...] = jnp.concatenate([rh, rh, rl, fh, sh, fl, sl, jnp.zeros_like(rh)], axis=1).astype(BF16)
    for l in range(2):
        evl[l] = weight3(jnp.concatenate([w_env[l], w_value[l], w_latent[l]], axis=0))
        tens[l] = weight3(w_tensor_t[l].T)
        mix[l] = weight3(w_mix[l])
        mix_t[l] = weight3(w_mix[l].T)
        lt_t[l] = weight3(jnp.concatenate([w_latent[l].T, w_tensor_t[l]], axis=0))
        val_t[l] = weight3(w_value[l].T)
        env_t[l] = weight3(w_env[l].T)
    read[...] = weight3(w_read[...])
    read_t[...] = weight3(w_read[...].T)
    rad_t[...] = weight3(w_radial_t[...])
    diagonal = lax.broadcasted_iota(jnp.int32, (LAT, LAT), 0) == lax.broadcasted_iota(jnp.int32, (LAT, LAT), 1)
    column[...] = jnp.sum(jnp.where(diagonal, read_vec[...], 0.0), axis=1, keepdims=True)

    near, far = 1 - flip_ref[0, 0], 1 - flip_ref[0, 1]
    slot = second_ref[...] - OWN
    group = slot >> 8
    group = group ^ jnp.where(group < 2, near, far)
    ids_ref[0] = first_ref[...]
    ids_ref[1] = jnp.where(slot < 0, second_ref[...], OWN + group * GHOST + (slot & (GHOST - 1)))
    mask_ref[...] = valid_ref[...].astype(F32)
    span = 512
    at = lax.broadcasted_iota(jnp.int32, (WIN, span), 0).astype(F32).astype(BF16)

    def body(c, carry):
        blocks = [pl.ds(c * (span // 128) + i, 1) for i in range(span // 128)]
        first = jnp.concatenate([ids_ref[0, b, :] for b in blocks], axis=1)
        second = jnp.concatenate([ids_ref[1, b, :] for b in blocks], axis=1)
        out = pl.ds(pl.multiple_of(c * span, span), span)
        for w in range(ROWS // WIN):
            tile = window_hot(second, w, -1.0, at)
            if w < OWN // WIN:
                tile = tile + window_hot(first, w, 1.0, at)
            oh_ref[w * WIN : (w + 1) * WIN, out] = tile
        return carry

    lax.fori_loop(0, live_ref[0, 0] * (CHUNK // span), body, 0)


def own_gather_kernel(live_ref, own_ref, oh_ref, gap_out):
    table = stack2(own_ref[...])

    def body(c, carry):
        at = lanes(c)
        gap_out[:, at] = fold2(dot(table, oh_ref[:OWN, at]))
        return carry

    lax.fori_loop(0, live_ref[0, 0], body, 0)


def own_scatter_kernel(live_ref, parts_ref, oh_ref, own_out, acc_ref):
    acc_ref[...] = jnp.zeros_like(acc_ref)

    def body(c, carry):
        at = lanes(c)
        acc_ref[...] += dot_nt(oh_ref[:OWN, at], parts_ref[:, at])
        return carry

    lax.fori_loop(0, live_ref[0, 0], body, 0)
    own_out[...] = join_parts(acc_ref[...], own_out.shape[0])


def embed_kernel(
    live_ref, own_ref, c0, c1, c2, c3, ids_ref, mask_ref, oh_ref, w_embed, w_evl,
    geo_out, slope_out, lat_out, evh_out, parts_out, g0, g1, g2, g3, acc_ref,
):
    tables = [(own_ref, w * 128) for w in range(OWN // 128)]
    tables += [(c, w * 128) for c in (c0, c1, c2, c3) for w in range(GHOST // 128)]

    def pick(ids, count):
        block, place = ids >> 7, ids & 127
        found = [jnp.zeros(ids.shape, F32)] * 4
        for w, (ref, at) in enumerate(tables[:count]):
            here = block == w
            for k in range(4):
                row = jnp.broadcast_to(ref[k : k + 1, at : at + 128], ids.shape)
                value = jnp.take_along_axis(row, place, axis=1, mode="promise_in_bounds")
                found[k] = jnp.where(here, value, found[k])
        return found

    one = pick(ids_ref[0], OWN // 128)
    two = pick(ids_ref[1], ROWS // 128)
    mask = mask_ref[...]
    diff = [two[k] - one[k] for k in range(3)]
    sq = diff[0] * diff[0] + diff[1] * diff[1] + diff[2] * diff[2] + SOFTENING
    dist = jnp.sqrt(sq)
    inv = 1.0 / dist
    shrink = 1.0 - sq * (1.0 / CUTOFF**2)
    env = shrink * shrink
    columns = [d * inv for d in diff] + [env * mask, dist, mask, env * inv, one[3] + 8.0 * two[3]]
    for b in range(BRICK_BLOCKS):
        geo_out[:, b * 128 : (b + 1) * 128] = jnp.concatenate([column[b : b + 1] for column in columns], axis=0)
    acc_ref[...] = jnp.zeros_like(acc_ref)

    def body(c, carry):
        at = lanes(c)
        geo = geo_out[:, at]
        sines, _, _ = radial(geo[4:5])
        basis = sines * geo[6:7]
        bh = basis.astype(BF16).astype(F32)
        bl = basis - bh
        row = lax.broadcasted_iota(jnp.int32, (8, CHUNK), 0).astype(F32)
        code = geo[7:8]
        other = jnp.floor(code * 0.125)
        sf = jnp.where(row == code - 8.0 * other, 1.0, 0.0)
        ss = jnp.where(row == other, 1.0, 0.0)
        pre = dot(
            w_embed[...],
            jnp.concatenate([bh, bl, bh, sf, ss, sf, ss, jnp.zeros_like(bh)], axis=0).astype(BF16),
        )
        lat, slope = silu_and_slope(pre)
        slope_out[:, at] = slope
        lat_out[:, at] = lat
        evh = dense(w_evl[0], lat)
        evh_out[:, at] = evh
        scatter_ghosts(acc_ref, parts_out, spread2(weigh(geo, evh[:CH] * geo[3:4])), oh_ref, at)
        return carry

    lax.fori_loop(0, live_ref[0, 0], body, 0)
    emit(acc_ref, (g0, g1, g2, g3))


def combine_kernel(own_ref, r0, r1, r2, r3, ohs_ref, own_out, g0, g1, g2, g3):
    arrived = jnp.concatenate([r[...] for r in (r0, r1, r2, r3)], axis=1)
    owned = own_ref[...] + fold2(dot_nt(stack2(arrived), ohs_ref[...]))
    own_out[...] = owned
    ghosts = fold2(dot(stack2(owned), ohs_ref[...]))
    for m, out in enumerate((g0, g1, g2, g3)):
        out[...] = ghosts[:, m * GHOST : (m + 1) * GHOST]


def middle_kernel(
    live_ref, own_gap_ref, t0, t1, t2, t3, oh_ref, geo_ref, lat_ref, evh_ref, w_evl, w_tens, w_mix,
    gap_out, hid_out, lat_out, evh_out, parts_out, g0, g1, g2, g3, table_ref, acc_ref,
):
    fill_table(table_ref, (t0, t1, t2, t3))
    acc_ref[...] = jnp.zeros_like(acc_ref)

    def body(c, carry):
        at = lanes(c)
        gap = gather_ghosts(own_gap_ref, table_ref, oh_ref, at)
        gap_out[:, at] = gap
        geo = geo_ref[:, at]
        scalars = (ENV_SCALE * evh_ref[CH : 2 * CH, at]) * project(geo, gap)
        hid = evh_ref[2 * CH :, at] + dense(w_tens[0], scalars)
        hid_out[:, at] = hid
        lat = lat_ref[:, at] + dense(w_mix[0], hid * sigmoid(hid))
        lat_out[:, at] = lat
        evh = dense(w_evl[1], lat)
        evh_out[:, at] = evh
        vec = weigh(geo, evh[:CH] * geo[3:4])
        scatter_ghosts(acc_ref, parts_out, spread2(vec), oh_ref, at)
        return carry

    lax.fori_loop(0, live_ref[0, 0], body, 0)
    emit(acc_ref, (g0, g1, g2, g3))


def update_back(geo, gap, values, hid_slope, dlat, w_mix_t, w_lt_t, w_val_t):
    dhid = dense(w_mix_t, dlat) * hid_slope
    both = dense(w_lt_t, dhid)
    dscal = both[LAT:] * ENV_SCALE
    dval = project(geo, gap) * dscal
    dq = values * dscal
    return dlat + both[:LAT] + dense(w_val_t, dval), dq


def turn_kernel(
    live_ref, own_gap_ref, t0, t1, t2, t3, oh_ref, geo_ref, lat_ref, evh_ref, read_vec, w_tens, w_mix, w_read,
    w_read_t, w_mix_t, w_lt_t, w_val_t,
    energy_out, dlat_out, dgeo_out, parts_out, g0, g1, g2, g3, table_ref, acc_ref,
):
    fill_table(table_ref, (t0, t1, t2, t3))
    acc_ref[...] = jnp.zeros_like(acc_ref)
    rv = read_vec[...]

    def body(c, energy):
        at = lanes(c)
        gap = gather_ghosts(own_gap_ref, table_ref, oh_ref, at)
        geo = geo_ref[:, at]
        weight = geo[3:4]
        values = evh_ref[CH : 2 * CH, at]
        scalars = (ENV_SCALE * values) * project(geo, gap)
        hid = evh_ref[2 * CH :, at] + dense(w_tens[1], scalars)
        act, hid_slope = silu_and_slope(hid)
        lat = lat_ref[:, at] + dense(w_mix[1], act)
        out, out_slope = silu_and_slope(dense(w_read[...], lat))
        pair_energy = jnp.sum(rv * out, axis=0, keepdims=True) + PAIR_SHIFT
        dlat = dense(w_read_t[...], out_slope * (rv * weight))
        dlat, dq = update_back(geo, gap, values, hid_slope, dlat, w_mix_t[1], w_lt_t[1], w_val_t[1])
        dlat_out[:, at] = dlat
        dgeo_out[:, at] = put_rows(dir_grad(dq, gap) + [pair_energy], CHUNK)
        scatter_ghosts(acc_ref, parts_out, spread2(weigh(geo, dq)), oh_ref, at)
        return energy + pair_energy * weight

    energy = lax.fori_loop(0, live_ref[0, 0], body, jnp.zeros((1, CHUNK), F32))
    energy_out[...] = jnp.broadcast_to(jnp.sum(energy, axis=1, keepdims=True), energy_out.shape)
    emit(acc_ref, (g0, g1, g2, g3))


def environment_back(geo, dvec, env_values, dlat, dgeo, w_env_t):
    weight = geo[3:4]
    dscaled = project(geo, dvec)
    rows = dir_grad(env_values * weight, dvec)
    rows.append(jnp.sum(env_values * dscaled, axis=0, keepdims=True))
    return dlat + dense(w_env_t, dscaled * weight), dgeo + put_rows(rows, CHUNK)


def back_kernel(
    live_ref, own_gap_ref, t0, t1, t2, t3, oh_ref, geo_ref, evh1_ref, dlat_ref, dgeo_ref, gap_ref, hid_ref,
    evh0_ref, w_mix_t, w_lt_t, w_val_t, w_env_t,
    dlat_out, dgeo_out, parts_out, g0, g1, g2, g3, table_ref, acc_ref,
):
    fill_table(table_ref, (t0, t1, t2, t3))
    acc_ref[...] = jnp.zeros_like(acc_ref)

    def body(c, carry):
        at = lanes(c)
        dvec = gather_ghosts(own_gap_ref, table_ref, oh_ref, at)
        geo = geo_ref[:, at]
        dlat, dgeo = environment_back(geo, dvec, evh1_ref[:CH, at], dlat_ref[:, at], dgeo_ref[:, at], w_env_t[1])
        gap = gap_ref[:, at]
        _, hid_slope = silu_and_slope(hid_ref[:, at])
        dlat, dq = update_back(geo, gap, evh0_ref[CH : 2 * CH, at], hid_slope, dlat, w_mix_t[0], w_lt_t[0], w_val_t[0])
        dlat_out[:, at] = dlat
        dgeo_out[:, at] = dgeo + put_rows(dir_grad(dq, gap), CHUNK)
        scatter_ghosts(acc_ref, parts_out, spread2(weigh(geo, dq)), oh_ref, at)
        return carry

    lax.fori_loop(0, live_ref[0, 0], body, 0)
    emit(acc_ref, (g0, g1, g2, g3))


def force_kernel(
    live_ref, own_gap_ref, t0, t1, t2, t3, oh_ref, geo_ref, evh0_ref, dlat_ref, dgeo_ref, slope_ref,
    w_env_t, w_rad_t,
    parts_out, g0, g1, g2, g3, table_ref, acc_ref,
):
    fill_table(table_ref, (t0, t1, t2, t3))
    acc_ref[...] = jnp.zeros_like(acc_ref)

    def body(c, carry):
        at = lanes(c)
        dvec = gather_ghosts(own_gap_ref, table_ref, oh_ref, at)
        geo = geo_ref[:, at]
        dlat, dgeo = environment_back(geo, dvec, evh0_ref[:CH, at], dlat_ref[:, at], dgeo_ref[:, at], w_env_t[0])
        dbasis = dense(w_rad_t[...], dlat * slope_ref[:, at])
        dist, mask = geo[4:5], geo[5:6]
        inv = 1.0 / dist
        shrink = 1.0 - dist * dist * (1.0 / CUTOFF**2)
        env = shrink * shrink
        sines, cosines, freq = radial(dist)
        along = jnp.sum(dbasis * sines, axis=0, keepdims=True) * inv
        ddist = (jnp.sum(dbasis * (freq * cosines), axis=0, keepdims=True) - along) * (inv * env)
        denv = along + mask * dgeo[3:4]
        ddist = ddist - denv * shrink * dist * (4.0 / CUTOFF**2)
        row = lax.broadcasted_iota(jnp.int32, (8, CHUNK), 0)
        unit = jnp.where(row < 3, geo, 0.0)
        dunit = jnp.where(row < 3, dgeo, 0.0)
        radial_part = ddist - jnp.sum(unit * dunit, axis=0, keepdims=True) * inv
        ddiff = dunit * inv + unit * radial_part
        hi = ddiff.astype(BF16).astype(F32)
        both = jnp.concatenate([hi, ddiff - hi], axis=0).astype(BF16)
        parts = jnp.concatenate([both, jnp.zeros((WIDE - 16, CHUNK), BF16)], axis=0)
        scatter_ghosts(acc_ref, parts_out, parts, oh_ref, at)
        return carry

    lax.fori_loop(0, live_ref[0, 0], body, 0)
    emit(acc_ref, (g0, g1, g2, g3))


def final_kernel(own_ref, r0, r1, r2, r3, ohs_ref, out_ref):
    arrived = jnp.concatenate([r[...] for r in (r0, r1, r2, r3)], axis=1)
    hi, mid, lo = split3(arrived)
    parts = jnp.concatenate([hi, mid, lo, jnp.zeros_like(hi)], axis=0).astype(BF16)
    got = dot_nt(parts, ohs_ref[...])
    out_ref[...] = (own_ref[...] + got[0:8] + got[8:16] + got[16:24])[0:3]


def call(kernel, outs, *args, scratch=(), smem=0, fetched=0):
    vmem = pl.BlockSpec(memory_space=pltpu.VMEM)
    scalar = pl.BlockSpec(memory_space=pltpu.SMEM)
    anywhere = pl.BlockSpec(memory_space=pltpu.HBM)
    held = len(args) - fetched
    args = args[:held] + tuple(pltpu.with_memory_space_constraint(a, pltpu.HBM) for a in args[held:])
    buffers = [pltpu.VMEM(a.shape, a.dtype) for a in args[len(args) - fetched :]]
    if fetched:
        buffers.append(pltpu.SemaphoreType.DMA((fetched,)))
    return pl.pallas_call(
        kernel,
        out_shape=[jax.ShapeDtypeStruct(s, d) for s, d in outs],
        in_specs=[scalar] * smem + [vmem] * (len(args) - smem - fetched) + [anywhere] * fetched,
        out_specs=[scalar if s == (1, 1) else vmem for s, _ in outs],
        scratch_shapes=buffers + [pltpu.VMEM(s, d) for s, d in scratch],
        compiler_params=pltpu.CompilerParams(vmem_limit_bytes=VMEM_LIMIT),
    )(*args)


def matching(m, count):
    pairs = []
    for i in range(count):
        j = (i ^ 1, ((i + 1) ^ 1) - 1, i ^ 2, ((i + 2) ^ 2) - 2)[m]
        if 0 <= j < count:
            pairs.append((i, j))
    return pairs


def exchange(blocks):
    count = lax.axis_size("brick")
    got = [None] * 4
    for m in (2, 3, 1, 0):
        got[m] = lax.ppermute(blocks[m], "brick", matching(m, count))
    return got


def exchange_and_add(blocks, energy, step):
    blocks, energy = lax.optimization_barrier((blocks, energy))
    energy = add_across(energy, step)
    return exchange(blocks), energy


def add_across(value, step):
    count = lax.axis_size("brick")
    if step >= count:
        return value
    return value + lax.ppermute(value, "brick", [(i, i ^ step) for i in range(count)])


def per_device(
    positions, species, pair_first, pair_second, pair_valid, send_list, w_radial, w_first, w_second, w_value, w_env,
    w_latent, w_tensor, w_mix, w_read, read_vec,
):
    brick = lax.axis_index("brick")
    flips = jnp.stack([brick & 1, (brick >> 1) & 1]).reshape(1, 2)
    spec = species[None, :]

    message = ((8, GHOST), F32)
    *messages, ohs, live, atoms = call(
        send_kernel,
        [message] * 4 + [((OWN, 4 * GHOST), BF16), ((1, 1), jnp.int32), ((8, OWN), F32)],
        flips, positions, spec, send_list, pair_valid, smem=1, fetched=4,
    )
    coords = exchange(messages)
    shapes = (
        (LAT, 64), (2, 2 * CH + LAT, 3 * LAT), (2, LAT, 3 * CH), (2, LAT, 3 * LAT), (LAT, 3 * LAT), (LAT, 3 * LAT),
        (2, LAT, 3 * LAT), (2, LAT + CH, 3 * LAT), (2, LAT, 3 * CH), (2, LAT, 3 * CH), (NB, 3 * LAT),
    )
    oh, ids, mask, embed, evl, tens, mix, read, read_t, mix_t, lt_t, val_t, env_t, rad_t, column = call(
        prepare_kernel,
        [((ROWS, PAIRS), BF16), ((2, BRICK_BLOCKS, 128), ID), ((BRICK_BLOCKS, 128), F32)]
        + [(s, BF16) for s in shapes]
        + [((LAT, 1), F32)],
        flips, live, pair_first, pair_second, pair_valid, w_radial.T, w_first.T, w_second.T, w_value, w_env, w_latent,
        jnp.swapaxes(w_tensor, 1, 2), w_mix, w_read, read_vec[None, :],
        smem=2, fetched=13,
    )

    def rows(n):
        return ((n, PAIRS), F32)

    owned = ((VEC, OWN), F32)
    ghosted = [((VEC, GHOST), F32)] * 4
    partials = [((2 * WIDE, PAIRS), BF16)] + ghosted
    table = ((2 * VEC, 4 * GHOST), BF16)
    acc = ((4 * GHOST, 2 * WIDE), F32)

    def own_part(parts, out):
        return call(own_scatter_kernel, [out], live, parts, oh, scratch=[((OWN, parts.shape[0]), F32)], smem=1)[0]

    def gathered(own, listed):
        (gap,) = call(own_gather_kernel, [rows(VEC)], live, own, oh, smem=1)
        return [gap] + listed

    def combine(own, arrived):
        own, *listed = call(combine_kernel, [owned] + ghosted, own, *arrived, ohs)
        return own, listed

    def complete(parts, ghosts):
        arrived = exchange(ghosts)
        own, listed = combine(own_part(parts, owned), arrived)
        return gathered(own, exchange(listed))

    def complete_and_add(parts, ghosts, energy, steps):
        arrived, energy = exchange_and_add(ghosts, energy, steps[0])
        own, listed = combine(own_part(parts, owned), arrived)
        listed, energy = exchange_and_add(listed, energy, steps[1])
        return gathered(own, listed), energy

    geo, slope, lat0, evh0, parts, *ghosts = call(
        embed_kernel,
        [rows(8), rows(LAT), rows(LAT), rows(2 * CH + LAT)] + partials,
        live, atoms, *coords, ids, mask, oh, embed, evl,
        scratch=[acc],
        smem=1,
    )
    given = complete(parts, ghosts)
    gap0, hid0, lat1, evh1, parts, *ghosts = call(
        middle_kernel,
        [rows(VEC), rows(LAT), rows(LAT), rows(2 * CH + LAT)] + partials,
        live, *given, oh, geo, lat0, evh0, evl, tens, mix,
        scratch=[table, acc], smem=1,
    )
    given = complete(parts, ghosts)
    energy, dlat, dgeo, parts, *ghosts = call(
        turn_kernel,
        [((8, 128), F32), rows(LAT), rows(8)] + partials,
        live, *given, oh, geo, lat1, evh1, column, tens, mix, read, read_t, mix_t, lt_t, val_t,
        scratch=[table, acc], smem=1,
    )
    energy = add_across(energy, 1)
    given, energy = complete_and_add(parts, ghosts, energy, (2, 4))
    dlat, dgeo, parts, *ghosts = call(
        back_kernel,
        [rows(LAT), rows(8)] + partials,
        live, *given, oh, geo, evh1, dlat, dgeo, gap0, hid0, evh0, mix_t, lt_t, val_t, env_t,
        scratch=[table, acc], smem=1,
    )
    given, energy = complete_and_add(parts, ghosts, energy, (8, 16))
    parts, *ghosts = call(
        force_kernel,
        [((WIDE, PAIRS), BF16)] + [((8, GHOST), F32)] * 4,
        live, *given, oh, geo, evh0, dlat, dgeo, slope, env_t, rad_t,
        scratch=[table, ((4 * GHOST, WIDE), F32)], smem=1,
    )
    arrived, energy = exchange_and_add(ghosts, energy, 32)
    own = own_part(parts, ((8, OWN), F32))
    (forces,) = call(final_kernel, [((3, OWN), F32)], own, *arrived, ohs)
    total = add_across(energy, 64)
    return (forces, total[0, 0] / (lax.axis_size("brick") * PAIRS))


def solution(mesh):
    line = P("brick", None)
    return jax.shard_map(
        per_device,
        mesh=mesh,
        in_specs=(P(None, "brick"), P("brick"), line, line, line, line) + (P(),) * 10,
        out_specs=(P(None, "brick"), P()),
        check_vma=False,
    )
```

```python
import functools
import math

import jax
import jax.numpy as jnp
import numpy as np
from jax import lax
from jax.experimental import pallas as pl
from jax.experimental.pallas import tpu as pltpu
from jax.sharding import PartitionSpec as P

F32 = jnp.float32
BF16 = jnp.bfloat16
ID = jnp.int32

CUTOFF = 6.0
SOFTENING = 0.25
ENV_SCALE = 0.25
PAIR_SHIFT = 1.0

LAT = 64
CH = 32
NB = 8
VEC = 3 * CH
OWN = 512
GHOST = 256
ROWS = OWN + 4 * GHOST
WIN = 256
BRICK_BLOCKS = 48
PAIRS = BRICK_BLOCKS * 128
CHUNK = 3072
CHUNK_BLOCKS = CHUNK // 128
WIDE = 128

VMEM_LIMIT = 7 * 1024 * 1024


def fit_trig():
    r = np.cos(np.linspace(0.0, np.pi, 4001)) * 0.5
    x = r * r
    base = np.polynomial.chebyshev.Chebyshev
    safe = np.where(r == 0.0, 1.0, r)
    sine = np.where(r == 0.0, 2 * np.pi, np.sin(2 * np.pi * safe) / safe)
    s = base.fit(x, sine, 8, domain=[0.0, 0.25]).convert(kind=np.polynomial.Polynomial)
    c = base.fit(x, np.cos(2 * np.pi * r), 8, domain=[0.0, 0.25]).convert(kind=np.polynomial.Polynomial)
    return [float(v) for v in s.coef], [float(v) for v in c.coef]


SIN_COEF, COS_COEF = fit_trig()


def horner(coef, x):
    out = jnp.full_like(x, coef[-1])
    for c in coef[-2::-1]:
        out = out * x + c
    return out


def dot(a, b):
    return lax.dot_general(a, b, (((1,), (0,)), ((), ())), preferred_element_type=F32)


def dot_nt(a, b):
    return lax.dot_general(a, b, (((1,), (1,)), ((), ())), preferred_element_type=F32)


def split2(x):
    hi = x.astype(BF16)
    lo = (x - hi.astype(F32)).astype(BF16)
    return hi, lo


def split3(x):
    hi = x.astype(BF16).astype(F32)
    rest = x - hi
    mid = rest.astype(BF16).astype(F32)
    return hi, mid, (rest - mid)


def stack2(x):
    hi, lo = split2(x)
    return jnp.concatenate([hi, lo], axis=0)


def spread2(x):
    hi, lo = split2(x)
    pad = jnp.zeros((WIDE - x.shape[0], x.shape[1]), BF16)
    return jnp.concatenate([hi, pad, lo, pad], axis=0)


def weight3(w):
    hi, lo = split2(w)
    return jnp.concatenate([hi.astype(F32), hi.astype(F32), lo.astype(F32)], axis=1).astype(BF16)


def dense(w3, x):
    hi, lo = split2(x)
    return dot(w3, jnp.concatenate([hi, lo, hi], axis=0))


def sigmoid(x):
    return 0.5 * jnp.tanh(0.5 * x) + 0.5


def silu_and_slope(x):
    s = sigmoid(x)
    y = x * s
    return y, s + y * (1.0 - s)


def hot(ids, rows):
    at = lax.broadcasted_iota(jnp.int32, (rows, ids.shape[1]), 0)
    return jnp.where(at == ids, 1.0, 0.0).astype(BF16)


def window_hot(ids, window, value, at):
    local = jnp.clip(ids - window * WIN, -1, WIN).astype(F32).astype(BF16)
    return jnp.where(at == local, jnp.full((), value, BF16), jnp.zeros((), BF16))


def fold2(x):
    half = x.shape[0] // 2
    return x[:half] + x[half:]


def radial(dist):
    k = (lax.broadcasted_iota(jnp.int32, (NB, dist.shape[1]), 0) + 1).astype(F32)
    turns = k * (dist * (1.0 / (2.0 * CUTOFF)))
    r = turns - jnp.round(turns)
    x = r * r
    return r * horner(SIN_COEF, x), horner(COS_COEF, x), k * (math.pi / CUTOFF)


def lanes(c):
    return pl.ds(pl.multiple_of(c * CHUNK, CHUNK), CHUNK)


def weigh(geo, values):
    return jnp.concatenate([geo[m : m + 1] * values for m in range(3)], axis=0)


def project(geo, vectors):
    return (
        geo[0:1] * vectors[:CH]
        + geo[1:2] * vectors[CH : 2 * CH]
        + geo[2:3] * vectors[2 * CH :]
    )


def put_rows(rows, n):
    at = lax.broadcasted_iota(jnp.int32, (8, n), 0)
    out = jnp.zeros((8, n), F32)
    for i, row in enumerate(rows):
        out = jnp.where(at == i, row, out)
    return out


def dir_grad(dq, vectors):
    return [jnp.sum(dq * vectors[m * CH : (m + 1) * CH], axis=0, keepdims=True) for m in range(3)]


def fill_table(table_ref, ghost_refs):
    for m, ghost in enumerate(ghost_refs):
        hi, lo = split2(ghost[...])
        at = m * GHOST
        table_ref[:VEC, at : at + GHOST] = hi
        table_ref[VEC:, at : at + GHOST] = lo


def gather_ghosts(own_gap_ref, table_ref, oh_ref, at):
    return own_gap_ref[:, at] + fold2(dot(table_ref[...], oh_ref[OWN:, at]))


def scatter_ghosts(acc_ref, parts_out, parts, oh_ref, at):
    parts_out[:, at] = parts
    acc_ref[...] += dot_nt(oh_ref[OWN:, at], parts)


def emit(acc_ref, ghost_outs):
    for m, out in enumerate(ghost_outs):
        out[...] = join_parts(acc_ref[m * GHOST : (m + 1) * GHOST, :], out.shape[0])


def join_parts(acc, rows):
    if acc.shape[1] == WIDE:
        turned = acc.T
        return turned[:rows] + turned[rows : 2 * rows]
    return (acc[:, :WIDE] + acc[:, WIDE:]).T[:rows]


def fetch(sources, targets, sems):
    copies = [pltpu.make_async_copy(a, b, sems.at[i]) for i, (a, b) in enumerate(zip(sources, targets))]
    for copy in copies:
        copy.start()
    for copy in copies:
        copy.wait()


def send_kernel(
    flip_ref, pos_in, spec_in, send_in, valid_in, m0, m1, m2, m3, ohs_ref, live_ref, atoms_ref,
    pos_ref, spec_ref, send_ref, valid_ref, sems,
):
    fetch((pos_in, spec_in, send_in, valid_in), (pos_ref, spec_ref, send_ref, valid_ref), sems)
    live = jnp.sum(valid_ref[:, 0:1].astype(F32)).astype(jnp.int32)
    live_ref[0, 0] = (live + CHUNK_BLOCKS - 1) // CHUNK_BLOCKS
    columns = []
    for m in range(4):
        other = jnp.full((1, GHOST), flip_ref[0, m // 2], jnp.int32) == 1
        ids = jnp.where(other, send_ref[m ^ 1 : (m ^ 1) + 1, :], send_ref[m : m + 1, :])
        columns.append(hot(ids, OWN))
    oh = jnp.concatenate(columns, axis=1)
    ohs_ref[...] = oh
    atoms = put_rows([pos_ref[i : i + 1, :] for i in range(3)] + [spec_ref[...].astype(F32)], OWN)
    atoms_ref[...] = atoms
    hi, mid, lo = split3(atoms)
    got = dot(jnp.concatenate([hi, mid, lo, jnp.zeros_like(hi)], axis=0).astype(BF16), oh)
    got = got[0:8] + got[8:16] + got[16:24]
    for m, out in enumerate((m0, m1, m2, m3)):
        out[...] = got[:, m * GHOST : (m + 1) * GHOST]


def prepare_kernel(
    flip_ref, live_ref, *refs
):
    sources, refs = refs[:13], refs[13:]
    oh_ref, ids_ref, mask_ref, embed, evl, tens, mix, read, read_t, mix_t, lt_t, val_t, env_t, rad_t, column = refs[:15]
    fetch(sources, refs[15:28], refs[28])
    (
        first_ref, second_ref, valid_ref,
        w_radial_t, w_first_t, w_second_t, w_value, w_env, w_latent, w_tensor_t, w_mix, w_read, read_vec,
    ) = refs[15:28]

    def parts(w):
        hi, lo = split2(w)
        return hi.astype(F32), lo.astype(F32)

    rh, rl = parts(w_radial_t[...].T)
    fh, fl = parts(w_first_t[...].T)
    sh, sl = parts(w_second_t[...].T)
    embed[...] = jnp.concatenate([rh, rh, rl, fh, sh, fl, sl, jnp.zeros_like(rh)], axis=1).astype(BF16)
    for l in range(2):
        evl[l] = weight3(jnp.concatenate([w_env[l], w_value[l], w_latent[l]], axis=0))
        tens[l] = weight3(w_tensor_t[l].T)
        mix[l] = weight3(w_mix[l])
        mix_t[l] = weight3(w_mix[l].T)
        lt_t[l] = weight3(jnp.concatenate([w_latent[l].T, w_tensor_t[l]], axis=0))
        val_t[l] = weight3(w_value[l].T)
        env_t[l] = weight3(w_env[l].T)
    read[...] = weight3(w_read[...])
    read_t[...] = weight3(w_read[...].T)
    rad_t[...] = weight3(w_radial_t[...])
    diagonal = lax.broadcasted_iota(jnp.int32, (LAT, LAT), 0) == lax.broadcasted_iota(jnp.int32, (LAT, LAT), 1)
    column[...] = jnp.sum(jnp.where(diagonal, read_vec[...], 0.0), axis=1, keepdims=True)

    near, far = 1 - flip_ref[0, 0], 1 - flip_ref[0, 1]
    slot = second_ref[...] - OWN
    group = slot >> 8
    group = group ^ jnp.where(group < 2, near, far)
    ids_ref[0] = first_ref[...]
    ids_ref[1] = jnp.where(slot < 0, second_ref[...], OWN + group * GHOST + (slot & (GHOST - 1)))
    mask_ref[...] = valid_ref[...].astype(F32)
    span = 512
    at = lax.broadcasted_iota(jnp.int32, (WIN, span), 0).astype(F32).astype(BF16)

    def body(c, carry):
        blocks = [pl.ds(c * (span // 128) + i, 1) for i in range(span // 128)]
        first = jnp.concatenate([ids_ref[0, b, :] for b in blocks], axis=1)
        second = jnp.concatenate([ids_ref[1, b, :] for b in blocks], axis=1)
        out = pl.ds(pl.multiple_of(c * span, span), span)
        for w in range(ROWS // WIN):
            tile = window_hot(second, w, -1.0, at)
            if w < OWN // WIN:
                tile = tile + window_hot(first, w, 1.0, at)
            oh_ref[w * WIN : (w + 1) * WIN, out] = tile
        return carry

    lax.fori_loop(0, live_ref[0, 0] * (CHUNK // span), body, 0)


def own_gather_kernel(live_ref, own_ref, oh_ref, gap_out):
    table = stack2(own_ref[...])

    def body(c, carry):
        at = lanes(c)
        gap_out[:, at] = fold2(dot(table, oh_ref[:OWN, at]))
        return carry

    lax.fori_loop(0, live_ref[0, 0], body, 0)


def own_scatter_kernel(live_ref, parts_ref, oh_ref, own_out, acc_ref):
    acc_ref[...] = jnp.zeros_like(acc_ref)

    def body(c, carry):
        at = lanes(c)
        acc_ref[...] += dot_nt(oh_ref[:OWN, at], parts_ref[:, at])
        return carry

    lax.fori_loop(0, live_ref[0, 0], body, 0)
    own_out[...] = join_parts(acc_ref[...], own_out.shape[0])


def embed_kernel(
    live_ref, own_ref, c2, c3, c1, c0, ids_ref, mask_ref, oh_ref, w_embed, w_evl,
    geo_out, slope_out, lat_out, evh_out, parts_out, g0, g1, g2, g3, acc_ref,
):
    tables = [(own_ref, w * 128) for w in range(OWN // 128)]
    tables += [(c, w * 128) for c in (c0, c1, c2, c3) for w in range(GHOST // 128)]

    def pick(ids, count):
        block, place = ids >> 7, ids & 127
        found = [jnp.zeros(ids.shape, F32)] * 4
        for w, (ref, at) in enumerate(tables[:count]):
            here = block == w
            for k in range(4):
                row = jnp.broadcast_to(ref[k : k + 1, at : at + 128], ids.shape)
                value = jnp.take_along_axis(row, place, axis=1, mode="promise_in_bounds")
                found[k] = jnp.where(here, value, found[k])
        return found

    one = pick(ids_ref[0], OWN // 128)
    two = pick(ids_ref[1], ROWS // 128)
    mask = mask_ref[...]
    diff = [two[k] - one[k] for k in range(3)]
    sq = diff[0] * diff[0] + diff[1] * diff[1] + diff[2] * diff[2] + SOFTENING
    dist = jnp.sqrt(sq)
    inv = 1.0 / dist
    shrink = 1.0 - sq * (1.0 / CUTOFF**2)
    env = shrink * shrink
    columns = [d * inv for d in diff] + [env * mask, dist, mask, env * inv, one[3] + 8.0 * two[3]]
    for b in range(BRICK_BLOCKS):
        geo_out[:, b * 128 : (b + 1) * 128] = jnp.concatenate([column[b : b + 1] for column in columns], axis=0)
    acc_ref[...] = jnp.zeros_like(acc_ref)

    def body(c, carry):
        at = lanes(c)
        geo = geo_out[:, at]
        sines, _, _ = radial(geo[4:5])
        basis = sines * geo[6:7]
        bh = basis.astype(BF16).astype(F32)
        bl = basis - bh
        row = lax.broadcasted_iota(jnp.int32, (8, CHUNK), 0).astype(F32)
        code = geo[7:8]
        other = jnp.floor(code * 0.125)
        sf = jnp.where(row == code - 8.0 * other, 1.0, 0.0)
        ss = jnp.where(row == other, 1.0, 0.0)
        pre = dot(
            w_embed[...],
            jnp.concatenate([bh, bl, bh, sf, ss, sf, ss, jnp.zeros_like(bh)], axis=0).astype(BF16),
        )
        lat, slope = silu_and_slope(pre)
        slope_out[:, at] = slope
        lat_out[:, at] = lat
        evh = dense(w_evl[0], lat)
        evh_out[:, at] = evh
        scatter_ghosts(acc_ref, parts_out, spread2(weigh(geo, evh[:CH] * geo[3:4])), oh_ref, at)
        return carry

    lax.fori_loop(0, live_ref[0, 0], body, 0)
    emit(acc_ref, (g0, g1, g2, g3))


def combine_kernel(own_ref, r2, r3, r1, r0, ohs_ref, own_out, g0, g1, g2, g3):
    arrived = jnp.concatenate([r[...] for r in (r0, r1, r2, r3)], axis=1)
    owned = own_ref[...] + fold2(dot_nt(stack2(arrived), ohs_ref[...]))
    own_out[...] = owned
    ghosts = fold2(dot(stack2(owned), ohs_ref[...]))
    for m, out in enumerate((g0, g1, g2, g3)):
        out[...] = ghosts[:, m * GHOST : (m + 1) * GHOST]


def middle_kernel(
    live_ref, own_gap_ref, t2, t3, t1, t0, oh_ref, geo_ref, lat_ref, evh_ref, w_evl, w_tens, w_mix,
    gap_out, hid_out, lat_out, evh_out, parts_out, g0, g1, g2, g3, table_ref, acc_ref,
):
    fill_table(table_ref, (t0, t1, t2, t3))
    acc_ref[...] = jnp.zeros_like(acc_ref)

    def body(c, carry):
        at = lanes(c)
        gap = gather_ghosts(own_gap_ref, table_ref, oh_ref, at)
        gap_out[:, at] = gap
        geo = geo_ref[:, at]
        scalars = (ENV_SCALE * evh_ref[CH : 2 * CH, at]) * project(geo, gap)
        hid = evh_ref[2 * CH :, at] + dense(w_tens[0], scalars)
        hid_out[:, at] = hid
        lat = lat_ref[:, at] + dense(w_mix[0], hid * sigmoid(hid))
        lat_out[:, at] = lat
        evh = dense(w_evl[1], lat)
        evh_out[:, at] = evh
        vec = weigh(geo, evh[:CH] * geo[3:4])
        scatter_ghosts(acc_ref, parts_out, spread2(vec), oh_ref, at)
        return carry

    lax.fori_loop(0, live_ref[0, 0], body, 0)
    emit(acc_ref, (g0, g1, g2, g3))


def update_back(geo, gap, values, hid_slope, dlat, w_mix_t, w_lt_t, w_val_t):
    dhid = dense(w_mix_t, dlat) * hid_slope
    both = dense(w_lt_t, dhid)
    dscal = both[LAT:] * ENV_SCALE
    dval = project(geo, gap) * dscal
    dq = values * dscal
    return dlat + both[:LAT] + dense(w_val_t, dval), dq


def turn_kernel(
    live_ref, own_gap_ref, t2, t3, t1, t0, oh_ref, geo_ref, lat_ref, evh_ref, read_vec, w_tens, w_mix, w_read,
    w_read_t, w_mix_t, w_lt_t, w_val_t,
    energy_out, dlat_out, dgeo_out, parts_out, g0, g1, g2, g3, table_ref, acc_ref,
):
    fill_table(table_ref, (t0, t1, t2, t3))
    acc_ref[...] = jnp.zeros_like(acc_ref)
    rv = read_vec[...]

    def body(c, energy):
        at = lanes(c)
        gap = gather_ghosts(own_gap_ref, table_ref, oh_ref, at)
        geo = geo_ref[:, at]
        weight = geo[3:4]
        values = evh_ref[CH : 2 * CH, at]
        scalars = (ENV_SCALE * values) * project(geo, gap)
        hid = evh_ref[2 * CH :, at] + dense(w_tens[1], scalars)
        act, hid_slope = silu_and_slope(hid)
        lat = lat_ref[:, at] + dense(w_mix[1], act)
        out, out_slope = silu_and_slope(dense(w_read[...], lat))
        pair_energy = jnp.sum(rv * out, axis=0, keepdims=True) + PAIR_SHIFT
        dlat = dense(w_read_t[...], out_slope * (rv * weight))
        dlat, dq = update_back(geo, gap, values, hid_slope, dlat, w_mix_t[1], w_lt_t[1], w_val_t[1])
        dlat_out[:, at] = dlat
        dgeo_out[:, at] = put_rows(dir_grad(dq, gap) + [pair_energy], CHUNK)
        scatter_ghosts(acc_ref, parts_out, spread2(weigh(geo, dq)), oh_ref, at)
        return energy + pair_energy * weight

    energy = lax.fori_loop(0, live_ref[0, 0], body, jnp.zeros((1, CHUNK), F32))
    energy_out[...] = jnp.broadcast_to(jnp.sum(energy, axis=1, keepdims=True), energy_out.shape)
    emit(acc_ref, (g0, g1, g2, g3))


def environment_back(geo, dvec, env_values, dlat, dgeo, w_env_t):
    weight = geo[3:4]
    dscaled = project(geo, dvec)
    rows = dir_grad(env_values * weight, dvec)
    rows.append(jnp.sum(env_values * dscaled, axis=0, keepdims=True))
    return dlat + dense(w_env_t, dscaled * weight), dgeo + put_rows(rows, CHUNK)


def back_kernel(
    live_ref, own_gap_ref, t2, t3, t1, t0, oh_ref, geo_ref, evh1_ref, dlat_ref, dgeo_ref, gap_ref, hid_ref,
    evh0_ref, w_mix_t, w_lt_t, w_val_t, w_env_t,
    dlat_out, dgeo_out, parts_out, g0, g1, g2, g3, table_ref, acc_ref,
):
    fill_table(table_ref, (t0, t1, t2, t3))
    acc_ref[...] = jnp.zeros_like(acc_ref)

    def body(c, carry):
        at = lanes(c)
        dvec = gather_ghosts(own_gap_ref, table_ref, oh_ref, at)
        geo = geo_ref[:, at]
        dlat, dgeo = environment_back(geo, dvec, evh1_ref[:CH, at], dlat_ref[:, at], dgeo_ref[:, at], w_env_t[1])
        gap = gap_ref[:, at]
        _, hid_slope = silu_and_slope(hid_ref[:, at])
        dlat, dq = update_back(geo, gap, evh0_ref[CH : 2 * CH, at], hid_slope, dlat, w_mix_t[0], w_lt_t[0], w_val_t[0])
        dlat_out[:, at] = dlat
        dgeo_out[:, at] = dgeo + put_rows(dir_grad(dq, gap), CHUNK)
        scatter_ghosts(acc_ref, parts_out, spread2(weigh(geo, dq)), oh_ref, at)
        return carry

    lax.fori_loop(0, live_ref[0, 0], body, 0)
    emit(acc_ref, (g0, g1, g2, g3))


def force_kernel(
    live_ref, own_gap_ref, t2, t3, t1, t0, oh_ref, geo_ref, evh0_ref, dlat_ref, dgeo_ref, slope_ref,
    w_env_t, w_rad_t,
    parts_out, g0, g1, g2, g3, table_ref, acc_ref,
):
    fill_table(table_ref, (t0, t1, t2, t3))
    acc_ref[...] = jnp.zeros_like(acc_ref)

    def body(c, carry):
        at = lanes(c)
        dvec = gather_ghosts(own_gap_ref, table_ref, oh_ref, at)
        geo = geo_ref[:, at]
        dlat, dgeo = environment_back(geo, dvec, evh0_ref[:CH, at], dlat_ref[:, at], dgeo_ref[:, at], w_env_t[0])
        dbasis = dense(w_rad_t[...], dlat * slope_ref[:, at])
        dist, mask = geo[4:5], geo[5:6]
        inv = 1.0 / dist
        shrink = 1.0 - dist * dist * (1.0 / CUTOFF**2)
        env = shrink * shrink
        sines, cosines, freq = radial(dist)
        along = jnp.sum(dbasis * sines, axis=0, keepdims=True) * inv
        ddist = (jnp.sum(dbasis * (freq * cosines), axis=0, keepdims=True) - along) * (inv * env)
        denv = along + mask * dgeo[3:4]
        ddist = ddist - denv * shrink * dist * (4.0 / CUTOFF**2)
        row = lax.broadcasted_iota(jnp.int32, (8, CHUNK), 0)
        unit = jnp.where(row < 3, geo, 0.0)
        dunit = jnp.where(row < 3, dgeo, 0.0)
        radial_part = ddist - jnp.sum(unit * dunit, axis=0, keepdims=True) * inv
        ddiff = dunit * inv + unit * radial_part
        hi = ddiff.astype(BF16).astype(F32)
        both = jnp.concatenate([hi, ddiff - hi], axis=0).astype(BF16)
        parts = jnp.concatenate([both, jnp.zeros((WIDE - 16, CHUNK), BF16)], axis=0)
        scatter_ghosts(acc_ref, parts_out, parts, oh_ref, at)
        return carry

    lax.fori_loop(0, live_ref[0, 0], body, 0)
    emit(acc_ref, (g0, g1, g2, g3))


def final_kernel(pairs, own_ref, r2, r3, r1, r0, ohs_ref, energy_ref, other_ref, out_ref, energy_out):
    arrived = jnp.concatenate([r[...] for r in (r0, r1, r2, r3)], axis=1)
    hi, mid, lo = split3(arrived)
    parts = jnp.concatenate([hi, mid, lo, jnp.zeros_like(hi)], axis=0).astype(BF16)
    got = dot_nt(parts, ohs_ref[...])
    out_ref[...] = (own_ref[...] + got[0:8] + got[8:16] + got[16:24])[0:3]
    total = energy_ref[...] + other_ref[...]
    energy_out[...] = total[0:1, 0:1] / float(pairs)


def call(kernel, outs, *args, scratch=(), smem=0, fetched=0):
    vmem = pl.BlockSpec(memory_space=pltpu.VMEM)
    scalar = pl.BlockSpec(memory_space=pltpu.SMEM)
    anywhere = pl.BlockSpec(memory_space=pltpu.HBM)
    held = len(args) - fetched
    args = args[:held] + tuple(pltpu.with_memory_space_constraint(a, pltpu.HBM) for a in args[held:])
    buffers = [pltpu.VMEM(a.shape, a.dtype) for a in args[len(args) - fetched :]]
    if fetched:
        buffers.append(pltpu.SemaphoreType.DMA((fetched,)))
    return pl.pallas_call(
        kernel,
        out_shape=[jax.ShapeDtypeStruct(s, d) for s, d in outs],
        in_specs=[scalar] * smem + [vmem] * (len(args) - smem - fetched) + [anywhere] * fetched,
        out_specs=[scalar if s == (1, 1) and d == ID else vmem for s, d in outs],
        scratch_shapes=buffers + [pltpu.VMEM(s, d) for s, d in scratch],
        compiler_params=pltpu.CompilerParams(vmem_limit_bytes=VMEM_LIMIT),
    )(*args)


ORDER = (2, 3, 1, 0)


def matching(m, count):
    pairs = []
    for i in range(count):
        j = (i ^ 1, ((i + 1) ^ 1) - 1, i ^ 2, ((i + 2) ^ 2) - 2)[m]
        if 0 <= j < count:
            pairs.append((i, j))
    return pairs


def exchange(blocks):
    count = lax.axis_size("brick")
    return [lax.ppermute(blocks[m], "brick", matching(m, count)) for m in ORDER]


def exchange_and_add(blocks, energy, step):
    blocks, energy = lax.optimization_barrier((blocks, energy))
    energy = add_across(energy, step)
    return exchange(blocks), energy


def from_across(value, step):
    count = lax.axis_size("brick")
    if step >= count:
        return jnp.zeros_like(value)
    return lax.ppermute(value, "brick", [(i, i ^ step) for i in range(count)])


def add_across(value, step):
    return value + from_across(value, step)


def per_device(
    positions, species, pair_first, pair_second, pair_valid, send_list, w_radial, w_first, w_second, w_value, w_env,
    w_latent, w_tensor, w_mix, w_read, read_vec,
):
    brick = lax.axis_index("brick")
    flips = jnp.stack([brick & 1, (brick >> 1) & 1]).reshape(1, 2)
    spec = species[None, :]

    message = ((8, GHOST), F32)
    *messages, ohs, live, atoms = call(
        send_kernel,
        [message] * 4 + [((OWN, 4 * GHOST), BF16), ((1, 1), jnp.int32), ((8, OWN), F32)],
        flips, positions, spec, send_list, pair_valid, smem=1, fetched=4,
    )
    coords = exchange(messages)
    shapes = (
        (LAT, 64), (2, 2 * CH + LAT, 3 * LAT), (2, LAT, 3 * CH), (2, LAT, 3 * LAT), (LAT, 3 * LAT), (LAT, 3 * LAT),
        (2, LAT, 3 * LAT), (2, LAT + CH, 3 * LAT), (2, LAT, 3 * CH), (2, LAT, 3 * CH), (NB, 3 * LAT),
    )
    oh, ids, mask, embed, evl, tens, mix, read, read_t, mix_t, lt_t, val_t, env_t, rad_t, column = call(
        prepare_kernel,
        [((ROWS, PAIRS), BF16), ((2, BRICK_BLOCKS, 128), ID), ((BRICK_BLOCKS, 128), F32)]
        + [(s, BF16) for s in shapes]
        + [((LAT, 1), F32)],
        flips, live, pair_first, pair_second, pair_valid, w_radial.T, w_first.T, w_second.T, w_value, w_env, w_latent,
        jnp.swapaxes(w_tensor, 1, 2), w_mix, w_read, read_vec[None, :],
        smem=2, fetched=13,
    )

    def rows(n):
        return ((n, PAIRS), F32)

    owned = ((VEC, OWN), F32)
    ghosted = [((VEC, GHOST), F32)] * 4
    partials = [((2 * WIDE, PAIRS), BF16)] + ghosted
    table = ((2 * VEC, 4 * GHOST), BF16)
    acc = ((4 * GHOST, 2 * WIDE), F32)

    def own_part(parts, out):
        return call(own_scatter_kernel, [out], live, parts, oh, scratch=[((OWN, parts.shape[0]), F32)], smem=1)[0]

    def gathered(own, listed):
        (gap,) = call(own_gather_kernel, [rows(VEC)], live, own, oh, smem=1)
        return [gap] + listed

    def combine(own, arrived):
        own, *listed = call(combine_kernel, [owned] + ghosted, own, *arrived, ohs)
        return own, listed

    def complete(parts, ghosts):
        arrived = exchange(ghosts)
        own, listed = combine(own_part(parts, owned), arrived)
        return gathered(own, exchange(listed))

    def complete_and_add(parts, ghosts, energy, steps):
        arrived, energy = exchange_and_add(ghosts, energy, steps[0])
        own, listed = combine(own_part(parts, owned), arrived)
        listed, energy = exchange_and_add(listed, energy, steps[1])
        return gathered(own, listed), energy

    geo, slope, lat0, evh0, parts, *ghosts = call(
        embed_kernel,
        [rows(8), rows(LAT), rows(LAT), rows(2 * CH + LAT)] + partials,
        live, atoms, *coords, ids, mask, oh, embed, evl,
        scratch=[acc],
        smem=1,
    )
    given = complete(parts, ghosts)
    gap0, hid0, lat1, evh1, parts, *ghosts = call(
        middle_kernel,
        [rows(VEC), rows(LAT), rows(LAT), rows(2 * CH + LAT)] + partials,
        live, *given, oh, geo, lat0, evh0, evl, tens, mix,
        scratch=[table, acc], smem=1,
    )
    given = complete(parts, ghosts)
    energy, dlat, dgeo, parts, *ghosts = call(
        turn_kernel,
        [((8, 128), F32), rows(LAT), rows(8)] + partials,
        live, *given, oh, geo, lat1, evh1, column, tens, mix, read, read_t, mix_t, lt_t, val_t,
        scratch=[table, acc], smem=1,
    )
    energy = add_across(energy, 1)
    given, energy = complete_and_add(parts, ghosts, energy, (2, 4))
    dlat, dgeo, parts, *ghosts = call(
        back_kernel,
        [rows(LAT), rows(8)] + partials,
        live, *given, oh, geo, evh1, dlat, dgeo, gap0, hid0, evh0, mix_t, lt_t, val_t, env_t,
        scratch=[table, acc], smem=1,
    )
    given, energy = complete_and_add(parts, ghosts, energy, (8, 16))
    parts, *ghosts = call(
        force_kernel,
        [((WIDE, PAIRS), BF16)] + [((8, GHOST), F32)] * 4,
        live, *given, oh, geo, evh0, dlat, dgeo, slope, env_t, rad_t,
        scratch=[table, ((4 * GHOST, WIDE), F32)], smem=1,
    )
    arrived, energy = exchange_and_add(ghosts, energy, 32)
    own = own_part(parts, ((8, OWN), F32))
    forces, total = call(
        functools.partial(final_kernel, lax.axis_size("brick") * PAIRS),
        [((3, OWN), F32), ((1, 1), F32)],
        own, *arrived, ohs, energy, from_across(energy, 64),
    )
    return (forces, total.reshape(()))


def solution(mesh):
    line = P("brick", None)
    return jax.shard_map(
        per_device,
        mesh=mesh,
        in_specs=(P(None, "brick"), P("brick"), line, line, line, line) + (P(),) * 10,
        out_specs=(P(None, "brick"), P()),
        check_vma=False,
    )
```

```python
import functools
import math

import jax
import jax.numpy as jnp
import numpy as np
from jax import lax
from jax.experimental import pallas as pl
from jax.experimental.pallas import tpu as pltpu
from jax.sharding import PartitionSpec as P

F32 = jnp.float32
BF16 = jnp.bfloat16
ID = jnp.int32

CUTOFF = 6.0
SOFTENING = 0.25
ENV_SCALE = 0.25
PAIR_SHIFT = 1.0

LAT = 64
CH = 32
NB = 8
VEC = 3 * CH
USE = 2 * CH + LAT
OWN = 512
GHOST = 256
ROWS = OWN + 4 * GHOST
WIN = 256
BRICK_BLOCKS = 48
PAIRS = BRICK_BLOCKS * 128
CHUNK = 3072
CHUNK_BLOCKS = CHUNK // 128
WIDE = 128

VMEM_LIMIT = 7 * 1024 * 1024


def fit_trig():
    r = np.cos(np.linspace(0.0, np.pi, 4001)) * 0.5
    x = r * r
    base = np.polynomial.chebyshev.Chebyshev
    safe = np.where(r == 0.0, 1.0, r)
    sine = np.where(r == 0.0, 2 * np.pi, np.sin(2 * np.pi * safe) / safe)
    s = base.fit(x, sine, 8, domain=[0.0, 0.25]).convert(kind=np.polynomial.Polynomial)
    c = base.fit(x, np.cos(2 * np.pi * r), 8, domain=[0.0, 0.25]).convert(kind=np.polynomial.Polynomial)
    return [float(v) for v in s.coef], [float(v) for v in c.coef]


SIN_COEF, COS_COEF = fit_trig()


def horner(coef, x):
    out = jnp.full_like(x, coef[-1])
    for c in coef[-2::-1]:
        out = out * x + c
    return out


def dot(a, b):
    return lax.dot_general(a, b, (((1,), (0,)), ((), ())), preferred_element_type=F32)


def dot_nt(a, b):
    return lax.dot_general(a, b, (((1,), (1,)), ((), ())), preferred_element_type=F32)


def split2(x):
    hi = x.astype(BF16)
    lo = (x - hi.astype(F32)).astype(BF16)
    return hi, lo


def split3(x):
    hi = x.astype(BF16).astype(F32)
    rest = x - hi
    mid = rest.astype(BF16).astype(F32)
    return hi, mid, (rest - mid)


def stack2(x):
    hi, lo = split2(x)
    return jnp.concatenate([hi, lo], axis=0)


def spread2(x):
    hi, lo = split2(x)
    pad = jnp.zeros((WIDE - x.shape[0], x.shape[1]), BF16)
    return jnp.concatenate([hi, pad, lo, pad], axis=0)


def weight3(w):
    hi, lo = split2(w)
    return jnp.concatenate([hi.astype(F32), hi.astype(F32), lo.astype(F32)], axis=1).astype(BF16)


def dense(w3, x):
    hi, lo = split2(x)
    return dot(w3, jnp.concatenate([hi, lo, hi], axis=0))


def sigmoid(x):
    return 0.5 * jnp.tanh(0.5 * x) + 0.5


def silu_and_slope(x):
    s = sigmoid(x)
    y = x * s
    return y, s + y * (1.0 - s)


def hot(ids, rows):
    at = lax.broadcasted_iota(jnp.int32, (rows, ids.shape[1]), 0)
    return jnp.where(at == ids, 1.0, 0.0).astype(BF16)


def window_hot(ids, window, value, at):
    local = jnp.clip(ids - window * WIN, -1, WIN).astype(F32).astype(BF16)
    return jnp.where(at == local, jnp.full((), value, BF16), jnp.zeros((), BF16))


def fold2(x):
    half = x.shape[0] // 2
    return x[:half] + x[half:]


def radial(dist):
    k = (lax.broadcasted_iota(jnp.int32, (NB, dist.shape[1]), 0) + 1).astype(F32)
    turns = k * (dist * (1.0 / (2.0 * CUTOFF)))
    r = turns - jnp.round(turns)
    x = r * r
    return r * horner(SIN_COEF, x), horner(COS_COEF, x), k * (math.pi / CUTOFF)


def lanes(c):
    return pl.ds(pl.multiple_of(c * CHUNK, CHUNK), CHUNK)


def weigh(geo, values):
    return jnp.concatenate([geo[m : m + 1] * values for m in range(3)], axis=0)


def project(geo, vectors):
    return (
        geo[0:1] * vectors[:CH]
        + geo[1:2] * vectors[CH : 2 * CH]
        + geo[2:3] * vectors[2 * CH :]
    )


def put_rows(rows, n):
    at = lax.broadcasted_iota(jnp.int32, (8, n), 0)
    out = jnp.zeros((8, n), F32)
    for i, row in enumerate(rows):
        out = jnp.where(at == i, row, out)
    return out


def dir_grad(dq, vectors):
    return [jnp.sum(dq * vectors[m * CH : (m + 1) * CH], axis=0, keepdims=True) for m in range(3)]


def fill_table(table_ref, ghost_refs):
    for m, ghost in enumerate(ghost_refs):
        hi, lo = split2(ghost[...])
        at = m * GHOST
        table_ref[:VEC, at : at + GHOST] = hi
        table_ref[VEC:, at : at + GHOST] = lo


def gather_ghosts(own_gap_ref, table_ref, oh_ref, at):
    return own_gap_ref[:, at] + fold2(dot(table_ref[...], oh_ref[OWN:, at]))


def scatter_ghosts(acc_ref, parts_out, parts, oh_ref, at):
    parts_out[:, at] = parts
    acc_ref[...] += dot_nt(oh_ref[OWN:, at], parts)


def emit(acc_ref, ghost_outs):
    for m, out in enumerate(ghost_outs):
        out[...] = join_parts(acc_ref[m * GHOST : (m + 1) * GHOST, :], out.shape[0])


def join_parts(acc, rows):
    if acc.shape[1] == WIDE:
        turned = acc.T
        return turned[:rows] + turned[rows : 2 * rows]
    return (acc[:, :WIDE] + acc[:, WIDE:]).T[:rows]


def fetch(sources, targets, sems):
    copies = [pltpu.make_async_copy(a, b, sems.at[i]) for i, (a, b) in enumerate(zip(sources, targets))]
    for copy in copies:
        copy.start()
    for copy in copies:
        copy.wait()


def send_kernel(
    flip_ref, pos_in, spec_in, send_in, valid_in, m0, m1, m2, m3, ohs_ref, live_ref, atoms_ref,
    pos_ref, spec_ref, send_ref, valid_ref, sems,
):
    fetch((pos_in, spec_in, send_in, valid_in), (pos_ref, spec_ref, send_ref, valid_ref), sems)
    live = jnp.sum(valid_ref[:, 0:1].astype(F32)).astype(jnp.int32)
    live_ref[0, 0] = (live + CHUNK_BLOCKS - 1) // CHUNK_BLOCKS
    columns = []
    for m in range(4):
        other = jnp.full((1, GHOST), flip_ref[0, m // 2], jnp.int32) == 1
        ids = jnp.where(other, send_ref[m ^ 1 : (m ^ 1) + 1, :], send_ref[m : m + 1, :])
        columns.append(hot(ids, OWN))
    oh = jnp.concatenate(columns, axis=1)
    ohs_ref[...] = oh
    atoms = put_rows([pos_ref[i : i + 1, :] for i in range(3)] + [spec_ref[...].astype(F32)], OWN)
    atoms_ref[...] = atoms
    hi, mid, lo = split3(atoms)
    got = dot(jnp.concatenate([hi, mid, lo, jnp.zeros_like(hi)], axis=0).astype(BF16), oh)
    got = got[0:8] + got[8:16] + got[16:24]
    for m, out in enumerate((m0, m1, m2, m3)):
        out[...] = got[:, m * GHOST : (m + 1) * GHOST]


def prepare_kernel(
    flip_ref, *refs
):
    sources, refs = refs[:13], refs[13:]
    oh_ref, ids_ref, mask_ref, embed, enter, tens, step, leave, read_t, lt1_t, val1_t, env1_t, lt0_t, val0_t, env0_t, rad_t, column = refs[:17]
    fetch(sources, refs[17:30], refs[30])
    (
        first_ref, second_ref, valid_ref,
        w_radial_t, w_first_t, w_second_t, w_value, w_env, w_latent, w_tensor_t, w_mix, w_read, read_vec,
    ) = refs[17:30]

    def parts(w):
        hi, lo = split2(w)
        return hi.astype(F32), lo.astype(F32)

    rh, rl = parts(w_radial_t[...].T)
    fh, fl = parts(w_first_t[...].T)
    sh, sl = parts(w_second_t[...].T)
    embed[...] = jnp.concatenate([rh, rh, rl, fh, sh, fl, sl, jnp.zeros_like(rh)], axis=1).astype(BF16)
    use0, use1 = (jnp.concatenate([w_env[l], w_value[l], w_latent[l]], axis=0) for l in range(2))
    use_mix0 = dense(weight3(use1), w_mix[0])
    read3 = weight3(w_read[...])
    read_mix0, read_mix1 = dense(read3, w_mix[0]), dense(read3, w_mix[1])
    enter[...] = jnp.concatenate([weight3(use0), weight3(use1), read3], axis=0)
    for l in range(2):
        tens[l] = weight3(w_tensor_t[l].T)
    step[...] = weight3(jnp.concatenate([use_mix0, read_mix0], axis=0))
    leave[...] = weight3(read_mix1)
    read_t[...] = weight3(jnp.concatenate([w_read[...].T, read_mix1.T, read_mix0.T], axis=0))
    lt1_t[...] = weight3(jnp.concatenate([w_latent[1].T, w_tensor_t[1], use_mix0[2 * CH :].T], axis=0))
    val1_t[...] = weight3(jnp.concatenate([w_value[1].T, use_mix0[CH : 2 * CH].T], axis=0))
    env1_t[...] = weight3(jnp.concatenate([w_env[1].T, use_mix0[:CH].T], axis=0))
    lt0_t[...] = weight3(jnp.concatenate([w_latent[0].T, w_tensor_t[0]], axis=0))
    val0_t[...] = weight3(w_value[0].T)
    env0_t[...] = weight3(w_env[0].T)
    rad_t[...] = weight3(w_radial_t[...])
    diagonal = lax.broadcasted_iota(jnp.int32, (LAT, LAT), 0) == lax.broadcasted_iota(jnp.int32, (LAT, LAT), 1)
    column[...] = jnp.sum(jnp.where(diagonal, read_vec[...], 0.0), axis=1, keepdims=True)

    near, far = 1 - flip_ref[0, 0], 1 - flip_ref[0, 1]
    slot = second_ref[...] - OWN
    group = slot >> 8
    group = group ^ jnp.where(group < 2, near, far)
    ids_ref[0] = first_ref[...]
    ids_ref[1] = jnp.where(slot < 0, second_ref[...], OWN + group * GHOST + (slot & (GHOST - 1)))
    mask_ref[...] = valid_ref[...].astype(F32)
    span = 512
    at = lax.broadcasted_iota(jnp.int32, (WIN, span), 0).astype(F32).astype(BF16)

    def body(c, carry):
        blocks = [pl.ds(c * (span // 128) + i, 1) for i in range(span // 128)]
        first = jnp.concatenate([ids_ref[0, b, :] for b in blocks], axis=1)
        second = jnp.concatenate([ids_ref[1, b, :] for b in blocks], axis=1)
        out = pl.ds(pl.multiple_of(c * span, span), span)
        for w in range(ROWS // WIN):
            tile = window_hot(second, w, -1.0, at)
            if w < OWN // WIN:
                tile = tile + window_hot(first, w, 1.0, at)
            oh_ref[w * WIN : (w + 1) * WIN, out] = tile
        return carry

    lax.fori_loop(0, PAIRS // span, body, 0)


def own_gather_kernel(own_ref, oh_ref, gap_out):
    table = stack2(own_ref[...])
    for c in range(PAIRS // CHUNK):
        at = slice(c * CHUNK, (c + 1) * CHUNK)
        gap_out[:, at] = fold2(dot(table, oh_ref[:OWN, at]))


def own_scatter_kernel(parts_ref, oh_ref, own_out):
    own_out[...] = join_parts(dot_nt(oh_ref[:OWN, :], parts_ref[...]), own_out.shape[0])


def clear_rest(live_ref, parts_out):
    def body(c, carry):
        parts_out[:, lanes(c)] = jnp.zeros((parts_out.shape[0], CHUNK), BF16)
        return carry

    lax.fori_loop(live_ref[0, 0], PAIRS // CHUNK, body, 0)


def embed_kernel(
    live_ref, own_ref, c2, c3, c1, c0, ids_ref, mask_ref, oh_ref, w_embed, w_enter,
    geo_out, slope_out, use_out, next_out, parts_out, g0, g1, g2, g3, acc_ref,
):
    tables = [(own_ref, w * 128) for w in range(OWN // 128)]
    tables += [(c, w * 128) for c in (c0, c1, c2, c3) for w in range(GHOST // 128)]

    def pick(ids, count):
        block, place = ids >> 7, ids & 127
        found = [jnp.zeros(ids.shape, F32)] * 4
        for w, (ref, at) in enumerate(tables[:count]):
            here = block == w
            for k in range(4):
                row = jnp.broadcast_to(ref[k : k + 1, at : at + 128], ids.shape)
                value = jnp.take_along_axis(row, place, axis=1, mode="promise_in_bounds")
                found[k] = jnp.where(here, value, found[k])
        return found

    one = pick(ids_ref[0], OWN // 128)
    two = pick(ids_ref[1], ROWS // 128)
    mask = mask_ref[...]
    diff = [two[k] - one[k] for k in range(3)]
    sq = diff[0] * diff[0] + diff[1] * diff[1] + diff[2] * diff[2] + SOFTENING
    dist = jnp.sqrt(sq)
    inv = 1.0 / dist
    shrink = 1.0 - sq * (1.0 / CUTOFF**2)
    env = shrink * shrink
    columns = [d * inv for d in diff] + [env * mask, dist, mask, env * inv, one[3] + 8.0 * two[3]]
    for b in range(BRICK_BLOCKS):
        geo_out[:, b * 128 : (b + 1) * 128] = jnp.concatenate([column[b : b + 1] for column in columns], axis=0)
    acc_ref[...] = jnp.zeros_like(acc_ref)
    clear_rest(live_ref, parts_out)

    def body(c, carry):
        at = lanes(c)
        geo = geo_out[:, at]
        sines, _, _ = radial(geo[4:5])
        basis = sines * geo[6:7]
        bh = basis.astype(BF16).astype(F32)
        bl = basis - bh
        row = lax.broadcasted_iota(jnp.int32, (8, CHUNK), 0).astype(F32)
        code = geo[7:8]
        other = jnp.floor(code * 0.125)
        sf = jnp.where(row == code - 8.0 * other, 1.0, 0.0)
        ss = jnp.where(row == other, 1.0, 0.0)
        pre = dot(
            w_embed[...],
            jnp.concatenate([bh, bl, bh, sf, ss, sf, ss, jnp.zeros_like(bh)], axis=0).astype(BF16),
        )
        lat, slope = silu_and_slope(pre)
        slope_out[:, at] = slope
        enter = dense(w_enter[...], lat)
        use_out[:, at] = enter[: 2 * CH]
        next_out[:, at] = enter[2 * CH :]
        scatter_ghosts(acc_ref, parts_out, spread2(weigh(geo, enter[:CH] * geo[3:4])), oh_ref, at)
        return carry

    lax.fori_loop(0, live_ref[0, 0], body, 0)
    emit(acc_ref, (g0, g1, g2, g3))


def combine_kernel(own_ref, r2, r3, r1, r0, ohs_ref, own_out, g0, g1, g2, g3):
    arrived = jnp.concatenate([r[...] for r in (r0, r1, r2, r3)], axis=1)
    owned = own_ref[...] + fold2(dot_nt(stack2(arrived), ohs_ref[...]))
    own_out[...] = owned
    ghosts = fold2(dot(stack2(owned), ohs_ref[...]))
    for m, out in enumerate((g0, g1, g2, g3)):
        out[...] = ghosts[:, m * GHOST : (m + 1) * GHOST]


def middle_kernel(
    live_ref, own_gap_ref, t2, t3, t1, t0, oh_ref, geo_ref, use_ref, next_ref, w_tens, w_step,
    gap_out, next_out, parts_out, g0, g1, g2, g3, table_ref, acc_ref,
):
    fill_table(table_ref, (t0, t1, t2, t3))
    acc_ref[...] = jnp.zeros_like(acc_ref)
    clear_rest(live_ref, parts_out)

    def body(c, carry):
        at = lanes(c)
        gap = gather_ghosts(own_gap_ref, table_ref, oh_ref, at)
        gap_out[:, at] = gap
        geo = geo_ref[:, at]
        scalars = (ENV_SCALE * use_ref[CH : 2 * CH, at]) * project(geo, gap)
        hid = next_ref[:LAT, at] + dense(w_tens[0], scalars)
        later = next_ref[LAT:, at] + dense(w_step[...], hid * sigmoid(hid))
        next_out[:LAT, at] = hid
        next_out[LAT:, at] = later
        scatter_ghosts(acc_ref, parts_out, spread2(weigh(geo, later[:CH] * geo[3:4])), oh_ref, at)
        return carry

    lax.fori_loop(0, live_ref[0, 0], body, 0)
    emit(acc_ref, (g0, g1, g2, g3))


def update_back(geo, gap, values, dhid, w_lt_t, w_val_t):
    both = dense(w_lt_t, dhid)
    dscal = both[LAT : LAT + CH] * ENV_SCALE
    return both, dense(w_val_t, project(geo, gap) * dscal), values * dscal


def turn_kernel(
    live_ref, own_gap_ref, t2, t3, t1, t0, oh_ref, geo_ref, next_ref, read_vec, w_tens, w_leave, w_read_t, w_lt_t, w_val_t,
    energy_out, dlat_out, dgeo_out, parts_out, g0, g1, g2, g3, table_ref, acc_ref,
):
    fill_table(table_ref, (t0, t1, t2, t3))
    acc_ref[...] = jnp.zeros_like(acc_ref)
    clear_rest(live_ref, parts_out)
    rv = read_vec[...]

    def body(c, energy):
        at = lanes(c)
        gap = gather_ghosts(own_gap_ref, table_ref, oh_ref, at)
        geo = geo_ref[:, at]
        weight = geo[3:4]
        values = next_ref[LAT + CH : LAT + 2 * CH, at]
        scalars = (ENV_SCALE * values) * project(geo, gap)
        hid = next_ref[LAT + 2 * CH : LAT + USE, at] + dense(w_tens[1], scalars)
        act, hid_slope = silu_and_slope(hid)
        out, out_slope = silu_and_slope(next_ref[LAT + USE :, at] + dense(w_leave[...], act))
        pair_energy = jnp.sum(rv * out, axis=0, keepdims=True) + PAIR_SHIFT
        back = dense(w_read_t[...], out_slope * (rv * weight))
        both, more, dq = update_back(geo, gap, values, back[LAT : 2 * LAT] * hid_slope, w_lt_t[...], w_val_t[...])
        dlat_out[:LAT, at] = back[:LAT] + both[:LAT] + more[:LAT]
        dlat_out[LAT:, at] = back[2 * LAT :] + both[LAT + CH :] + more[LAT:]
        dgeo_out[:, at] = put_rows(dir_grad(dq, gap) + [pair_energy], CHUNK)
        scatter_ghosts(acc_ref, parts_out, spread2(weigh(geo, dq)), oh_ref, at)
        return energy + pair_energy * weight

    energy = lax.fori_loop(0, live_ref[0, 0], body, jnp.zeros((1, CHUNK), F32))
    energy_out[...] = jnp.broadcast_to(jnp.sum(energy, axis=1, keepdims=True), energy_out.shape)
    emit(acc_ref, (g0, g1, g2, g3))


def environment_back(geo, dvec, env_values, dlat, dgeo, w_env_t):
    weight = geo[3:4]
    dscaled = project(geo, dvec)
    rows = dir_grad(env_values * weight, dvec)
    rows.append(jnp.sum(env_values * dscaled, axis=0, keepdims=True))
    return dlat + dense(w_env_t, dscaled * weight), dgeo + put_rows(rows, CHUNK)


def back_kernel(
    live_ref, own_gap_ref, t2, t3, t1, t0, oh_ref, geo_ref, next_ref, dlat_ref, dgeo_ref, gap_ref, use_ref,
    w_lt_t, w_val_t, w_env_t,
    dlat_out, dgeo_out, parts_out, g0, g1, g2, g3, table_ref, acc_ref,
):
    fill_table(table_ref, (t0, t1, t2, t3))
    acc_ref[...] = jnp.zeros_like(acc_ref)
    clear_rest(live_ref, parts_out)

    def body(c, carry):
        at = lanes(c)
        dvec = gather_ghosts(own_gap_ref, table_ref, oh_ref, at)
        geo = geo_ref[:, at]
        dlat, dgeo = environment_back(geo, dvec, next_ref[LAT : LAT + CH, at], dlat_ref[:, at], dgeo_ref[:, at], w_env_t[...])
        gap = gap_ref[:, at]
        _, hid_slope = silu_and_slope(next_ref[:LAT, at])
        both, more, dq = update_back(geo, gap, use_ref[CH : 2 * CH, at], dlat[LAT:] * hid_slope, w_lt_t[...], w_val_t[...])
        dlat_out[:LAT, at] = dlat[:LAT] + both[:LAT] + more
        dgeo_out[:, at] = dgeo + put_rows(dir_grad(dq, gap), CHUNK)
        scatter_ghosts(acc_ref, parts_out, spread2(weigh(geo, dq)), oh_ref, at)
        return carry

    lax.fori_loop(0, live_ref[0, 0], body, 0)
    emit(acc_ref, (g0, g1, g2, g3))


def force_kernel(
    live_ref, own_gap_ref, t2, t3, t1, t0, oh_ref, geo_ref, use_ref, dlat_ref, dgeo_ref, slope_ref,
    w_env_t, w_rad_t,
    parts_out, g0, g1, g2, g3, table_ref, acc_ref,
):
    fill_table(table_ref, (t0, t1, t2, t3))
    acc_ref[...] = jnp.zeros_like(acc_ref)
    clear_rest(live_ref, parts_out)

    def body(c, carry):
        at = lanes(c)
        dvec = gather_ghosts(own_gap_ref, table_ref, oh_ref, at)
        geo = geo_ref[:, at]
        dlat, dgeo = environment_back(geo, dvec, use_ref[:CH, at], dlat_ref[:LAT, at], dgeo_ref[:, at], w_env_t[...])
        dbasis = dense(w_rad_t[...], dlat * slope_ref[:, at])
        dist, mask = geo[4:5], geo[5:6]
        inv = 1.0 / dist
        shrink = 1.0 - dist * dist * (1.0 / CUTOFF**2)
        env = shrink * shrink
        sines, cosines, freq = radial(dist)
        along = jnp.sum(dbasis * sines, axis=0, keepdims=True) * inv
        ddist = (jnp.sum(dbasis * (freq * cosines), axis=0, keepdims=True) - along) * (inv * env)
        denv = along + mask * dgeo[3:4]
        ddist = ddist - denv * shrink * dist * (4.0 / CUTOFF**2)
        row = lax.broadcasted_iota(jnp.int32, (8, CHUNK), 0)
        unit = jnp.where(row < 3, geo, 0.0)
        dunit = jnp.where(row < 3, dgeo, 0.0)
        radial_part = ddist - jnp.sum(unit * dunit, axis=0, keepdims=True) * inv
        ddiff = dunit * inv + unit * radial_part
        hi = ddiff.astype(BF16).astype(F32)
        both = jnp.concatenate([hi, ddiff - hi], axis=0).astype(BF16)
        parts = jnp.concatenate([both, jnp.zeros((WIDE - 16, CHUNK), BF16)], axis=0)
        scatter_ghosts(acc_ref, parts_out, parts, oh_ref, at)
        return carry

    lax.fori_loop(0, live_ref[0, 0], body, 0)
    emit(acc_ref, (g0, g1, g2, g3))


def final_kernel(pairs, own_ref, r2, r3, r1, r0, ohs_ref, energy_ref, other_ref, out_ref, energy_out):
    arrived = jnp.concatenate([r[...] for r in (r0, r1, r2, r3)], axis=1)
    hi, mid, lo = split3(arrived)
    parts = jnp.concatenate([hi, mid, lo, jnp.zeros_like(hi)], axis=0).astype(BF16)
    got = dot_nt(parts, ohs_ref[...])
    out_ref[...] = (own_ref[...] + got[0:8] + got[8:16] + got[16:24])[0:3]
    total = energy_ref[...] + other_ref[...]
    energy_out[...] = total[0:1, 0:1] / float(pairs)


def call(kernel, outs, *args, scratch=(), smem=0, fetched=0, aliases=None):
    vmem = pl.BlockSpec(memory_space=pltpu.VMEM)
    scalar = pl.BlockSpec(memory_space=pltpu.SMEM)
    anywhere = pl.BlockSpec(memory_space=pltpu.HBM)
    held = len(args) - fetched
    args = args[:held] + tuple(pltpu.with_memory_space_constraint(a, pltpu.HBM) for a in args[held:])
    buffers = [pltpu.VMEM(a.shape, a.dtype) for a in args[len(args) - fetched :]]
    if fetched:
        buffers.append(pltpu.SemaphoreType.DMA((fetched,)))
    return pl.pallas_call(
        kernel,
        out_shape=[jax.ShapeDtypeStruct(s, d) for s, d in outs],
        in_specs=[scalar] * smem + [vmem] * (len(args) - smem - fetched) + [anywhere] * fetched,
        out_specs=[scalar if s == (1, 1) and d == ID else vmem for s, d in outs],
        scratch_shapes=buffers + [pltpu.VMEM(s, d) for s, d in scratch],
        input_output_aliases=aliases or {},
        compiler_params=pltpu.CompilerParams(vmem_limit_bytes=VMEM_LIMIT),
    )(*args)


ORDER = (2, 3, 1, 0)


def matching(m, count):
    pairs = []
    for i in range(count):
        j = (i ^ 1, ((i + 1) ^ 1) - 1, i ^ 2, ((i + 2) ^ 2) - 2)[m]
        if 0 <= j < count:
            pairs.append((i, j))
    return pairs


def exchange(blocks):
    count = lax.axis_size("brick")
    return [lax.ppermute(blocks[m], "brick", matching(m, count)) for m in ORDER]


def exchange_and_add(blocks, energy, step):
    blocks, energy = lax.optimization_barrier((blocks, energy))
    energy = add_across(energy, step)
    return exchange(blocks), energy


def from_across(value, step):
    count = lax.axis_size("brick")
    if step >= count:
        return jnp.zeros_like(value)
    return lax.ppermute(value, "brick", [(i, i ^ step) for i in range(count)])


def add_across(value, step):
    return value + from_across(value, step)


def per_device(
    positions, species, pair_first, pair_second, pair_valid, send_list, w_radial, w_first, w_second, w_value, w_env,
    w_latent, w_tensor, w_mix, w_read, read_vec,
):
    brick = lax.axis_index("brick")
    flips = jnp.stack([brick & 1, (brick >> 1) & 1]).reshape(1, 2)
    spec = species[None, :]

    message = ((8, GHOST), F32)
    *messages, ohs, live, atoms = call(
        send_kernel,
        [message] * 4 + [((OWN, 4 * GHOST), BF16), ((1, 1), jnp.int32), ((8, OWN), F32)],
        flips, positions, spec, send_list, pair_valid, smem=1, fetched=4,
    )
    coords = exchange(messages)
    shapes = (
        (LAT, 64), (2 * USE + LAT, 3 * LAT), (2, LAT, 3 * CH), (USE + LAT, 3 * LAT), (LAT, 3 * LAT), (3 * LAT, 3 * LAT),
        (2 * LAT + CH, 3 * LAT), (2 * LAT, 3 * CH), (2 * LAT, 3 * CH), (LAT + CH, 3 * LAT), (LAT, 3 * CH), (LAT, 3 * CH),
        (NB, 3 * LAT),
    )
    oh, ids, mask, embed, enter, tens, step, leave, read_t, lt1_t, val1_t, env1_t, lt0_t, val0_t, env0_t, rad_t, column = call(
        prepare_kernel,
        [((ROWS, PAIRS), BF16), ((2, BRICK_BLOCKS, 128), ID), ((BRICK_BLOCKS, 128), F32)]
        + [(s, BF16) for s in shapes]
        + [((LAT, 1), F32)],
        flips, pair_first, pair_second, pair_valid, w_radial.T, w_first.T, w_second.T, w_value, w_env, w_latent,
        jnp.swapaxes(w_tensor, 1, 2), w_mix, w_read, read_vec[None, :],
        smem=1, fetched=13,
    )

    def rows(n):
        return ((n, PAIRS), F32)

    owned = ((VEC, OWN), F32)
    ghosted = [((VEC, GHOST), F32)] * 4
    partials = [((2 * WIDE, PAIRS), BF16)] + ghosted
    table = ((2 * VEC, 4 * GHOST), BF16)
    acc = ((4 * GHOST, 2 * WIDE), F32)

    def own_part(parts, out):
        return call(own_scatter_kernel, [out], parts, oh)[0]

    def gathered(own, listed):
        (gap,) = call(own_gather_kernel, [rows(VEC)], own, oh)
        return [gap] + listed

    def combine(own, arrived):
        own, *listed = call(combine_kernel, [owned] + ghosted, own, *arrived, ohs)
        return own, listed

    def complete(parts, ghosts):
        arrived = exchange(ghosts)
        own, listed = combine(own_part(parts, owned), arrived)
        return gathered(own, exchange(listed))

    def complete_and_add(parts, ghosts, energy, steps):
        arrived, energy = exchange_and_add(ghosts, energy, steps[0])
        own, listed = combine(own_part(parts, owned), arrived)
        listed, energy = exchange_and_add(listed, energy, steps[1])
        return gathered(own, listed), energy

    geo, slope, use, later, parts, *ghosts = call(
        embed_kernel,
        [rows(8), rows(LAT), rows(2 * CH), rows(USE + 2 * LAT)] + partials,
        live, atoms, *coords, ids, mask, oh, embed, enter,
        scratch=[acc],
        smem=1,
    )
    given = complete(parts, ghosts)
    gap0, later, parts, *ghosts = call(
        middle_kernel,
        [rows(VEC), rows(USE + 2 * LAT)] + partials,
        live, *given, oh, geo, use, later, tens, step,
        scratch=[table, acc], smem=1, aliases={1: 0, 9: 1},
    )
    given = complete(parts, ghosts)
    energy, dlat, dgeo, parts, *ghosts = call(
        turn_kernel,
        [((8, 128), F32), rows(2 * LAT), rows(8)] + partials,
        live, *given, oh, geo, later, column, tens, leave, read_t, lt1_t, val1_t,
        scratch=[table, acc], smem=1,
    )
    energy = add_across(energy, 1)
    given, energy = complete_and_add(parts, ghosts, energy, (2, 4))
    dlat, dgeo, parts, *ghosts = call(
        back_kernel,
        [rows(2 * LAT), rows(8)] + partials,
        live, *given, oh, geo, later, dlat, dgeo, gap0, use, lt0_t, val0_t, env1_t,
        scratch=[table, acc], smem=1, aliases={9: 0, 10: 1},
    )
    given, energy = complete_and_add(parts, ghosts, energy, (8, 16))
    parts, *ghosts = call(
        force_kernel,
        [((WIDE, PAIRS), BF16)] + [((8, GHOST), F32)] * 4,
        live, *given, oh, geo, use, dlat, dgeo, slope, env0_t, rad_t,
        scratch=[table, ((4 * GHOST, WIDE), F32)], smem=1,
    )
    arrived, energy = exchange_and_add(ghosts, energy, 32)
    own = own_part(parts, ((8, OWN), F32))
    forces, total = call(
        functools.partial(final_kernel, lax.axis_size("brick") * PAIRS),
        [((3, OWN), F32), ((1, 1), F32)],
        own, *arrived, ohs, energy, from_across(energy, 64),
    )
    return (forces, total.reshape(()))


def solution(mesh):
    line = P("brick", None)
    return jax.shard_map(
        per_device,
        mesh=mesh,
        in_specs=(P(None, "brick"), P("brick"), line, line, line, line) + (P(),) * 10,
        out_specs=(P(None, "brick"), P()),
        check_vma=False,
    )
```

```python
import functools
import math

import jax
import jax.numpy as jnp
import numpy as np
from jax import lax
from jax.experimental import pallas as pl
from jax.experimental.pallas import tpu as pltpu
from jax.sharding import PartitionSpec as P

F32 = jnp.float32
BF16 = jnp.bfloat16
ID = jnp.int32

CUTOFF = 6.0
SOFTENING = 0.25
ENV_SCALE = 0.25
PAIR_SHIFT = 1.0

LAT = 64
CH = 32
NB = 8
VEC = 3 * CH
USE = 2 * CH + LAT
OWN = 512
GHOST = 256
ROWS = OWN + 4 * GHOST
WIN = 256
BRICK_BLOCKS = 48
PAIRS = BRICK_BLOCKS * 128
CHUNK = 3072
CHUNK_BLOCKS = CHUNK // 128
WIDE = 128

VMEM_LIMIT = 7 * 1024 * 1024


def fit_trig():
    r = np.cos(np.linspace(0.0, np.pi, 4001)) * 0.5
    x = r * r
    base = np.polynomial.chebyshev.Chebyshev
    safe = np.where(r == 0.0, 1.0, r)
    sine = np.where(r == 0.0, 2 * np.pi, np.sin(2 * np.pi * safe) / safe)
    s = base.fit(x, sine, 8, domain=[0.0, 0.25]).convert(kind=np.polynomial.Polynomial)
    c = base.fit(x, np.cos(2 * np.pi * r), 8, domain=[0.0, 0.25]).convert(kind=np.polynomial.Polynomial)
    return [float(v) for v in s.coef], [float(v) for v in c.coef]


SIN_COEF, COS_COEF = fit_trig()


def horner(coef, x):
    out = jnp.full_like(x, coef[-1])
    for c in coef[-2::-1]:
        out = out * x + c
    return out


def dot(a, b):
    return lax.dot_general(a, b, (((1,), (0,)), ((), ())), preferred_element_type=F32)


def dot_nt(a, b):
    return lax.dot_general(a, b, (((1,), (1,)), ((), ())), preferred_element_type=F32)


def split2(x):
    hi = x.astype(BF16)
    lo = (x - hi.astype(F32)).astype(BF16)
    return hi, lo


def split3(x):
    hi = x.astype(BF16).astype(F32)
    rest = x - hi
    mid = rest.astype(BF16).astype(F32)
    return hi, mid, (rest - mid)


def stack2(x):
    hi, lo = split2(x)
    return jnp.concatenate([hi, lo], axis=0)


def spread2(x):
    hi, lo = split2(x)
    pad = jnp.zeros((WIDE - x.shape[0], x.shape[1]), BF16)
    return jnp.concatenate([hi, pad, lo, pad], axis=0)


def weight3(w):
    hi, lo = split2(w)
    return jnp.concatenate([hi.astype(F32), hi.astype(F32), lo.astype(F32)], axis=1).astype(BF16)


def dense(w3, x):
    hi, lo = split2(x)
    return dot(w3, jnp.concatenate([hi, lo, hi], axis=0))


def sigmoid(x):
    return 0.5 * jnp.tanh(0.5 * x) + 0.5


def silu_and_slope(x):
    s = sigmoid(x)
    y = x * s
    return y, s + y * (1.0 - s)


def hot(ids, rows):
    at = lax.broadcasted_iota(jnp.int32, (rows, ids.shape[1]), 0)
    return jnp.where(at == ids, 1.0, 0.0).astype(BF16)


def window_hot(ids, window, value, at):
    local = jnp.clip(ids - window * WIN, -1, WIN).astype(F32).astype(BF16)
    return jnp.where(at == local, jnp.full((), value, BF16), jnp.zeros((), BF16))


def fold2(x):
    half = x.shape[0] // 2
    return x[:half] + x[half:]


def radial(dist):
    k = (lax.broadcasted_iota(jnp.int32, (NB, dist.shape[1]), 0) + 1).astype(F32)
    turns = k * (dist * (1.0 / (2.0 * CUTOFF)))
    r = turns - jnp.round(turns)
    x = r * r
    return r * horner(SIN_COEF, x), horner(COS_COEF, x), k * (math.pi / CUTOFF)


def lanes(c):
    return pl.ds(pl.multiple_of(c * CHUNK, CHUNK), CHUNK)


def weigh(geo, values):
    return jnp.concatenate([geo[m : m + 1] * values for m in range(3)], axis=0)


def project(geo, vectors):
    return (
        geo[0:1] * vectors[:CH]
        + geo[1:2] * vectors[CH : 2 * CH]
        + geo[2:3] * vectors[2 * CH :]
    )


def put_rows(rows, n):
    at = lax.broadcasted_iota(jnp.int32, (8, n), 0)
    out = jnp.zeros((8, n), F32)
    for i, row in enumerate(rows):
        out = jnp.where(at == i, row, out)
    return out


def dir_grad(dq, vectors):
    return [jnp.sum(dq * vectors[m * CH : (m + 1) * CH], axis=0, keepdims=True) for m in range(3)]


def fill_table(table_ref, ghost_refs):
    for m, ghost in enumerate(ghost_refs):
        hi, lo = split2(ghost[...])
        at = m * GHOST
        table_ref[:VEC, at : at + GHOST] = hi
        table_ref[VEC:, at : at + GHOST] = lo


def gather_ghosts(own_gap_ref, table_ref, oh_ref, at):
    return own_gap_ref[:, at] + fold2(dot(table_ref[...], oh_ref[OWN:, at]))


def scatter_ghosts(acc_ref, parts_out, parts, oh_ref, at):
    parts_out[:, at] = parts
    acc_ref[...] += dot_nt(oh_ref[OWN:, at], parts)


def emit(acc_ref, ghost_outs):
    for m, out in enumerate(ghost_outs):
        out[...] = join_parts(acc_ref[m * GHOST : (m + 1) * GHOST, :], out.shape[0])


def join_parts(acc, rows):
    if acc.shape[1] == WIDE:
        turned = acc.T
        return turned[:rows] + turned[rows : 2 * rows]
    return (acc[:, :WIDE] + acc[:, WIDE:]).T[:rows]


def start_fetch(sources, targets, sems):
    copies = [pltpu.make_async_copy(a, b, sems.at[i]) for i, (a, b) in enumerate(zip(sources, targets))]
    for copy in copies:
        copy.start()
    return copies


def fetch(sources, targets, sems):
    for copy in start_fetch(sources, targets, sems):
        copy.wait()


def pick(tables, ids, count):
    block, place = ids >> 7, ids & 127
    found = [jnp.zeros(ids.shape, F32)] * 4
    for w, (ref, at) in enumerate(tables[:count]):
        here = block == w
        for k in range(4):
            row = jnp.broadcast_to(ref[k : k + 1, at : at + 128], ids.shape)
            value = jnp.take_along_axis(row, place, axis=1, mode="promise_in_bounds")
            found[k] = jnp.where(here, value, found[k])
    return found


def send_kernel(
    flip_ref, pos_in, spec_in, send_in, valid_in, first_in, second_in,
    m0, m1, m2, m3, lists_ref, live_ref, atoms_ref, ids_ref, mask_ref,
    pos_ref, spec_ref, send_ref, valid_ref, first_ref, second_ref, sems,
):
    fetch(
        (pos_in, spec_in, send_in, valid_in, first_in, second_in),
        (pos_ref, spec_ref, send_ref, valid_ref, first_ref, second_ref),
        sems,
    )
    live = jnp.sum(valid_ref[:, 0:1].astype(F32)).astype(jnp.int32)
    live_ref[0, 0] = (live + CHUNK_BLOCKS - 1) // CHUNK_BLOCKS
    lists = []
    for m in range(4):
        other = jnp.full((1, GHOST), flip_ref[0, m // 2], jnp.int32) == 1
        lists.append(jnp.where(other, send_ref[m ^ 1 : (m ^ 1) + 1, :], send_ref[m : m + 1, :]))
    lists_ref[...] = jnp.concatenate(lists, axis=0)
    atoms_ref[...] = put_rows([pos_ref[i : i + 1, :] for i in range(3)] + [spec_ref[...].astype(F32)], OWN)
    halves = [ids[:, h * 128 : (h + 1) * 128] for ids in lists for h in range(GHOST // 128)]
    found = pick([(atoms_ref, w * 128) for w in range(OWN // 128)], jnp.concatenate(halves, axis=0), OWN // 128)
    for m, out in enumerate((m0, m1, m2, m3)):
        out[...] = put_rows(
            [jnp.concatenate([f[2 * m : 2 * m + 1], f[2 * m + 1 : 2 * m + 2]], axis=1) for f in found], GHOST
        )
    near, far = 1 - flip_ref[0, 0], 1 - flip_ref[0, 1]
    slot = second_ref[...] - OWN
    group = slot >> 8
    group = group ^ jnp.where(group < 2, near, far)
    ids_ref[0] = first_ref[...]
    ids_ref[1] = jnp.where(slot < 0, second_ref[...], OWN + group * GHOST + (slot & (GHOST - 1)))
    mask_ref[...] = valid_ref[...].astype(F32)


def lists_kernel(lists_ref, ohs_ref):
    at = lax.broadcasted_iota(jnp.int32, (WIN, GHOST), 0).astype(F32).astype(BF16)
    for m in range(4):
        for w in range(OWN // WIN):
            tile = window_hot(lists_ref[m : m + 1, :], w, 1.0, at)
            ohs_ref[w * WIN : (w + 1) * WIN, m * GHOST : (m + 1) * GHOST] = tile


def build_incidence(ids_ref, oh_ref):
    span = 512
    at = lax.broadcasted_iota(jnp.int32, (WIN, span), 0).astype(F32).astype(BF16)

    def body(c, carry):
        blocks = [pl.ds(c * (span // 128) + i, 1) for i in range(span // 128)]
        first = jnp.concatenate([ids_ref[0, b, :] for b in blocks], axis=1)
        second = jnp.concatenate([ids_ref[1, b, :] for b in blocks], axis=1)
        out = pl.ds(pl.multiple_of(c * span, span), span)
        for w in range(ROWS // WIN):
            tile = window_hot(second, w, -1.0, at)
            if w < OWN // WIN:
                tile = tile + window_hot(first, w, 1.0, at)
            oh_ref[w * WIN : (w + 1) * WIN, out] = tile
        return carry

    lax.fori_loop(0, PAIRS // span, body, 0)


def prepare_kernel(ids_ref, *refs):
    sources, refs = refs[:7], refs[7:]
    oh_ref, embed, enter = refs[:3]
    copies = start_fetch(sources, refs[3:10], refs[10])
    w_radial_t, w_first_t, w_second_t, w_value, w_env, w_latent, w_read = refs[3:10]
    build_incidence(ids_ref, oh_ref)
    for copy in copies:
        copy.wait()

    def parts(w):
        hi, lo = split2(w)
        return hi.astype(F32), lo.astype(F32)

    rh, rl = parts(w_radial_t[...].T)
    fh, fl = parts(w_first_t[...].T)
    sh, sl = parts(w_second_t[...].T)
    embed[...] = jnp.concatenate([rh, rh, rl, fh, sh, fl, sl, jnp.zeros_like(rh)], axis=1).astype(BF16)
    for l in range(2):
        use = jnp.concatenate([w_env[l], w_value[l], w_latent[l]], axis=0)
        enter[l * USE : (l + 1) * USE, :] = weight3(use)
    enter[2 * USE :, :] = weight3(w_read[...])


def weights_kernel(*refs):
    sources, refs = refs[:8], refs[8:]
    tens, step, leave, read_t, lt1_t, val1_t, env1_t, lt0_t, val0_t, env0_t, rad_t, column = refs[:12]
    fetch(sources, refs[12:20], refs[20])
    w_radial_t, w_value, w_env, w_latent, w_tensor_t, w_mix, w_read, read_vec = refs[12:20]
    use1 = jnp.concatenate([w_env[1], w_value[1], w_latent[1]], axis=0)
    use_mix0 = dense(weight3(use1), w_mix[0])
    read3 = weight3(w_read[...])
    read_mix0, read_mix1 = dense(read3, w_mix[0]), dense(read3, w_mix[1])
    for l in range(2):
        tens[l] = weight3(w_tensor_t[l].T)
    step[...] = weight3(jnp.concatenate([use_mix0, read_mix0], axis=0))
    leave[...] = weight3(read_mix1)
    read_t[...] = weight3(jnp.concatenate([w_read[...].T, read_mix1.T, read_mix0.T], axis=0))
    lt1_t[...] = weight3(jnp.concatenate([w_latent[1].T, w_tensor_t[1], use_mix0[2 * CH :].T], axis=0))
    val1_t[...] = weight3(jnp.concatenate([w_value[1].T, use_mix0[CH : 2 * CH].T], axis=0))
    env1_t[...] = weight3(jnp.concatenate([w_env[1].T, use_mix0[:CH].T], axis=0))
    lt0_t[...] = weight3(jnp.concatenate([w_latent[0].T, w_tensor_t[0]], axis=0))
    val0_t[...] = weight3(w_value[0].T)
    env0_t[...] = weight3(w_env[0].T)
    rad_t[...] = weight3(w_radial_t[...])
    diagonal = lax.broadcasted_iota(jnp.int32, (LAT, LAT), 0) == lax.broadcasted_iota(jnp.int32, (LAT, LAT), 1)
    column[...] = jnp.sum(jnp.where(diagonal, read_vec[...], 0.0), axis=1, keepdims=True)


def own_gather_kernel(own_ref, oh_ref, gap_out):
    table = stack2(own_ref[...])
    for c in range(PAIRS // CHUNK):
        at = slice(c * CHUNK, (c + 1) * CHUNK)
        gap_out[:, at] = fold2(dot(table, oh_ref[:OWN, at]))


def own_scatter_kernel(parts_ref, oh_ref, own_out):
    own_out[...] = join_parts(dot_nt(oh_ref[:OWN, :], parts_ref[...]), own_out.shape[0])


def clear_rest(live_ref, parts_out):
    def body(c, carry):
        parts_out[:, lanes(c)] = jnp.zeros((parts_out.shape[0], CHUNK), BF16)
        return carry

    lax.fori_loop(live_ref[0, 0], PAIRS // CHUNK, body, 0)


def embed_kernel(
    live_ref, own_ref, c2, c3, c1, c0, ids_ref, mask_ref, oh_ref, w_embed, w_enter,
    geo_out, slope_out, use_out, next_out, parts_out, g0, g1, g2, g3, acc_ref,
):
    tables = [(own_ref, w * 128) for w in range(OWN // 128)]
    tables += [(c, w * 128) for c in (c0, c1, c2, c3) for w in range(GHOST // 128)]

    one = pick(tables, ids_ref[0], OWN // 128)
    two = pick(tables, ids_ref[1], ROWS // 128)
    mask = mask_ref[...]
    diff = [two[k] - one[k] for k in range(3)]
    sq = diff[0] * diff[0] + diff[1] * diff[1] + diff[2] * diff[2] + SOFTENING
    dist = jnp.sqrt(sq)
    inv = 1.0 / dist
    shrink = 1.0 - sq * (1.0 / CUTOFF**2)
    env = shrink * shrink
    columns = [d * inv for d in diff] + [env * mask, dist, mask, env * inv, one[3] + 8.0 * two[3]]
    for b in range(BRICK_BLOCKS):
        geo_out[:, b * 128 : (b + 1) * 128] = jnp.concatenate([column[b : b + 1] for column in columns], axis=0)
    acc_ref[...] = jnp.zeros_like(acc_ref)
    clear_rest(live_ref, parts_out)

    def body(c, carry):
        at = lanes(c)
        geo = geo_out[:, at]
        sines, _, _ = radial(geo[4:5])
        basis = sines * geo[6:7]
        bh = basis.astype(BF16).astype(F32)
        bl = basis - bh
        row = lax.broadcasted_iota(jnp.int32, (8, CHUNK), 0).astype(F32)
        code = geo[7:8]
        other = jnp.floor(code * 0.125)
        sf = jnp.where(row == code - 8.0 * other, 1.0, 0.0)
        ss = jnp.where(row == other, 1.0, 0.0)
        pre = dot(
            w_embed[...],
            jnp.concatenate([bh, bl, bh, sf, ss, sf, ss, jnp.zeros_like(bh)], axis=0).astype(BF16),
        )
        lat, slope = silu_and_slope(pre)
        slope_out[:, at] = slope
        enter = dense(w_enter[...], lat)
        use_out[:, at] = enter[: 2 * CH]
        next_out[:, at] = enter[2 * CH :]
        scatter_ghosts(acc_ref, parts_out, spread2(weigh(geo, enter[:CH] * geo[3:4])), oh_ref, at)
        return carry

    lax.fori_loop(0, live_ref[0, 0], body, 0)
    emit(acc_ref, (g0, g1, g2, g3))


def combine_kernel(own_ref, r2, r3, r1, r0, ohs_ref, own_out, g0, g1, g2, g3):
    arrived = jnp.concatenate([r[...] for r in (r0, r1, r2, r3)], axis=1)
    owned = own_ref[...] + fold2(dot_nt(stack2(arrived), ohs_ref[...]))
    own_out[...] = owned
    ghosts = fold2(dot(stack2(owned), ohs_ref[...]))
    for m, out in enumerate((g0, g1, g2, g3)):
        out[...] = ghosts[:, m * GHOST : (m + 1) * GHOST]


def middle_kernel(
    live_ref, own_gap_ref, t2, t3, t1, t0, oh_ref, geo_ref, use_ref, next_ref, w_tens, w_step,
    gap_out, next_out, parts_out, g0, g1, g2, g3, table_ref, acc_ref,
):
    fill_table(table_ref, (t0, t1, t2, t3))
    acc_ref[...] = jnp.zeros_like(acc_ref)
    clear_rest(live_ref, parts_out)

    def body(c, carry):
        at = lanes(c)
        gap = gather_ghosts(own_gap_ref, table_ref, oh_ref, at)
        gap_out[:, at] = gap
        geo = geo_ref[:, at]
        scalars = (ENV_SCALE * use_ref[CH : 2 * CH, at]) * project(geo, gap)
        hid = next_ref[:LAT, at] + dense(w_tens[0], scalars)
        later = next_ref[LAT:, at] + dense(w_step[...], hid * sigmoid(hid))
        next_out[:LAT, at] = hid
        next_out[LAT:, at] = later
        scatter_ghosts(acc_ref, parts_out, spread2(weigh(geo, later[:CH] * geo[3:4])), oh_ref, at)
        return carry

    lax.fori_loop(0, live_ref[0, 0], body, 0)
    emit(acc_ref, (g0, g1, g2, g3))


def update_back(geo, gap, values, dhid, w_lt_t, w_val_t):
    both = dense(w_lt_t, dhid)
    dscal = both[LAT : LAT + CH] * ENV_SCALE
    return both, dense(w_val_t, project(geo, gap) * dscal), values * dscal


def turn_kernel(
    live_ref, own_gap_ref, t2, t3, t1, t0, oh_ref, geo_ref, next_ref, read_vec, w_tens, w_leave, w_read_t, w_lt_t, w_val_t,
    energy_out, dlat_out, dgeo_out, parts_out, g0, g1, g2, g3, table_ref, acc_ref,
):
    fill_table(table_ref, (t0, t1, t2, t3))
    acc_ref[...] = jnp.zeros_like(acc_ref)
    clear_rest(live_ref, parts_out)
    rv = read_vec[...]

    def body(c, energy):
        at = lanes(c)
        gap = gather_ghosts(own_gap_ref, table_ref, oh_ref, at)
        geo = geo_ref[:, at]
        weight = geo[3:4]
        values = next_ref[LAT + CH : LAT + 2 * CH, at]
        scalars = (ENV_SCALE * values) * project(geo, gap)
        hid = next_ref[LAT + 2 * CH : LAT + USE, at] + dense(w_tens[1], scalars)
        act, hid_slope = silu_and_slope(hid)
        out, out_slope = silu_and_slope(next_ref[LAT + USE :, at] + dense(w_leave[...], act))
        pair_energy = jnp.sum(rv * out, axis=0, keepdims=True) + PAIR_SHIFT
        back = dense(w_read_t[...], out_slope * (rv * weight))
        both, more, dq = update_back(geo, gap, values, back[LAT : 2 * LAT] * hid_slope, w_lt_t[...], w_val_t[...])
        dlat_out[:LAT, at] = back[:LAT] + both[:LAT] + more[:LAT]
        dlat_out[LAT:, at] = back[2 * LAT :] + both[LAT + CH :] + more[LAT:]
        dgeo_out[:, at] = put_rows(dir_grad(dq, gap) + [pair_energy], CHUNK)
        scatter_ghosts(acc_ref, parts_out, spread2(weigh(geo, dq)), oh_ref, at)
        return energy + pair_energy * weight

    energy = lax.fori_loop(0, live_ref[0, 0], body, jnp.zeros((1, CHUNK), F32))
    energy_out[...] = jnp.broadcast_to(jnp.sum(energy, axis=1, keepdims=True), energy_out.shape)
    emit(acc_ref, (g0, g1, g2, g3))


def environment_back(geo, dvec, env_values, dlat, dgeo, w_env_t):
    weight = geo[3:4]
    dscaled = project(geo, dvec)
    rows = dir_grad(env_values * weight, dvec)
    rows.append(jnp.sum(env_values * dscaled, axis=0, keepdims=True))
    return dlat + dense(w_env_t, dscaled * weight), dgeo + put_rows(rows, CHUNK)


def back_kernel(
    live_ref, own_gap_ref, t2, t3, t1, t0, oh_ref, geo_ref, next_ref, dlat_ref, dgeo_ref, gap_ref, use_ref,
    w_lt_t, w_val_t, w_env_t,
    dlat_out, dgeo_out, parts_out, g0, g1, g2, g3, table_ref, acc_ref,
):
    fill_table(table_ref, (t0, t1, t2, t3))
    acc_ref[...] = jnp.zeros_like(acc_ref)
    clear_rest(live_ref, parts_out)

    def body(c, carry):
        at = lanes(c)
        dvec = gather_ghosts(own_gap_ref, table_ref, oh_ref, at)
        geo = geo_ref[:, at]
        dlat, dgeo = environment_back(geo, dvec, next_ref[LAT : LAT + CH, at], dlat_ref[:, at], dgeo_ref[:, at], w_env_t[...])
        gap = gap_ref[:, at]
        _, hid_slope = silu_and_slope(next_ref[:LAT, at])
        both, more, dq = update_back(geo, gap, use_ref[CH : 2 * CH, at], dlat[LAT:] * hid_slope, w_lt_t[...], w_val_t[...])
        dlat_out[:LAT, at] = dlat[:LAT] + both[:LAT] + more
        dgeo_out[:, at] = dgeo + put_rows(dir_grad(dq, gap), CHUNK)
        scatter_ghosts(acc_ref, parts_out, spread2(weigh(geo, dq)), oh_ref, at)
        return carry

    lax.fori_loop(0, live_ref[0, 0], body, 0)
    emit(acc_ref, (g0, g1, g2, g3))


def force_kernel(
    live_ref, own_gap_ref, t2, t3, t1, t0, oh_ref, geo_ref, use_ref, dlat_ref, dgeo_ref, slope_ref,
    w_env_t, w_rad_t,
    parts_out, g0, g1, g2, g3, table_ref, acc_ref,
):
    fill_table(table_ref, (t0, t1, t2, t3))
    acc_ref[...] = jnp.zeros_like(acc_ref)
    clear_rest(live_ref, parts_out)

    def body(c, carry):
        at = lanes(c)
        dvec = gather_ghosts(own_gap_ref, table_ref, oh_ref, at)
        geo = geo_ref[:, at]
        dlat, dgeo = environment_back(geo, dvec, use_ref[:CH, at], dlat_ref[:LAT, at], dgeo_ref[:, at], w_env_t[...])
        dbasis = dense(w_rad_t[...], dlat * slope_ref[:, at])
        dist, mask = geo[4:5], geo[5:6]
        inv = 1.0 / dist
        shrink = 1.0 - dist * dist * (1.0 / CUTOFF**2)
        env = shrink * shrink
        sines, cosines, freq = radial(dist)
        along = jnp.sum(dbasis * sines, axis=0, keepdims=True) * inv
        ddist = (jnp.sum(dbasis * (freq * cosines), axis=0, keepdims=True) - along) * (inv * env)
        denv = along + mask * dgeo[3:4]
        ddist = ddist - denv * shrink * dist * (4.0 / CUTOFF**2)
        row = lax.broadcasted_iota(jnp.int32, (8, CHUNK), 0)
        unit = jnp.where(row < 3, geo, 0.0)
        dunit = jnp.where(row < 3, dgeo, 0.0)
        radial_part = ddist - jnp.sum(unit * dunit, axis=0, keepdims=True) * inv
        ddiff = dunit * inv + unit * radial_part
        hi = ddiff.astype(BF16).astype(F32)
        both = jnp.concatenate([hi, ddiff - hi], axis=0).astype(BF16)
        parts = jnp.concatenate([both, jnp.zeros((WIDE - 16, CHUNK), BF16)], axis=0)
        scatter_ghosts(acc_ref, parts_out, parts, oh_ref, at)
        return carry

    lax.fori_loop(0, live_ref[0, 0], body, 0)
    emit(acc_ref, (g0, g1, g2, g3))


def final_kernel(pairs, own_ref, r2, r3, r1, r0, ohs_ref, energy_ref, other_ref, out_ref, energy_out):
    arrived = jnp.concatenate([r[...] for r in (r0, r1, r2, r3)], axis=1)
    hi, mid, lo = split3(arrived)
    parts = jnp.concatenate([hi, mid, lo, jnp.zeros_like(hi)], axis=0).astype(BF16)
    got = dot_nt(parts, ohs_ref[...])
    out_ref[...] = (own_ref[...] + got[0:8] + got[8:16] + got[16:24])[0:3]
    total = energy_ref[...] + other_ref[...]
    energy_out[...] = total[0:1, 0:1] / float(pairs)


def call(kernel, outs, *args, scratch=(), smem=0, fetched=0, aliases=None):
    vmem = pl.BlockSpec(memory_space=pltpu.VMEM)
    scalar = pl.BlockSpec(memory_space=pltpu.SMEM)
    anywhere = pl.BlockSpec(memory_space=pltpu.HBM)
    held = len(args) - fetched
    args = args[:held] + tuple(pltpu.with_memory_space_constraint(a, pltpu.HBM) for a in args[held:])
    buffers = [pltpu.VMEM(a.shape, a.dtype) for a in args[len(args) - fetched :]]
    if fetched:
        buffers.append(pltpu.SemaphoreType.DMA((fetched,)))
    return pl.pallas_call(
        kernel,
        out_shape=[jax.ShapeDtypeStruct(s, d) for s, d in outs],
        in_specs=[scalar] * smem + [vmem] * (len(args) - smem - fetched) + [anywhere] * fetched,
        out_specs=[scalar if s == (1, 1) and d == ID else vmem for s, d in outs],
        scratch_shapes=buffers + [pltpu.VMEM(s, d) for s, d in scratch],
        input_output_aliases=aliases or {},
        compiler_params=pltpu.CompilerParams(vmem_limit_bytes=VMEM_LIMIT),
    )(*args)


ORDER = (2, 3, 1, 0)


def matching(m, count):
    pairs = []
    for i in range(count):
        j = (i ^ 1, ((i + 1) ^ 1) - 1, i ^ 2, ((i + 2) ^ 2) - 2)[m]
        if 0 <= j < count:
            pairs.append((i, j))
    return pairs


def exchange(blocks):
    count = lax.axis_size("brick")
    return [lax.ppermute(blocks[m], "brick", matching(m, count)) for m in ORDER]


def exchange_and_add(blocks, energy, step):
    blocks, energy = lax.optimization_barrier((blocks, energy))
    energy = add_across(energy, step)
    return exchange(blocks), energy


def from_across(value, step):
    count = lax.axis_size("brick")
    if step >= count:
        return jnp.zeros_like(value)
    return lax.ppermute(value, "brick", [(i, i ^ step) for i in range(count)])


def add_across(value, step):
    return value + from_across(value, step)


def per_device(
    positions, species, pair_first, pair_second, pair_valid, send_list, w_radial, w_first, w_second, w_value, w_env,
    w_latent, w_tensor, w_mix, w_read, read_vec,
):
    brick = lax.axis_index("brick")
    flips = jnp.stack([brick & 1, (brick >> 1) & 1]).reshape(1, 2)
    spec = species[None, :]

    message = ((8, GHOST), F32)
    *messages, lists, live, atoms, ids, mask = call(
        send_kernel,
        [message] * 4
        + [((4, GHOST), ID), ((1, 1), ID), ((8, OWN), F32), ((2, BRICK_BLOCKS, 128), ID), ((BRICK_BLOCKS, 128), F32)],
        flips, positions, spec, send_list, pair_valid, pair_first, pair_second, smem=1, fetched=6,
    )
    coords = exchange(messages)
    oh, embed, enter = call(
        prepare_kernel,
        [((ROWS, PAIRS), BF16), ((LAT, 64), BF16), ((2 * USE + LAT, 3 * LAT), BF16)],
        ids, w_radial.T, w_first.T, w_second.T, w_value, w_env, w_latent, w_read,
        fetched=7,
    )

    def rows(n):
        return ((n, PAIRS), F32)

    owned = ((VEC, OWN), F32)
    ghosted = [((VEC, GHOST), F32)] * 4
    partials = [((2 * WIDE, PAIRS), BF16)] + ghosted
    table = ((2 * VEC, 4 * GHOST), BF16)
    acc = ((4 * GHOST, 2 * WIDE), F32)

    def own_part(parts, out):
        return call(own_scatter_kernel, [out], parts, oh)[0]

    def gathered(own, listed):
        (gap,) = call(own_gather_kernel, [rows(VEC)], own, oh)
        return [gap] + listed

    def combine(own, arrived, ohs):
        own, *listed = call(combine_kernel, [owned] + ghosted, own, *arrived, ohs)
        return own, listed

    def complete(parts, ghosts, ohs):
        arrived = exchange(ghosts)
        own, listed = combine(own_part(parts, owned), arrived, ohs)
        return gathered(own, exchange(listed))

    def complete_and_add(parts, ghosts, energy, steps):
        arrived, energy = exchange_and_add(ghosts, energy, steps[0])
        own, listed = combine(own_part(parts, owned), arrived, ohs)
        listed, energy = exchange_and_add(listed, energy, steps[1])
        return gathered(own, listed), energy

    geo, slope, use, later, parts, *ghosts = call(
        embed_kernel,
        [rows(8), rows(LAT), rows(2 * CH), rows(USE + 2 * LAT)] + partials,
        live, atoms, *coords, ids, mask, oh, embed, enter,
        scratch=[acc],
        smem=1,
    )
    ghosts, lists = lax.optimization_barrier((ghosts, lists))
    (ohs,) = call(lists_kernel, [((OWN, 4 * GHOST), BF16)], lists)
    arrived = exchange(ghosts)
    own, listed = combine(own_part(parts, owned), arrived, ohs)
    sources = (
        w_radial.T, w_value, w_env, w_latent, jnp.swapaxes(w_tensor, 1, 2), w_mix, w_read, read_vec[None, :],
    )
    listed, sources = lax.optimization_barrier((listed, sources))
    given = gathered(own, exchange(listed))
    shapes = (
        (2, LAT, 3 * CH), (USE + LAT, 3 * LAT), (LAT, 3 * LAT), (3 * LAT, 3 * LAT),
        (2 * LAT + CH, 3 * LAT), (2 * LAT, 3 * CH), (2 * LAT, 3 * CH), (LAT + CH, 3 * LAT), (LAT, 3 * CH), (LAT, 3 * CH),
        (NB, 3 * LAT),
    )
    tens, step, leave, read_t, lt1_t, val1_t, env1_t, lt0_t, val0_t, env0_t, rad_t, column = call(
        weights_kernel, [(s, BF16) for s in shapes] + [((LAT, 1), F32)], *sources, fetched=8,
    )
    gap0, later, parts, *ghosts = call(
        middle_kernel,
        [rows(VEC), rows(USE + 2 * LAT)] + partials,
        live, *given, oh, geo, use, later, tens, step,
        scratch=[table, acc], smem=1, aliases={1: 0, 9: 1},
    )
    given = complete(parts, ghosts, ohs)
    energy, dlat, dgeo, parts, *ghosts = call(
        turn_kernel,
        [((8, 128), F32), rows(2 * LAT), rows(8)] + partials,
        live, *given, oh, geo, later, column, tens, leave, read_t, lt1_t, val1_t,
        scratch=[table, acc], smem=1,
    )
    energy = add_across(energy, 1)
    given, energy = complete_and_add(parts, ghosts, energy, (2, 4))
    dlat, dgeo, parts, *ghosts = call(
        back_kernel,
        [rows(2 * LAT), rows(8)] + partials,
        live, *given, oh, geo, later, dlat, dgeo, gap0, use, lt0_t, val0_t, env1_t,
        scratch=[table, acc], smem=1, aliases={9: 0, 10: 1},
    )
    given, energy = complete_and_add(parts, ghosts, energy, (8, 16))
    parts, *ghosts = call(
        force_kernel,
        [((WIDE, PAIRS), BF16)] + [((8, GHOST), F32)] * 4,
        live, *given, oh, geo, use, dlat, dgeo, slope, env0_t, rad_t,
        scratch=[table, ((4 * GHOST, WIDE), F32)], smem=1,
    )
    arrived, energy = exchange_and_add(ghosts, energy, 32)
    own = own_part(parts, ((8, OWN), F32))
    forces, total = call(
        functools.partial(final_kernel, lax.axis_size("brick") * PAIRS),
        [((3, OWN), F32), ((1, 1), F32)],
        own, *arrived, ohs, energy, from_across(energy, 64),
    )
    return (forces, total.reshape(()))


def solution(mesh):
    line = P("brick", None)
    return jax.shard_map(
        per_device,
        mesh=mesh,
        in_specs=(P(None, "brick"), P("brick"), line, line, line, line) + (P(),) * 10,
        out_specs=(P(None, "brick"), P()),
        check_vma=False,
    )
```

```python
import functools
import math

import jax
import jax.numpy as jnp
import numpy as np
from jax import lax
from jax.experimental import pallas as pl
from jax.experimental.pallas import tpu as pltpu
from jax.sharding import PartitionSpec as P

F32 = jnp.float32
BF16 = jnp.bfloat16
ID = jnp.int32

CUTOFF = 6.0
SOFTENING = 0.25
ENV_SCALE = 0.25
PAIR_SHIFT = 1.0

LAT = 64
CH = 32
NB = 8
VEC = 3 * CH
USE = 2 * CH + LAT
OWN = 512
GHOST = 256
ROWS = OWN + 4 * GHOST
WIN = 256
BRICK_BLOCKS = 48
PAIRS = BRICK_BLOCKS * 128
CHUNK = 3072
CHUNK_BLOCKS = CHUNK // 128
WIDE = 128

VMEM_LIMIT = 7 * 1024 * 1024


def fit_trig():
    r = np.cos(np.linspace(0.0, np.pi, 4001)) * 0.5
    x = r * r
    base = np.polynomial.chebyshev.Chebyshev
    safe = np.where(r == 0.0, 1.0, r)
    sine = np.where(r == 0.0, 2 * np.pi, np.sin(2 * np.pi * safe) / safe)
    s = base.fit(x, sine, 8, domain=[0.0, 0.25]).convert(kind=np.polynomial.Polynomial)
    c = base.fit(x, np.cos(2 * np.pi * r), 8, domain=[0.0, 0.25]).convert(kind=np.polynomial.Polynomial)
    return [float(v) for v in s.coef], [float(v) for v in c.coef]


SIN_COEF, COS_COEF = fit_trig()


def horner(coef, x):
    out = jnp.full_like(x, coef[-1])
    for c in coef[-2::-1]:
        out = out * x + c
    return out


def dot(a, b):
    return lax.dot_general(a, b, (((1,), (0,)), ((), ())), preferred_element_type=F32)


def dot_nt(a, b):
    return lax.dot_general(a, b, (((1,), (1,)), ((), ())), preferred_element_type=F32)


def split2(x):
    hi = x.astype(BF16)
    lo = (x - hi.astype(F32)).astype(BF16)
    return hi, lo


def split3(x):
    hi = x.astype(BF16).astype(F32)
    rest = x - hi
    mid = rest.astype(BF16).astype(F32)
    return hi, mid, (rest - mid)


def stack2(x):
    hi, lo = split2(x)
    return jnp.concatenate([hi, lo], axis=0)


def spread2(x):
    hi, lo = split2(x)
    pad = jnp.zeros((WIDE - x.shape[0], x.shape[1]), BF16)
    return jnp.concatenate([hi, pad, lo, pad], axis=0)


def weight3(w):
    hi, lo = split2(w)
    return jnp.concatenate([hi.astype(F32), hi.astype(F32), lo.astype(F32)], axis=1).astype(BF16)


def dense(w3, x):
    hi, lo = split2(x)
    return dot(w3, jnp.concatenate([hi, lo, hi], axis=0))


def sigmoid(x):
    return 0.5 * jnp.tanh(0.5 * x) + 0.5


def silu_and_slope(x):
    s = sigmoid(x)
    y = x * s
    return y, s + y * (1.0 - s)


def hot(ids, rows):
    at = lax.broadcasted_iota(jnp.int32, (rows, ids.shape[1]), 0)
    return jnp.where(at == ids, 1.0, 0.0).astype(BF16)


def window_hot(ids, window, value, at):
    local = jnp.clip(ids - window * WIN, -1, WIN).astype(F32).astype(BF16)
    return jnp.where(at == local, jnp.full((), value, BF16), jnp.zeros((), BF16))


def fold2(x):
    half = x.shape[0] // 2
    return x[:half] + x[half:]


def radial(dist):
    k = (lax.broadcasted_iota(jnp.int32, (NB, dist.shape[1]), 0) + 1).astype(F32)
    turns = k * (dist * (1.0 / (2.0 * CUTOFF)))
    r = turns - jnp.round(turns)
    x = r * r
    return r * horner(SIN_COEF, x), horner(COS_COEF, x), k * (math.pi / CUTOFF)


def lanes(c):
    return pl.ds(pl.multiple_of(c * CHUNK, CHUNK), CHUNK)


def weigh(geo, values):
    return jnp.concatenate([geo[m : m + 1] * values for m in range(3)], axis=0)


def project(geo, vectors):
    return (
        geo[0:1] * vectors[:CH]
        + geo[1:2] * vectors[CH : 2 * CH]
        + geo[2:3] * vectors[2 * CH :]
    )


def put_rows(rows, n):
    at = lax.broadcasted_iota(jnp.int32, (8, n), 0)
    out = jnp.zeros((8, n), F32)
    for i, row in enumerate(rows):
        out = jnp.where(at == i, row, out)
    return out


def dir_grad(dq, vectors):
    return [jnp.sum(dq * vectors[m * CH : (m + 1) * CH], axis=0, keepdims=True) for m in range(3)]


def fill_table(table_ref, ghost_refs):
    for m, ghost in enumerate(ghost_refs):
        hi, lo = split2(ghost[...])
        at = m * GHOST
        table_ref[:VEC, at : at + GHOST] = hi
        table_ref[VEC:, at : at + GHOST] = lo


def gather_ghosts(own_gap_ref, table_ref, oh_ref, at):
    return own_gap_ref[:, at] + fold2(dot(table_ref[...], oh_ref[OWN:, at]))


def scatter_ghosts(acc_ref, parts_out, parts, oh_ref, at):
    parts_out[:, at] = parts
    acc_ref[...] += dot_nt(oh_ref[OWN:, at], parts)


def emit(acc_ref, ghost_outs):
    for m, out in enumerate(ghost_outs):
        out[...] = join_parts(acc_ref[m * GHOST : (m + 1) * GHOST, :], out.shape[0])


def join_parts(acc, rows):
    if acc.shape[1] == WIDE:
        turned = acc.T
        return turned[:rows] + turned[rows : 2 * rows]
    return (acc[:, :WIDE] + acc[:, WIDE:]).T[:rows]


def start_fetch(sources, targets, sems):
    copies = [pltpu.make_async_copy(a, b, sems.at[i]) for i, (a, b) in enumerate(zip(sources, targets))]
    for copy in copies:
        copy.start()
    return copies


def fetch(sources, targets, sems):
    for copy in start_fetch(sources, targets, sems):
        copy.wait()


def pick(tables, ids, count):
    block, place = ids >> 7, ids & 127
    found = [jnp.zeros(ids.shape, F32)] * 4
    for w, (ref, at) in enumerate(tables[:count]):
        here = block == w
        for k in range(4):
            row = jnp.broadcast_to(ref[k : k + 1, at : at + 128], ids.shape)
            value = jnp.take_along_axis(row, place, axis=1, mode="promise_in_bounds")
            found[k] = jnp.where(here, value, found[k])
    return found


def send_kernel(
    flip_ref, pos_in, spec_in, send_in, valid_in, first_in, second_in,
    m0, m1, m2, m3, lists_ref, live_ref, atoms_ref, ids_ref, mask_ref,
    pos_ref, spec_ref, send_ref, valid_ref, first_ref, second_ref, sems,
):
    fetch(
        (pos_in, spec_in, send_in, valid_in, first_in, second_in),
        (pos_ref, spec_ref, send_ref, valid_ref, first_ref, second_ref),
        sems,
    )
    live = jnp.sum(valid_ref[:, 0:1].astype(F32)).astype(jnp.int32)
    live_ref[0, 0] = (live + CHUNK_BLOCKS - 1) // CHUNK_BLOCKS
    lists = []
    for m in range(4):
        other = jnp.full((1, GHOST), flip_ref[0, m // 2], jnp.int32) == 1
        lists.append(jnp.where(other, send_ref[m ^ 1 : (m ^ 1) + 1, :], send_ref[m : m + 1, :]))
    lists_ref[...] = jnp.concatenate(lists, axis=0)
    atoms_ref[...] = put_rows([pos_ref[i : i + 1, :] for i in range(3)] + [spec_ref[...].astype(F32)], OWN)
    halves = [ids[:, h * 128 : (h + 1) * 128] for ids in lists for h in range(GHOST // 128)]
    found = pick([(atoms_ref, w * 128) for w in range(OWN // 128)], jnp.concatenate(halves, axis=0), OWN // 128)
    for m, out in enumerate((m0, m1, m2, m3)):
        out[...] = put_rows(
            [jnp.concatenate([f[2 * m : 2 * m + 1], f[2 * m + 1 : 2 * m + 2]], axis=1) for f in found], GHOST
        )
    near, far = 1 - flip_ref[0, 0], 1 - flip_ref[0, 1]
    slot = second_ref[...] - OWN
    group = slot >> 8
    group = group ^ jnp.where(group < 2, near, far)
    ids_ref[0] = first_ref[...]
    ids_ref[1] = jnp.where(slot < 0, second_ref[...], OWN + group * GHOST + (slot & (GHOST - 1)))
    mask_ref[...] = valid_ref[...].astype(F32)


def lists_kernel(lists_ref, ohs_ref):
    at = lax.broadcasted_iota(jnp.int32, (WIN, GHOST), 0).astype(F32).astype(BF16)
    for m in range(4):
        for w in range(OWN // WIN):
            tile = window_hot(lists_ref[m : m + 1, :], w, 1.0, at)
            ohs_ref[w * WIN : (w + 1) * WIN, m * GHOST : (m + 1) * GHOST] = tile


def build_incidence(ids_ref, oh_ref):
    span = 512
    at = lax.broadcasted_iota(jnp.int32, (WIN, span), 0).astype(F32).astype(BF16)

    def body(c, carry):
        blocks = [pl.ds(c * (span // 128) + i, 1) for i in range(span // 128)]
        first = jnp.concatenate([ids_ref[0, b, :] for b in blocks], axis=1)
        second = jnp.concatenate([ids_ref[1, b, :] for b in blocks], axis=1)
        out = pl.ds(pl.multiple_of(c * span, span), span)
        for w in range(ROWS // WIN):
            tile = window_hot(second, w, -1.0, at)
            if w < OWN // WIN:
                tile = tile + window_hot(first, w, 1.0, at)
            oh_ref[w * WIN : (w + 1) * WIN, out] = tile
        return carry

    lax.fori_loop(0, PAIRS // span, body, 0)


def prepare_kernel(ids_ref, *refs):
    sources, refs = refs[:7], refs[7:]
    oh_ref, embed, enter = refs[:3]
    copies = start_fetch(sources, refs[3:10], refs[10])
    w_radial_t, w_first_t, w_second_t, w_value, w_env, w_latent, w_read = refs[3:10]
    build_incidence(ids_ref, oh_ref)
    for copy in copies:
        copy.wait()

    def parts(w):
        hi, lo = split2(w)
        return hi.astype(F32), lo.astype(F32)

    rh, rl = parts(w_radial_t[...].T)
    fh, fl = parts(w_first_t[...].T)
    sh, sl = parts(w_second_t[...].T)
    embed[...] = jnp.concatenate([rh, rh, rl, fh, sh, fl, sl, jnp.zeros_like(rh)], axis=1).astype(BF16)
    for l in range(2):
        use = jnp.concatenate([w_env[l], w_value[l], w_latent[l]], axis=0)
        enter[l * USE : (l + 1) * USE, :] = weight3(use)
    enter[2 * USE :, :] = weight3(w_read[...])


def weights_kernel(*refs):
    sources, refs = refs[:8], refs[8:]
    tens, step, leave, read_t, lt1_t, val1_t, env1_t, lt0_t, val0_t, env0_t, rad_t, column = refs[:12]
    fetch(sources, refs[12:20], refs[20])
    w_radial_t, w_value, w_env, w_latent, w_tensor_t, w_mix, w_read, read_vec = refs[12:20]
    use1 = jnp.concatenate([w_env[1], w_value[1], w_latent[1]], axis=0)
    use_mix0 = dense(weight3(use1), w_mix[0])
    read3 = weight3(w_read[...])
    read_mix0, read_mix1 = dense(read3, w_mix[0]), dense(read3, w_mix[1])
    for l in range(2):
        tens[l] = weight3(w_tensor_t[l].T)
    step[...] = weight3(jnp.concatenate([use_mix0, read_mix0], axis=0))
    leave[...] = weight3(read_mix1)
    read_t[...] = weight3(jnp.concatenate([w_read[...].T, read_mix1.T, read_mix0.T], axis=0))
    lt1_t[...] = weight3(jnp.concatenate([w_latent[1].T, w_tensor_t[1], use_mix0[2 * CH :].T], axis=0))
    val1_t[...] = weight3(jnp.concatenate([w_value[1].T, use_mix0[CH : 2 * CH].T], axis=0))
    env1_t[...] = weight3(jnp.concatenate([w_env[1].T, use_mix0[:CH].T], axis=0))
    lt0_t[...] = weight3(jnp.concatenate([w_latent[0].T, w_tensor_t[0]], axis=0))
    val0_t[...] = weight3(w_value[0].T)
    env0_t[...] = weight3(w_env[0].T)
    rad_t[...] = weight3(w_radial_t[...])
    diagonal = lax.broadcasted_iota(jnp.int32, (LAT, LAT), 0) == lax.broadcasted_iota(jnp.int32, (LAT, LAT), 1)
    column[...] = jnp.sum(jnp.where(diagonal, read_vec[...], 0.0), axis=1, keepdims=True)


def own_gather_kernel(own_ref, oh_ref, gap_out):
    table = stack2(own_ref[...])
    for c in range(PAIRS // CHUNK):
        at = slice(c * CHUNK, (c + 1) * CHUNK)
        gap_out[:, at] = fold2(dot(table, oh_ref[:OWN, at]))


def own_scatter_kernel(parts_ref, oh_ref, own_out):
    own_out[...] = join_parts(dot_nt(oh_ref[:OWN, :], parts_ref[...]), own_out.shape[0])


def clear_rest(live_ref, parts_out):
    def body(c, carry):
        parts_out[:, lanes(c)] = jnp.zeros((parts_out.shape[0], CHUNK), BF16)
        return carry

    lax.fori_loop(live_ref[0, 0], PAIRS // CHUNK, body, 0)


def embed_kernel(
    live_ref, own_ref, c3, c2, c1, c0, ids_ref, mask_ref, oh_ref, w_embed, w_enter,
    geo_out, slope_out, use_out, next_out, parts_out, g0, g1, g2, g3, acc_ref,
):
    tables = [(own_ref, w * 128) for w in range(OWN // 128)]
    tables += [(c, w * 128) for c in (c0, c1, c2, c3) for w in range(GHOST // 128)]

    one = pick(tables, ids_ref[0], OWN // 128)
    two = pick(tables, ids_ref[1], ROWS // 128)
    mask = mask_ref[...]
    diff = [two[k] - one[k] for k in range(3)]
    sq = diff[0] * diff[0] + diff[1] * diff[1] + diff[2] * diff[2] + SOFTENING
    dist = jnp.sqrt(sq)
    inv = 1.0 / dist
    shrink = 1.0 - sq * (1.0 / CUTOFF**2)
    env = shrink * shrink
    columns = [d * inv for d in diff] + [env * mask, dist, mask, env * inv, one[3] + 8.0 * two[3]]
    for b in range(BRICK_BLOCKS):
        geo_out[:, b * 128 : (b + 1) * 128] = jnp.concatenate([column[b : b + 1] for column in columns], axis=0)
    acc_ref[...] = jnp.zeros_like(acc_ref)
    clear_rest(live_ref, parts_out)

    def body(c, carry):
        at = lanes(c)
        geo = geo_out[:, at]
        sines, _, _ = radial(geo[4:5])
        basis = sines * geo[6:7]
        bh = basis.astype(BF16).astype(F32)
        bl = basis - bh
        row = lax.broadcasted_iota(jnp.int32, (8, CHUNK), 0).astype(F32)
        code = geo[7:8]
        other = jnp.floor(code * 0.125)
        sf = jnp.where(row == code - 8.0 * other, 1.0, 0.0)
        ss = jnp.where(row == other, 1.0, 0.0)
        pre = dot(
            w_embed[...],
            jnp.concatenate([bh, bl, bh, sf, ss, sf, ss, jnp.zeros_like(bh)], axis=0).astype(BF16),
        )
        lat, slope = silu_and_slope(pre)
        slope_out[:, at] = slope
        enter = dense(w_enter[...], lat)
        use_out[:, at] = enter[: 2 * CH]
        next_out[:, at] = enter[2 * CH :]
        scatter_ghosts(acc_ref, parts_out, spread2(weigh(geo, enter[:CH] * geo[3:4])), oh_ref, at)
        return carry

    lax.fori_loop(0, live_ref[0, 0], body, 0)
    emit(acc_ref, (g0, g1, g2, g3))


def combine_kernel(own_ref, r3, r2, r1, r0, ohs_ref, own_out, g0, g1, g2, g3):
    arrived = jnp.concatenate([r[...] for r in (r0, r1, r2, r3)], axis=1)
    owned = own_ref[...] + fold2(dot_nt(stack2(arrived), ohs_ref[...]))
    own_out[...] = owned
    ghosts = fold2(dot(stack2(owned), ohs_ref[...]))
    for m, out in enumerate((g0, g1, g2, g3)):
        out[...] = ghosts[:, m * GHOST : (m + 1) * GHOST]


def middle_kernel(
    live_ref, own_gap_ref, t3, t2, t1, t0, oh_ref, geo_ref, use_ref, next_ref, w_tens, w_step,
    gap_out, next_out, parts_out, g0, g1, g2, g3, table_ref, acc_ref,
):
    fill_table(table_ref, (t0, t1, t2, t3))
    acc_ref[...] = jnp.zeros_like(acc_ref)
    clear_rest(live_ref, parts_out)

    def body(c, carry):
        at = lanes(c)
        gap = gather_ghosts(own_gap_ref, table_ref, oh_ref, at)
        gap_out[:, at] = gap
        geo = geo_ref[:, at]
        scalars = (ENV_SCALE * use_ref[CH : 2 * CH, at]) * project(geo, gap)
        hid = next_ref[:LAT, at] + dense(w_tens[0], scalars)
        later = next_ref[LAT:, at] + dense(w_step[...], hid * sigmoid(hid))
        next_out[:LAT, at] = hid
        next_out[LAT:, at] = later
        scatter_ghosts(acc_ref, parts_out, spread2(weigh(geo, later[:CH] * geo[3:4])), oh_ref, at)
        return carry

    lax.fori_loop(0, live_ref[0, 0], body, 0)
    emit(acc_ref, (g0, g1, g2, g3))


def update_back(geo, gap, values, dhid, w_lt_t, w_val_t):
    both = dense(w_lt_t, dhid)
    dscal = both[LAT : LAT + CH] * ENV_SCALE
    return both, dense(w_val_t, project(geo, gap) * dscal), values * dscal


def turn_kernel(
    live_ref, own_gap_ref, t3, t2, t1, t0, oh_ref, geo_ref, next_ref, read_vec, w_tens, w_leave, w_read_t, w_lt_t, w_val_t,
    energy_out, dlat_out, dgeo_out, parts_out, g0, g1, g2, g3, table_ref, acc_ref,
):
    fill_table(table_ref, (t0, t1, t2, t3))
    acc_ref[...] = jnp.zeros_like(acc_ref)
    clear_rest(live_ref, parts_out)
    rv = read_vec[...]

    def body(c, energy):
        at = lanes(c)
        gap = gather_ghosts(own_gap_ref, table_ref, oh_ref, at)
        geo = geo_ref[:, at]
        weight = geo[3:4]
        values = next_ref[LAT + CH : LAT + 2 * CH, at]
        scalars = (ENV_SCALE * values) * project(geo, gap)
        hid = next_ref[LAT + 2 * CH : LAT + USE, at] + dense(w_tens[1], scalars)
        act, hid_slope = silu_and_slope(hid)
        out, out_slope = silu_and_slope(next_ref[LAT + USE :, at] + dense(w_leave[...], act))
        pair_energy = jnp.sum(rv * out, axis=0, keepdims=True) + PAIR_SHIFT
        back = dense(w_read_t[...], out_slope * (rv * weight))
        both, more, dq = update_back(geo, gap, values, back[LAT : 2 * LAT] * hid_slope, w_lt_t[...], w_val_t[...])
        dlat_out[:LAT, at] = back[:LAT] + both[:LAT] + more[:LAT]
        dlat_out[LAT:, at] = back[2 * LAT :] + both[LAT + CH :] + more[LAT:]
        dgeo_out[:, at] = put_rows(dir_grad(dq, gap) + [pair_energy], CHUNK)
        scatter_ghosts(acc_ref, parts_out, spread2(weigh(geo, dq)), oh_ref, at)
        return energy + pair_energy * weight

    energy = lax.fori_loop(0, live_ref[0, 0], body, jnp.zeros((1, CHUNK), F32))
    energy_out[...] = jnp.broadcast_to(jnp.sum(energy, axis=1, keepdims=True), energy_out.shape)
    emit(acc_ref, (g0, g1, g2, g3))


def environment_back(geo, dvec, env_values, dlat, dgeo, w_env_t):
    weight = geo[3:4]
    dscaled = project(geo, dvec)
    rows = dir_grad(env_values * weight, dvec)
    rows.append(jnp.sum(env_values * dscaled, axis=0, keepdims=True))
    return dlat + dense(w_env_t, dscaled * weight), dgeo + put_rows(rows, CHUNK)


def back_kernel(
    live_ref, own_gap_ref, t3, t2, t1, t0, oh_ref, geo_ref, next_ref, dlat_ref, dgeo_ref, gap_ref, use_ref,
    w_lt_t, w_val_t, w_env_t,
    dlat_out, dgeo_out, parts_out, g0, g1, g2, g3, table_ref, acc_ref,
):
    fill_table(table_ref, (t0, t1, t2, t3))
    acc_ref[...] = jnp.zeros_like(acc_ref)
    clear_rest(live_ref, parts_out)

    def body(c, carry):
        at = lanes(c)
        dvec = gather_ghosts(own_gap_ref, table_ref, oh_ref, at)
        geo = geo_ref[:, at]
        dlat, dgeo = environment_back(geo, dvec, next_ref[LAT : LAT + CH, at], dlat_ref[:, at], dgeo_ref[:, at], w_env_t[...])
        gap = gap_ref[:, at]
        _, hid_slope = silu_and_slope(next_ref[:LAT, at])
        both, more, dq = update_back(geo, gap, use_ref[CH : 2 * CH, at], dlat[LAT:] * hid_slope, w_lt_t[...], w_val_t[...])
        dlat_out[:LAT, at] = dlat[:LAT] + both[:LAT] + more
        dgeo_out[:, at] = dgeo + put_rows(dir_grad(dq, gap), CHUNK)
        scatter_ghosts(acc_ref, parts_out, spread2(weigh(geo, dq)), oh_ref, at)
        return carry

    lax.fori_loop(0, live_ref[0, 0], body, 0)
    emit(acc_ref, (g0, g1, g2, g3))


def force_kernel(
    live_ref, own_gap_ref, t3, t2, t1, t0, oh_ref, geo_ref, use_ref, dlat_ref, dgeo_ref, slope_ref,
    w_env_t, w_rad_t,
    parts_out, g0, g1, g2, g3, table_ref, acc_ref,
):
    fill_table(table_ref, (t0, t1, t2, t3))
    acc_ref[...] = jnp.zeros_like(acc_ref)
    clear_rest(live_ref, parts_out)

    def body(c, carry):
        at = lanes(c)
        dvec = gather_ghosts(own_gap_ref, table_ref, oh_ref, at)
        geo = geo_ref[:, at]
        dlat, dgeo = environment_back(geo, dvec, use_ref[:CH, at], dlat_ref[:LAT, at], dgeo_ref[:, at], w_env_t[...])
        dbasis = dense(w_rad_t[...], dlat * slope_ref[:, at])
        dist, mask = geo[4:5], geo[5:6]
        inv = 1.0 / dist
        shrink = 1.0 - dist * dist * (1.0 / CUTOFF**2)
        env = shrink * shrink
        sines, cosines, freq = radial(dist)
        along = jnp.sum(dbasis * sines, axis=0, keepdims=True) * inv
        ddist = (jnp.sum(dbasis * (freq * cosines), axis=0, keepdims=True) - along) * (inv * env)
        denv = along + mask * dgeo[3:4]
        ddist = ddist - denv * shrink * dist * (4.0 / CUTOFF**2)
        row = lax.broadcasted_iota(jnp.int32, (8, CHUNK), 0)
        unit = jnp.where(row < 3, geo, 0.0)
        dunit = jnp.where(row < 3, dgeo, 0.0)
        radial_part = ddist - jnp.sum(unit * dunit, axis=0, keepdims=True) * inv
        ddiff = dunit * inv + unit * radial_part
        hi = ddiff.astype(BF16).astype(F32)
        both = jnp.concatenate([hi, ddiff - hi], axis=0).astype(BF16)
        parts = jnp.concatenate([both, jnp.zeros((WIDE - 16, CHUNK), BF16)], axis=0)
        scatter_ghosts(acc_ref, parts_out, parts, oh_ref, at)
        return carry

    lax.fori_loop(0, live_ref[0, 0], body, 0)
    emit(acc_ref, (g0, g1, g2, g3))


def final_kernel(pairs, own_ref, r3, r2, r1, r0, ohs_ref, energy_ref, other_ref, out_ref, energy_out):
    arrived = jnp.concatenate([r[...] for r in (r0, r1, r2, r3)], axis=1)
    hi, mid, lo = split3(arrived)
    parts = jnp.concatenate([hi, mid, lo, jnp.zeros_like(hi)], axis=0).astype(BF16)
    got = dot_nt(parts, ohs_ref[...])
    out_ref[...] = (own_ref[...] + got[0:8] + got[8:16] + got[16:24])[0:3]
    total = energy_ref[...] + other_ref[...]
    energy_out[...] = total[0:1, 0:1] / float(pairs)


def call(kernel, outs, *args, scratch=(), smem=0, fetched=0, aliases=None):
    vmem = pl.BlockSpec(memory_space=pltpu.VMEM)
    scalar = pl.BlockSpec(memory_space=pltpu.SMEM)
    anywhere = pl.BlockSpec(memory_space=pltpu.HBM)
    held = len(args) - fetched
    args = args[:held] + tuple(pltpu.with_memory_space_constraint(a, pltpu.HBM) for a in args[held:])
    buffers = [pltpu.VMEM(a.shape, a.dtype) for a in args[len(args) - fetched :]]
    if fetched:
        buffers.append(pltpu.SemaphoreType.DMA((fetched,)))
    return pl.pallas_call(
        kernel,
        out_shape=[jax.ShapeDtypeStruct(s, d) for s, d in outs],
        in_specs=[scalar] * smem + [vmem] * (len(args) - smem - fetched) + [anywhere] * fetched,
        out_specs=[scalar if s == (1, 1) and d == ID else vmem for s, d in outs],
        scratch_shapes=buffers + [pltpu.VMEM(s, d) for s, d in scratch],
        input_output_aliases=aliases or {},
        compiler_params=pltpu.CompilerParams(vmem_limit_bytes=VMEM_LIMIT),
    )(*args)


ORDER = (3, 2, 1, 0)


def matching(m, count):
    pairs = []
    for i in range(count):
        j = (i ^ 1, ((i + 1) ^ 1) - 1, i ^ 2, ((i + 2) ^ 2) - 2)[m]
        if 0 <= j < count:
            pairs.append((i, j))
    return pairs


def exchange(blocks):
    count = lax.axis_size("brick")
    return [lax.ppermute(blocks[m], "brick", matching(m, count)) for m in ORDER]


def exchange_and_add(blocks, energy, step):
    blocks, energy = lax.optimization_barrier((blocks, energy))
    energy = add_across(energy, step)
    return exchange(blocks), energy


def from_across(value, step):
    count = lax.axis_size("brick")
    if step >= count:
        return jnp.zeros_like(value)
    return lax.ppermute(value, "brick", [(i, i ^ step) for i in range(count)])


def add_across(value, step):
    return value + from_across(value, step)


def per_device(
    positions, species, pair_first, pair_second, pair_valid, send_list, w_radial, w_first, w_second, w_value, w_env,
    w_latent, w_tensor, w_mix, w_read, read_vec,
):
    brick = lax.axis_index("brick")
    flips = jnp.stack([brick & 1, (brick >> 1) & 1]).reshape(1, 2)
    spec = species[None, :]

    message = ((8, GHOST), F32)
    *messages, lists, live, atoms, ids, mask = call(
        send_kernel,
        [message] * 4
        + [((4, GHOST), ID), ((1, 1), ID), ((8, OWN), F32), ((2, BRICK_BLOCKS, 128), ID), ((BRICK_BLOCKS, 128), F32)],
        flips, positions, spec, send_list, pair_valid, pair_first, pair_second, smem=1, fetched=6,
    )
    coords = exchange(messages)
    oh, embed, enter = call(
        prepare_kernel,
        [((ROWS, PAIRS), BF16), ((LAT, 64), BF16), ((2 * USE + LAT, 3 * LAT), BF16)],
        ids, w_radial.T, w_first.T, w_second.T, w_value, w_env, w_latent, w_read,
        fetched=7,
    )

    def rows(n):
        return ((n, PAIRS), F32)

    owned = ((VEC, OWN), F32)
    ghosted = [((VEC, GHOST), F32)] * 4
    partials = [((2 * WIDE, PAIRS), BF16)] + ghosted
    table = ((2 * VEC, 4 * GHOST), BF16)
    acc = ((4 * GHOST, 2 * WIDE), F32)

    def own_part(parts, out):
        return call(own_scatter_kernel, [out], parts, oh)[0]

    def gathered(own, listed):
        (gap,) = call(own_gather_kernel, [rows(VEC)], own, oh)
        return [gap] + listed

    def combine(own, arrived, ohs):
        own, *listed = call(combine_kernel, [owned] + ghosted, own, *arrived, ohs)
        return own, listed

    def complete(parts, ghosts, ohs):
        arrived = exchange(ghosts)
        own, listed = combine(own_part(parts, owned), arrived, ohs)
        return gathered(own, exchange(listed))

    def complete_and_add(parts, ghosts, energy, steps):
        arrived, energy = exchange_and_add(ghosts, energy, steps[0])
        own, listed = combine(own_part(parts, owned), arrived, ohs)
        listed, energy = exchange_and_add(listed, energy, steps[1])
        return gathered(own, listed), energy

    geo, slope, use, later, parts, *ghosts = call(
        embed_kernel,
        [rows(8), rows(LAT), rows(2 * CH), rows(USE + 2 * LAT)] + partials,
        live, atoms, *coords, ids, mask, oh, embed, enter,
        scratch=[acc],
        smem=1,
    )
    ghosts, lists = lax.optimization_barrier((ghosts, lists))
    (ohs,) = call(lists_kernel, [((OWN, 4 * GHOST), BF16)], lists)
    arrived = exchange(ghosts)
    own, listed = combine(own_part(parts, owned), arrived, ohs)
    sources = (
        w_radial.T, w_value, w_env, w_latent, jnp.swapaxes(w_tensor, 1, 2), w_mix, w_read, read_vec[None, :],
    )
    listed, sources = lax.optimization_barrier((listed, sources))
    given = gathered(own, exchange(listed))
    shapes = (
        (2, LAT, 3 * CH), (USE + LAT, 3 * LAT), (LAT, 3 * LAT), (3 * LAT, 3 * LAT),
        (2 * LAT + CH, 3 * LAT), (2 * LAT, 3 * CH), (2 * LAT, 3 * CH), (LAT + CH, 3 * LAT), (LAT, 3 * CH), (LAT, 3 * CH),
        (NB, 3 * LAT),
    )
    tens, step, leave, read_t, lt1_t, val1_t, env1_t, lt0_t, val0_t, env0_t, rad_t, column = call(
        weights_kernel, [(s, BF16) for s in shapes] + [((LAT, 1), F32)], *sources, fetched=8,
    )
    gap0, later, parts, *ghosts = call(
        middle_kernel,
        [rows(VEC), rows(USE + 2 * LAT)] + partials,
        live, *given, oh, geo, use, later, tens, step,
        scratch=[table, acc], smem=1, aliases={1: 0, 9: 1},
    )
    given = complete(parts, ghosts, ohs)
    energy, dlat, dgeo, parts, *ghosts = call(
        turn_kernel,
        [((8, 128), F32), rows(2 * LAT), rows(8)] + partials,
        live, *given, oh, geo, later, column, tens, leave, read_t, lt1_t, val1_t,
        scratch=[table, acc], smem=1,
    )
    energy = add_across(energy, 1)
    given, energy = complete_and_add(parts, ghosts, energy, (2, 8))
    dlat, dgeo, parts, *ghosts = call(
        back_kernel,
        [rows(2 * LAT), rows(8)] + partials,
        live, *given, oh, geo, later, dlat, dgeo, gap0, use, lt0_t, val0_t, env1_t,
        scratch=[table, acc], smem=1, aliases={9: 0, 10: 1},
    )
    given, energy = complete_and_add(parts, ghosts, energy, (4, 32))
    parts, *ghosts = call(
        force_kernel,
        [((WIDE, PAIRS), BF16)] + [((8, GHOST), F32)] * 4,
        live, *given, oh, geo, use, dlat, dgeo, slope, env0_t, rad_t,
        scratch=[table, ((4 * GHOST, WIDE), F32)], smem=1,
    )
    arrived, energy = exchange_and_add(ghosts, energy, 16)
    own = own_part(parts, ((8, OWN), F32))
    forces, total = call(
        functools.partial(final_kernel, lax.axis_size("brick") * PAIRS),
        [((3, OWN), F32), ((1, 1), F32)],
        own, *arrived, ohs, energy, from_across(energy, 64),
    )
    return (forces, total.reshape(()))


def solution(mesh):
    line = P("brick", None)
    return jax.shard_map(
        per_device,
        mesh=mesh,
        in_specs=(P(None, "brick"), P("brick"), line, line, line, line) + (P(),) * 10,
        out_specs=(P(None, "brick"), P()),
        check_vma=False,
    )
```

```python
import functools
import math

import jax
import jax.numpy as jnp
import numpy as np
from jax import lax
from jax.experimental import pallas as pl
from jax.experimental.pallas import tpu as pltpu
from jax.sharding import PartitionSpec as P

F32 = jnp.float32
BF16 = jnp.bfloat16
ID = jnp.int32

CUTOFF = 6.0
SOFTENING = 0.25
ENV_SCALE = 0.25
PAIR_SHIFT = 1.0

LAT = 64
CH = 32
NB = 8
VEC = 3 * CH
USE = 2 * CH + LAT
OWN = 512
GHOST = 256
ROWS = OWN + 4 * GHOST
WIN = 256
BRICK_BLOCKS = 48
PAIRS = BRICK_BLOCKS * 128
CHUNK = 3072
CHUNK_BLOCKS = CHUNK // 128
WIDE = 128

VMEM_LIMIT = 7 * 1024 * 1024


def fit_trig():
    r = np.cos(np.linspace(0.0, np.pi, 4001)) * 0.5
    x = r * r
    base = np.polynomial.chebyshev.Chebyshev
    safe = np.where(r == 0.0, 1.0, r)
    sine = np.where(r == 0.0, 2 * np.pi, np.sin(2 * np.pi * safe) / safe)
    s = base.fit(x, sine, 8, domain=[0.0, 0.25]).convert(kind=np.polynomial.Polynomial)
    c = base.fit(x, np.cos(2 * np.pi * r), 8, domain=[0.0, 0.25]).convert(kind=np.polynomial.Polynomial)
    return [float(v) for v in s.coef], [float(v) for v in c.coef]


SIN_COEF, COS_COEF = fit_trig()


def horner(coef, x):
    out = jnp.full_like(x, coef[-1])
    for c in coef[-2::-1]:
        out = out * x + c
    return out


def dot(a, b):
    return lax.dot_general(a, b, (((1,), (0,)), ((), ())), preferred_element_type=F32)


def dot_nt(a, b):
    return lax.dot_general(a, b, (((1,), (1,)), ((), ())), preferred_element_type=F32)


def split2(x):
    hi = x.astype(BF16)
    lo = (x - hi.astype(F32)).astype(BF16)
    return hi, lo


def split3(x):
    hi = x.astype(BF16).astype(F32)
    rest = x - hi
    mid = rest.astype(BF16).astype(F32)
    return hi, mid, (rest - mid)


def stack2(x):
    hi, lo = split2(x)
    return jnp.concatenate([hi, lo], axis=0)


def spread2(x):
    hi, lo = split2(x)
    pad = jnp.zeros((WIDE - x.shape[0], x.shape[1]), BF16)
    return jnp.concatenate([hi, pad, lo, pad], axis=0)


def weight3(w):
    hi, lo = split2(w)
    return jnp.concatenate([hi.astype(F32), hi.astype(F32), lo.astype(F32)], axis=1).astype(BF16)


def dense(w3, x):
    hi, lo = split2(x)
    return dot(w3, jnp.concatenate([hi, lo, hi], axis=0))


def sigmoid(x):
    return 0.5 * jnp.tanh(0.5 * x) + 0.5


def silu_and_slope(x):
    s = sigmoid(x)
    y = x * s
    return y, s + y * (1.0 - s)


def hot(ids, rows):
    at = lax.broadcasted_iota(jnp.int32, (rows, ids.shape[1]), 0)
    return jnp.where(at == ids, 1.0, 0.0).astype(BF16)


def window_hot(ids, window, value, at):
    local = jnp.clip(ids - window * WIN, -1, WIN).astype(F32).astype(BF16)
    return jnp.where(at == local, jnp.full((), value, BF16), jnp.zeros((), BF16))


def fold2(x):
    half = x.shape[0] // 2
    return x[:half] + x[half:]


def radial(dist):
    k = (lax.broadcasted_iota(jnp.int32, (NB, dist.shape[1]), 0) + 1).astype(F32)
    turns = k * (dist * (1.0 / (2.0 * CUTOFF)))
    r = turns - jnp.round(turns)
    x = r * r
    return r * horner(SIN_COEF, x), horner(COS_COEF, x), k * (math.pi / CUTOFF)


def lanes(c):
    return pl.ds(pl.multiple_of(c * CHUNK, CHUNK), CHUNK)


def weigh(geo, values):
    return jnp.concatenate([geo[m : m + 1] * values for m in range(3)], axis=0)


def project(geo, vectors):
    return (
        geo[0:1] * vectors[:CH]
        + geo[1:2] * vectors[CH : 2 * CH]
        + geo[2:3] * vectors[2 * CH :]
    )


def put_rows(rows, n):
    at = lax.broadcasted_iota(jnp.int32, (8, n), 0)
    out = jnp.zeros((8, n), F32)
    for i, row in enumerate(rows):
        out = jnp.where(at == i, row, out)
    return out


def dir_grad(dq, vectors):
    return [jnp.sum(dq * vectors[m * CH : (m + 1) * CH], axis=0, keepdims=True) for m in range(3)]


def fill_table(table_ref, ghost_refs):
    for m, ghost in enumerate(ghost_refs):
        hi, lo = split2(ghost[...])
        at = m * GHOST
        table_ref[:VEC, at : at + GHOST] = hi
        table_ref[VEC:, at : at + GHOST] = lo


def gather_ghosts(own_gap_ref, table_ref, oh_ref, at):
    return own_gap_ref[:, at] + fold2(dot(table_ref[...], oh_ref[OWN:, at]))


def scatter_ghosts(acc_ref, parts_out, parts, oh_ref, at):
    parts_out[:, at] = parts
    acc_ref[...] += dot_nt(oh_ref[OWN:, at], parts)


def emit(acc_ref, ghost_outs):
    for m, out in enumerate(ghost_outs):
        out[...] = join_parts(acc_ref[m * GHOST : (m + 1) * GHOST, :], out.shape[0])


def join_parts(acc, rows):
    if acc.shape[1] == WIDE:
        turned = acc.T
        return turned[:rows] + turned[rows : 2 * rows]
    return (acc[:, :WIDE] + acc[:, WIDE:]).T[:rows]


def start_fetch(sources, targets, sems):
    copies = [pltpu.make_async_copy(a, b, sems.at[i]) for i, (a, b) in enumerate(zip(sources, targets))]
    for copy in copies:
        copy.start()
    return copies


def fetch(sources, targets, sems):
    for copy in start_fetch(sources, targets, sems):
        copy.wait()


def pick(tables, ids, count):
    block, place = ids >> 7, ids & 127
    found = [jnp.zeros(ids.shape, F32)] * 4
    for w, (ref, at) in enumerate(tables[:count]):
        here = block == w
        for k in range(4):
            row = jnp.broadcast_to(ref[k : k + 1, at : at + 128], ids.shape)
            value = jnp.take_along_axis(row, place, axis=1, mode="promise_in_bounds")
            found[k] = jnp.where(here, value, found[k])
    return found


def send_kernel(
    flip_ref, pos_in, spec_in, send_in, valid_in, first_in, second_in,
    m0, m1, m2, m3, lists_ref, live_ref, atoms_ref, ids_ref, mask_ref,
    pos_ref, spec_ref, send_ref, valid_ref, first_ref, second_ref, sems,
):
    fetch(
        (pos_in, spec_in, send_in, valid_in, first_in, second_in),
        (pos_ref, spec_ref, send_ref, valid_ref, first_ref, second_ref),
        sems,
    )
    live = jnp.sum(valid_ref[:, 0:1].astype(F32)).astype(jnp.int32)
    live_ref[0, 0] = (live + CHUNK_BLOCKS - 1) // CHUNK_BLOCKS
    lists = []
    for m in range(4):
        other = jnp.full((1, GHOST), flip_ref[0, m // 2], jnp.int32) == 1
        lists.append(jnp.where(other, send_ref[m ^ 1 : (m ^ 1) + 1, :], send_ref[m : m + 1, :]))
    lists_ref[...] = jnp.concatenate(lists, axis=0)
    atoms_ref[...] = put_rows([pos_ref[i : i + 1, :] for i in range(3)] + [spec_ref[...].astype(F32)], OWN)
    halves = [ids[:, h * 128 : (h + 1) * 128] for ids in lists for h in range(GHOST // 128)]
    found = pick([(atoms_ref, w * 128) for w in range(OWN // 128)], jnp.concatenate(halves, axis=0), OWN // 128)
    for m, out in enumerate((m0, m1, m2, m3)):
        out[...] = put_rows(
            [jnp.concatenate([f[2 * m : 2 * m + 1], f[2 * m + 1 : 2 * m + 2]], axis=1) for f in found], GHOST
        )
    near, far = 1 - flip_ref[0, 0], 1 - flip_ref[0, 1]
    slot = second_ref[...] - OWN
    group = slot >> 8
    group = group ^ jnp.where(group < 2, near, far)
    ids_ref[0] = first_ref[...]
    ids_ref[1] = jnp.where(slot < 0, second_ref[...], OWN + group * GHOST + (slot & (GHOST - 1)))
    mask_ref[...] = valid_ref[...].astype(F32)


def lists_kernel(lists_ref, ohs_ref):
    at = lax.broadcasted_iota(jnp.int32, (WIN, GHOST), 0).astype(F32).astype(BF16)
    for m in range(4):
        for w in range(OWN // WIN):
            tile = window_hot(lists_ref[m : m + 1, :], w, 1.0, at)
            ohs_ref[w * WIN : (w + 1) * WIN, m * GHOST : (m + 1) * GHOST] = tile


def build_incidence(ids_ref, oh_ref):
    span = 512
    at = lax.broadcasted_iota(jnp.int32, (WIN, span), 0).astype(F32).astype(BF16)

    def body(c, carry):
        blocks = [pl.ds(c * (span // 128) + i, 1) for i in range(span // 128)]
        first = jnp.concatenate([ids_ref[0, b, :] for b in blocks], axis=1)
        second = jnp.concatenate([ids_ref[1, b, :] for b in blocks], axis=1)
        out = pl.ds(pl.multiple_of(c * span, span), span)
        for w in range(ROWS // WIN):
            tile = window_hot(second, w, -1.0, at)
            if w < OWN // WIN:
                tile = tile + window_hot(first, w, 1.0, at)
            oh_ref[w * WIN : (w + 1) * WIN, out] = tile
        return carry

    lax.fori_loop(0, PAIRS // span, body, 0)


def prepare_kernel(ids_ref, *refs):
    sources, refs = refs[:7], refs[7:]
    oh_ref, embed, enter = refs[:3]
    copies = start_fetch(sources, refs[3:10], refs[10])
    w_radial_t, w_first_t, w_second_t, w_value, w_env, w_latent, w_read = refs[3:10]
    build_incidence(ids_ref, oh_ref)
    for copy in copies:
        copy.wait()

    def parts(w):
        hi, lo = split2(w)
        return hi.astype(F32), lo.astype(F32)

    rh, rl = parts(w_radial_t[...].T)
    fh, fl = parts(w_first_t[...].T)
    sh, sl = parts(w_second_t[...].T)
    embed[...] = jnp.concatenate([rh, rh, rl, fh, sh, fl, sl, jnp.zeros_like(rh)], axis=1).astype(BF16)
    for l in range(2):
        use = jnp.concatenate([w_env[l], w_value[l], w_latent[l]], axis=0)
        enter[l * USE : (l + 1) * USE, :] = weight3(use)
    enter[2 * USE :, :] = weight3(w_read[...])


def weights_kernel(*refs):
    sources, refs = refs[:8], refs[8:]
    tens, step, leave, read_t, lt1_t, val1_t, env1_t, lt0_t, val0_t, env0_t, rad_t, column = refs[:12]
    fetch(sources, refs[12:20], refs[20])
    w_radial_t, w_value, w_env, w_latent, w_tensor_t, w_mix, w_read, read_vec = refs[12:20]
    use1 = jnp.concatenate([w_env[1], w_value[1], w_latent[1]], axis=0)
    use_mix0 = dense(weight3(use1), w_mix[0])
    read3 = weight3(w_read[...])
    read_mix0, read_mix1 = dense(read3, w_mix[0]), dense(read3, w_mix[1])
    for l in range(2):
        tens[l] = weight3(w_tensor_t[l].T)
    step[...] = weight3(jnp.concatenate([use_mix0, read_mix0], axis=0))
    leave[...] = weight3(read_mix1)
    read_t[...] = weight3(jnp.concatenate([w_read[...].T, read_mix1.T, read_mix0.T], axis=0))
    lt1_t[...] = weight3(jnp.concatenate([w_latent[1].T, w_tensor_t[1], use_mix0[2 * CH :].T], axis=0))
    val1_t[...] = weight3(jnp.concatenate([w_value[1].T, use_mix0[CH : 2 * CH].T], axis=0))
    env1_t[...] = weight3(jnp.concatenate([w_env[1].T, use_mix0[:CH].T], axis=0))
    lt0_t[...] = weight3(jnp.concatenate([w_latent[0].T, w_tensor_t[0]], axis=0))
    val0_t[...] = weight3(w_value[0].T)
    env0_t[...] = weight3(w_env[0].T)
    rad_t[...] = weight3(w_radial_t[...])
    diagonal = lax.broadcasted_iota(jnp.int32, (LAT, LAT), 0) == lax.broadcasted_iota(jnp.int32, (LAT, LAT), 1)
    column[...] = jnp.sum(jnp.where(diagonal, read_vec[...], 0.0), axis=1, keepdims=True)


def own_gather_kernel(own_ref, oh_ref, gap_out):
    table = stack2(own_ref[...])
    for c in range(PAIRS // CHUNK):
        at = slice(c * CHUNK, (c + 1) * CHUNK)
        gap_out[:, at] = fold2(dot(table, oh_ref[:OWN, at]))


def own_scatter_kernel(parts_ref, oh_ref, own_out):
    own_out[...] = join_parts(dot_nt(oh_ref[:OWN, :], parts_ref[...]), own_out.shape[0])


def clear_rest(live_ref, parts_out):
    def body(c, carry):
        parts_out[:, lanes(c)] = jnp.zeros((parts_out.shape[0], CHUNK), BF16)
        return carry

    lax.fori_loop(live_ref[0, 0], PAIRS // CHUNK, body, 0)


def embed_kernel(
    live_ref, own_ref, c3, c2, c1, c0, ids_ref, mask_ref, oh_ref, w_embed, w_enter,
    geo_out, slope_out, use_out, next_out, parts_out, g0, g1, g2, g3, acc_ref,
):
    tables = [(own_ref, w * 128) for w in range(OWN // 128)]
    tables += [(c, w * 128) for c in (c0, c1, c2, c3) for w in range(GHOST // 128)]

    one = pick(tables, ids_ref[0], OWN // 128)
    two = pick(tables, ids_ref[1], ROWS // 128)
    mask = mask_ref[...]
    diff = [two[k] - one[k] for k in range(3)]
    sq = diff[0] * diff[0] + diff[1] * diff[1] + diff[2] * diff[2] + SOFTENING
    dist = jnp.sqrt(sq)
    inv = 1.0 / dist
    shrink = 1.0 - sq * (1.0 / CUTOFF**2)
    env = shrink * shrink
    columns = [d * inv for d in diff] + [env * mask, dist, mask, env * inv, one[3] + 8.0 * two[3]]
    for b in range(BRICK_BLOCKS):
        geo_out[:, b * 128 : (b + 1) * 128] = jnp.concatenate([column[b : b + 1] for column in columns], axis=0)
    acc_ref[...] = jnp.zeros_like(acc_ref)
    clear_rest(live_ref, parts_out)

    def body(c, carry):
        at = lanes(c)
        geo = geo_out[:, at]
        sines, _, _ = radial(geo[4:5])
        basis = sines * geo[6:7]
        bh = basis.astype(BF16).astype(F32)
        bl = basis - bh
        row = lax.broadcasted_iota(jnp.int32, (8, CHUNK), 0).astype(F32)
        code = geo[7:8]
        other = jnp.floor(code * 0.125)
        sf = jnp.where(row == code - 8.0 * other, 1.0, 0.0)
        ss = jnp.where(row == other, 1.0, 0.0)
        pre = dot(
            w_embed[...],
            jnp.concatenate([bh, bl, bh, sf, ss, sf, ss, jnp.zeros_like(bh)], axis=0).astype(BF16),
        )
        lat, slope = silu_and_slope(pre)
        slope_out[:, at] = slope
        enter = dense(w_enter[...], lat)
        use_out[:, at] = enter[: 2 * CH]
        next_out[:, at] = enter[2 * CH :]
        scatter_ghosts(acc_ref, parts_out, spread2(weigh(geo, enter[:CH] * geo[3:4])), oh_ref, at)
        return carry

    lax.fori_loop(0, live_ref[0, 0], body, 0)
    emit(acc_ref, (g0, g1, g2, g3))


def combine_kernel(own_ref, r3, r2, r1, r0, ohs_ref, own_out, g0, g1, g2, g3):
    arrived = jnp.concatenate([r[...] for r in (r0, r1, r2, r3)], axis=1)
    owned = own_ref[...] + fold2(dot_nt(stack2(arrived), ohs_ref[...]))
    own_out[...] = owned
    ghosts = fold2(dot(stack2(owned), ohs_ref[...]))
    for m, out in enumerate((g0, g1, g2, g3)):
        out[...] = ghosts[:, m * GHOST : (m + 1) * GHOST]


def middle_kernel(
    live_ref, own_gap_ref, t3, t2, t1, t0, oh_ref, geo_ref, use_ref, next_ref, w_tens, w_step,
    gap_out, next_out, parts_out, g0, g1, g2, g3, table_ref, acc_ref,
):
    fill_table(table_ref, (t0, t1, t2, t3))
    acc_ref[...] = jnp.zeros_like(acc_ref)
    clear_rest(live_ref, parts_out)

    def body(c, carry):
        at = lanes(c)
        gap = gather_ghosts(own_gap_ref, table_ref, oh_ref, at)
        gap_out[:, at] = gap
        geo = geo_ref[:, at]
        scalars = (ENV_SCALE * use_ref[CH : 2 * CH, at]) * project(geo, gap)
        hid = next_ref[:LAT, at] + dense(w_tens[0], scalars)
        later = next_ref[LAT:, at] + dense(w_step[...], hid * sigmoid(hid))
        next_out[:LAT, at] = hid
        next_out[LAT:, at] = later
        scatter_ghosts(acc_ref, parts_out, spread2(weigh(geo, later[:CH] * geo[3:4])), oh_ref, at)
        return carry

    lax.fori_loop(0, live_ref[0, 0], body, 0)
    emit(acc_ref, (g0, g1, g2, g3))


def update_back(geo, gap, values, dhid, w_lt_t, w_val_t):
    both = dense(w_lt_t, dhid)
    dscal = both[LAT : LAT + CH] * ENV_SCALE
    return both, dense(w_val_t, project(geo, gap) * dscal), values * dscal


def turn_kernel(
    live_ref, own_gap_ref, t3, t2, t1, t0, oh_ref, geo_ref, next_ref, read_vec, w_tens, w_leave, w_read_t, w_lt_t, w_val_t,
    energy_out, dlat_out, dgeo_out, parts_out, g0, g1, g2, g3, table_ref, acc_ref,
):
    fill_table(table_ref, (t0, t1, t2, t3))
    acc_ref[...] = jnp.zeros_like(acc_ref)
    clear_rest(live_ref, parts_out)
    rv = read_vec[...]

    def body(c, energy):
        at = lanes(c)
        gap = gather_ghosts(own_gap_ref, table_ref, oh_ref, at)
        geo = geo_ref[:, at]
        weight = geo[3:4]
        values = next_ref[LAT + CH : LAT + 2 * CH, at]
        scalars = (ENV_SCALE * values) * project(geo, gap)
        hid = next_ref[LAT + 2 * CH : LAT + USE, at] + dense(w_tens[1], scalars)
        act, hid_slope = silu_and_slope(hid)
        out, out_slope = silu_and_slope(next_ref[LAT + USE :, at] + dense(w_leave[...], act))
        pair_energy = jnp.sum(rv * out, axis=0, keepdims=True) + PAIR_SHIFT
        back = dense(w_read_t[...], out_slope * (rv * weight))
        both, more, dq = update_back(geo, gap, values, back[LAT : 2 * LAT] * hid_slope, w_lt_t[...], w_val_t[...])
        dlat_out[:LAT, at] = back[:LAT] + both[:LAT] + more[:LAT]
        dlat_out[LAT:, at] = back[2 * LAT :] + both[LAT + CH :] + more[LAT:]
        dgeo_out[:, at] = put_rows(dir_grad(dq, gap) + [pair_energy], CHUNK)
        scatter_ghosts(acc_ref, parts_out, spread2(weigh(geo, dq)), oh_ref, at)
        return energy + pair_energy * weight

    energy = lax.fori_loop(0, live_ref[0, 0], body, jnp.zeros((1, CHUNK), F32))
    energy_out[...] = jnp.broadcast_to(jnp.sum(energy, axis=1, keepdims=True), energy_out.shape)
    emit(acc_ref, (g0, g1, g2, g3))


def environment_back(geo, dvec, env_values, dlat, dgeo, w_env_t):
    weight = geo[3:4]
    dscaled = project(geo, dvec)
    rows = dir_grad(env_values * weight, dvec)
    rows.append(jnp.sum(env_values * dscaled, axis=0, keepdims=True))
    return dlat + dense(w_env_t, dscaled * weight), dgeo + put_rows(rows, CHUNK)


def back_kernel(
    live_ref, own_gap_ref, t3, t2, t1, t0, oh_ref, geo_ref, next_ref, dlat_ref, dgeo_ref, gap_ref, use_ref,
    w_lt_t, w_val_t, w_env_t,
    dlat_out, dgeo_out, parts_out, g0, g1, g2, g3, table_ref, acc_ref,
):
    fill_table(table_ref, (t0, t1, t2, t3))
    acc_ref[...] = jnp.zeros_like(acc_ref)
    clear_rest(live_ref, parts_out)

    def body(c, carry):
        at = lanes(c)
        dvec = gather_ghosts(own_gap_ref, table_ref, oh_ref, at)
        geo = geo_ref[:, at]
        dlat, dgeo = environment_back(geo, dvec, next_ref[LAT : LAT + CH, at], dlat_ref[:, at], dgeo_ref[:, at], w_env_t[...])
        gap = gap_ref[:, at]
        _, hid_slope = silu_and_slope(next_ref[:LAT, at])
        both, more, dq = update_back(geo, gap, use_ref[CH : 2 * CH, at], dlat[LAT:] * hid_slope, w_lt_t[...], w_val_t[...])
        dlat_out[:LAT, at] = dlat[:LAT] + both[:LAT] + more
        dgeo_out[:, at] = dgeo + put_rows(dir_grad(dq, gap), CHUNK)
        scatter_ghosts(acc_ref, parts_out, spread2(weigh(geo, dq)), oh_ref, at)
        return carry

    lax.fori_loop(0, live_ref[0, 0], body, 0)
    emit(acc_ref, (g0, g1, g2, g3))


def force_kernel(
    live_ref, own_gap_ref, t3, t2, t1, t0, oh_ref, geo_ref, use_ref, dlat_ref, dgeo_ref, slope_ref,
    w_env_t, w_rad_t,
    parts_out, g0, g1, g2, g3, table_ref, acc_ref,
):
    fill_table(table_ref, (t0, t1, t2, t3))
    acc_ref[...] = jnp.zeros_like(acc_ref)
    clear_rest(live_ref, parts_out)

    def body(c, carry):
        at = lanes(c)
        dvec = gather_ghosts(own_gap_ref, table_ref, oh_ref, at)
        geo = geo_ref[:, at]
        dlat, dgeo = environment_back(geo, dvec, use_ref[:CH, at], dlat_ref[:LAT, at], dgeo_ref[:, at], w_env_t[...])
        dbasis = dense(w_rad_t[...], dlat * slope_ref[:, at])
        dist, mask = geo[4:5], geo[5:6]
        inv = 1.0 / dist
        shrink = 1.0 - dist * dist * (1.0 / CUTOFF**2)
        env = shrink * shrink
        sines, cosines, freq = radial(dist)
        along = jnp.sum(dbasis * sines, axis=0, keepdims=True) * inv
        ddist = (jnp.sum(dbasis * (freq * cosines), axis=0, keepdims=True) - along) * (inv * env)
        denv = along + mask * dgeo[3:4]
        ddist = ddist - denv * shrink * dist * (4.0 / CUTOFF**2)
        row = lax.broadcasted_iota(jnp.int32, (8, CHUNK), 0)
        unit = jnp.where(row < 3, geo, 0.0)
        dunit = jnp.where(row < 3, dgeo, 0.0)
        radial_part = ddist - jnp.sum(unit * dunit, axis=0, keepdims=True) * inv
        ddiff = dunit * inv + unit * radial_part
        hi = ddiff.astype(BF16).astype(F32)
        both = jnp.concatenate([hi, ddiff - hi], axis=0).astype(BF16)
        parts = jnp.concatenate([both, jnp.zeros((WIDE - 16, CHUNK), BF16)], axis=0)
        scatter_ghosts(acc_ref, parts_out, parts, oh_ref, at)
        return carry

    lax.fori_loop(0, live_ref[0, 0], body, 0)
    emit(acc_ref, (g0, g1, g2, g3))


def final_kernel(pairs, own_ref, r3, r2, r1, r0, ohs_ref, energy_ref, other_ref, out_ref, energy_out):
    arrived = jnp.concatenate([r[...] for r in (r0, r1, r2, r3)], axis=1)
    hi, mid, lo = split3(arrived)
    parts = jnp.concatenate([hi, mid, lo, jnp.zeros_like(hi)], axis=0).astype(BF16)
    got = dot_nt(parts, ohs_ref[...])
    out_ref[...] = (own_ref[...] + got[0:8] + got[8:16] + got[16:24])[0:3]
    total = energy_ref[...] + other_ref[...]
    energy_out[...] = total[0:1, 0:1] / float(pairs)


def call(kernel, outs, *args, scratch=(), smem=0, fetched=0, aliases=None):
    vmem = pl.BlockSpec(memory_space=pltpu.VMEM)
    scalar = pl.BlockSpec(memory_space=pltpu.SMEM)
    anywhere = pl.BlockSpec(memory_space=pltpu.HBM)
    held = len(args) - fetched
    args = args[:held] + tuple(pltpu.with_memory_space_constraint(a, pltpu.HBM) for a in args[held:])
    buffers = [pltpu.VMEM(a.shape, a.dtype) for a in args[len(args) - fetched :]]
    if fetched:
        buffers.append(pltpu.SemaphoreType.DMA((fetched,)))
    return pl.pallas_call(
        kernel,
        out_shape=[jax.ShapeDtypeStruct(s, d) for s, d in outs],
        in_specs=[scalar] * smem + [vmem] * (len(args) - smem - fetched) + [anywhere] * fetched,
        out_specs=[scalar if s == (1, 1) and d == ID else vmem for s, d in outs],
        scratch_shapes=buffers + [pltpu.VMEM(s, d) for s, d in scratch],
        input_output_aliases=aliases or {},
        compiler_params=pltpu.CompilerParams(vmem_limit_bytes=VMEM_LIMIT),
    )(*args)


ORDER = (3, 2, 1, 0)


def matching(m, count):
    pairs = []
    for i in range(count):
        j = (i ^ 1, ((i + 1) ^ 1) - 1, i ^ 2, ((i + 2) ^ 2) - 2)[m]
        if 0 <= j < count:
            pairs.append((i, j))
    return pairs


def exchange(blocks):
    count = lax.axis_size("brick")
    return [lax.ppermute(blocks[m], "brick", matching(m, count)) for m in ORDER]


def exchange_and_add(blocks, energy, step):
    blocks, energy = lax.optimization_barrier((blocks, energy))
    energy = add_across(energy, step)
    return exchange(blocks), energy


def from_across(value, step):
    count = lax.axis_size("brick")
    if step >= count:
        return jnp.zeros_like(value)
    return lax.ppermute(value, "brick", [(i, i ^ step) for i in range(count)])


def add_across(value, step):
    return value + from_across(value, step)


def per_device(
    positions, species, pair_first, pair_second, pair_valid, send_list, w_radial, w_first, w_second, w_value, w_env,
    w_latent, w_tensor, w_mix, w_read, read_vec,
):
    brick = lax.axis_index("brick")
    flips = jnp.stack([brick & 1, (brick >> 1) & 1]).reshape(1, 2)
    spec = species[None, :]

    message = ((8, GHOST), F32)
    *messages, lists, live, atoms, ids, mask = call(
        send_kernel,
        [message] * 4
        + [((4, GHOST), ID), ((1, 1), ID), ((8, OWN), F32), ((2, BRICK_BLOCKS, 128), ID), ((BRICK_BLOCKS, 128), F32)],
        flips, positions, spec, send_list, pair_valid, pair_first, pair_second, smem=1, fetched=6,
    )
    coords = exchange(messages)
    oh, embed, enter = call(
        prepare_kernel,
        [((ROWS, PAIRS), BF16), ((LAT, 64), BF16), ((2 * USE + LAT, 3 * LAT), BF16)],
        ids, w_radial.T, w_first.T, w_second.T, w_value, w_env, w_latent, w_read,
        fetched=7,
    )

    def rows(n):
        return ((n, PAIRS), F32)

    owned = ((VEC, OWN), F32)
    ghosted = [((VEC, GHOST), F32)] * 4
    partials = [((2 * WIDE, PAIRS), BF16)] + ghosted
    table = ((2 * VEC, 4 * GHOST), BF16)
    acc = ((4 * GHOST, 2 * WIDE), F32)

    def own_part(parts, out):
        return call(own_scatter_kernel, [out], parts, oh)[0]

    def gathered(own, listed):
        (gap,) = call(own_gather_kernel, [rows(VEC)], own, oh)
        return [gap] + listed

    def combine(own, arrived, ohs):
        own, *listed = call(combine_kernel, [owned] + ghosted, own, *arrived, ohs)
        return own, listed

    def complete(parts, ghosts, ohs):
        arrived = exchange(ghosts)
        own, listed = combine(own_part(parts, owned), arrived, ohs)
        return gathered(own, exchange(listed))

    def complete_and_add(parts, ghosts, energy, steps):
        arrived, energy = exchange_and_add(ghosts, energy, steps[0])
        own, listed = combine(own_part(parts, owned), arrived, ohs)
        listed, energy = exchange_and_add(listed, energy, steps[1])
        return gathered(own, listed), energy

    geo, slope, use, later, parts, *ghosts = call(
        embed_kernel,
        [rows(8), rows(LAT), rows(2 * CH), rows(USE + 2 * LAT)] + partials,
        live, atoms, *coords, ids, mask, oh, embed, enter,
        scratch=[acc],
        smem=1,
    )
    ghosts, lists = lax.optimization_barrier((ghosts, lists))
    (ohs,) = call(lists_kernel, [((OWN, 4 * GHOST), BF16)], lists)
    arrived = exchange(ghosts)
    own, listed = combine(own_part(parts, owned), arrived, ohs)
    sources = (
        w_radial.T, w_value, w_env, w_latent, jnp.swapaxes(w_tensor, 1, 2), w_mix, w_read, read_vec[None, :],
    )
    listed, sources = lax.optimization_barrier((listed, sources))
    given = gathered(own, exchange(listed))
    shapes = (
        (2, LAT, 3 * CH), (USE + LAT, 3 * LAT), (LAT, 3 * LAT), (3 * LAT, 3 * LAT),
        (2 * LAT + CH, 3 * LAT), (2 * LAT, 3 * CH), (2 * LAT, 3 * CH), (LAT + CH, 3 * LAT), (LAT, 3 * CH), (LAT, 3 * CH),
        (NB, 3 * LAT),
    )
    tens, step, leave, read_t, lt1_t, val1_t, env1_t, lt0_t, val0_t, env0_t, rad_t, column = call(
        weights_kernel, [(s, BF16) for s in shapes] + [((LAT, 1), F32)], *sources, fetched=8,
    )
    gap0, later, parts, *ghosts = call(
        middle_kernel,
        [rows(VEC), rows(USE + 2 * LAT)] + partials,
        live, *given, oh, geo, use, later, tens, step,
        scratch=[table, acc], smem=1, aliases={1: 0, 9: 1},
    )
    given = complete(parts, ghosts, ohs)
    energy, dlat, dgeo, parts, *ghosts = call(
        turn_kernel,
        [((8, 128), F32), rows(2 * LAT), rows(8)] + partials,
        live, *given, oh, geo, later, column, tens, leave, read_t, lt1_t, val1_t,
        scratch=[table, acc], smem=1,
    )
    energy = add_across(energy, 1)
    given, energy = complete_and_add(parts, ghosts, energy, (16, 8))
    dlat, dgeo, parts, *ghosts = call(
        back_kernel,
        [rows(2 * LAT), rows(8)] + partials,
        live, *given, oh, geo, later, dlat, dgeo, gap0, use, lt0_t, val0_t, env1_t,
        scratch=[table, acc], smem=1, aliases={9: 0, 10: 1},
    )
    given, energy = complete_and_add(parts, ghosts, energy, (4, 32))
    parts, *ghosts = call(
        force_kernel,
        [((WIDE, PAIRS), BF16)] + [((8, GHOST), F32)] * 4,
        live, *given, oh, geo, use, dlat, dgeo, slope, env0_t, rad_t,
        scratch=[table, ((4 * GHOST, WIDE), F32)], smem=1,
    )
    arrived, energy = exchange_and_add(ghosts, energy, 64)
    own = own_part(parts, ((8, OWN), F32))
    forces, total = call(
        functools.partial(final_kernel, lax.axis_size("brick") * PAIRS),
        [((3, OWN), F32), ((1, 1), F32)],
        own, *arrived, ohs, energy, from_across(energy, 2),
    )
    return (forces, total.reshape(()))


def solution(mesh):
    line = P("brick", None)
    return jax.shard_map(
        per_device,
        mesh=mesh,
        in_specs=(P(None, "brick"), P("brick"), line, line, line, line) + (P(),) * 10,
        out_specs=(P(None, "brick"), P()),
        check_vma=False,
    )
```
